32 devices in a mesh: fsdp: 16 (over z, y, core), tp: 2 (over x).
Axes of the slice: x: 2, y: 2, z: 4, core: 2. Of those that a mesh axis runs over, the one named last changes fastest.
Arguments:
- entering_states: bfloat16 [35328, 1024], P(('fsdp', 'tp')), may hold values from -6 to 6
- bypass_states: bfloat16 [35328, 1024], P(('fsdp', 'tp')), may hold values from -6 to 6
- mentor_states: bfloat16 [35328, 1024], P(('fsdp', 'tp')), may hold values from -18 to 18
- occupancy_mask: int32 [32], P('fsdp'), may hold values from 0 to 1, as said below
- bypass_merge_matrix: bfloat16 [2048, 1024], P(('fsdp', 'tp')), may hold values from -0.125 to 0.125
- bypass_merge_offset: bfloat16 [1024], P(('fsdp', 'tp')), may hold values from -1.5 to 1.5
- mixer_layernorm_scale: bfloat16 [1024], P(('fsdp', 'tp')), may hold values from 0.25 to 1.75
- mixer_layernorm_offset: bfloat16 [1024], P(('fsdp', 'tp')), may hold values from -1.5 to 1.5
- asking_map_matrix: bfloat16 [1024, 1024], P('fsdp', 'tp'), may hold values from -0.3125 to 0.3125
- lookup_map_matrix: bfloat16 [1024, 1024], P('fsdp', 'tp'), may hold values from -0.3125 to 0.3125
- content_map_matrix: bfloat16 [1024, 1024], P('fsdp', 'tp'), may hold values from -0.1875 to 0.1875
- mixer_result_matrix: bfloat16 [1024, 1024], P('tp', 'fsdp'), may hold values from -0.25 to 0.25
- mixer_result_offset: bfloat16 [1024], P(('fsdp', 'tp')), may hold values from -1.5 to 1.5
- perceptron_layernorm_scale: bfloat16 [1024], P(('fsdp', 'tp')), may hold values from 0.25 to 1.75
- perceptron_layernorm_offset: bfloat16 [1024], P(('fsdp', 'tp')), may hold values from -1.5 to 1.5
- expand_layer_matrix: bfloat16 [1024, 4096], P('fsdp', 'tp'), may hold values from -0.1875 to 0.1875
- expand_layer_offset: bfloat16 [4096], P(('fsdp', 'tp')), may hold values from -1.5 to 1.5
- contract_layer_matrix: bfloat16 [4096, 1024], P('tp', 'fsdp'), may hold values from -0.09375 to 0.09375
- contract_layer_offset: bfloat16 [1024], P(('fsdp', 'tp')), may hold values from -1.5 to 1.5
Outputs:
- block_out: bfloat16 [35328, 1024], P(('fsdp', 'tp'))
- loss_value: float32 [], replicated
- grad_tokens: float32 [35328, 1024], P(('fsdp', 'tp'))
- grad_shortcut: float32 [35328, 1024], P(('fsdp', 'tp'))
- grad_merge_weight: float32 [2048, 1024], P(('fsdp', 'tp'))
- grad_merge_bias: float32 [1024], P(('fsdp', 'tp'))
- grad_first_gain: float32 [1024], P(('fsdp', 'tp'))
- grad_first_shift: float32 [1024], P(('fsdp', 'tp'))
- grad_query_weight: float32 [1024, 1024], P('fsdp', 'tp')
- grad_key_weight: float32 [1024, 1024], P('fsdp', 'tp')
- grad_value_weight: float32 [1024, 1024], P('fsdp', 'tp')
- grad_output_weight: float32 [1024, 1024], P('tp', 'fsdp')
- grad_output_bias: float32 [1024], P(('fsdp', 'tp'))
- grad_second_gain: float32 [1024], P(('fsdp', 'tp'))
- grad_second_shift: float32 [1024], P(('fsdp', 'tp'))
- grad_hidden_weight: float32 [1024, 4096], P('fsdp', 'tp')
- grad_hidden_bias: float32 [4096], P(('fsdp', 'tp'))
- grad_down_weight: float32 [4096, 1024], P('tp', 'fsdp')
- grad_down_bias: float32 [1024], P(('fsdp', 'tp'))
The draws below stay inside these ranges and needn't reach their ends.
Inputs may be any that keep to these rules, and one draw needn't show every extreme that they name: `occupancy_mask`: in each group of 2 slots (the slots of one index of fsdp) the live slots come first and at least one is live; in every draw some group has all 2 slots live.
All inputs are finite; a program needn't handle non-finite values.
Results may differ from the reference program's by a relative error of at most 0.015.
Values may be sent and summed in bfloat16 or wider, within the bound.
No kernel may reach another device: no remote copies, remote signals or barrier semaphores. Data moves between devices by JAX's collectives and lax.ppermute only.
A program may use at most 320 MiB of HBM per device.

```python
import jax
import jax.numpy as jnp
from jax import lax

D = 1024
HEADS = 16
FF = 4096
SEQ_LEN = 1104
SERIES_PLACES = 2
TOKENS = 35328
N_FSDP = 16


def draw_occupancy_mask(key, part):
    first_key, second_key = jax.random.split(jax.random.fold_in(key, 17))
    counts = jax.random.randint(first_key, (N_FSDP,), 1, SERIES_PLACES + 1)
    fullest = jax.random.randint(second_key, (), 0, N_FSDP)
    counts = jnp.where(jnp.arange(N_FSDP) == fullest, SERIES_PLACES, counts)
    flags = (jnp.arange(SERIES_PLACES)[None, :] < counts[:, None]).astype(jnp.int32)
    return flags.reshape(N_FSDP * SERIES_PLACES)


def draw_mentor_states(key, part):
    own_key = jax.random.fold_in(key, 29)
    place = jnp.arange(TOKENS, dtype=jnp.float32) / float(TOKENS)
    row_scale = 0.5 * jnp.exp(place * jnp.log(6.0))
    base = jnp.clip(jax.random.normal(own_key, (TOKENS, D), jnp.float32), -4.0, 4.0)
    return (base * row_scale[:, None]).astype(jnp.bfloat16)


def raised(result, key, source, target, parts, factor):
    def block_of(axis_at):
        return (jnp.arange(result.shape[axis_at]) // (result.shape[axis_at] // parts)).reshape((-1,) + (1,) * (result.ndim - 1 - axis_at))

    first = jax.random.permutation(key, parts)[block_of(target)]
    second = (block_of(target) + parts // 2) % parts
    return jnp.where((block_of(source) == first) | (block_of(source) == second), factor * result, result)


def levels(stream_key, shape, cuts, least, high):
    level = 1.0
    for axis_at, blocks in cuts:
        heights = jax.random.uniform(jax.random.fold_in(jax.random.fold_in(stream_key, 6), axis_at), (blocks,), jnp.float32, least / len(cuts), high / len(cuts))
        level = level * jnp.repeat(jnp.exp(heights), shape[axis_at] // blocks).reshape((-1,) + (1,) * (len(shape) - 1 - axis_at))
    return level


def gaussian(key, dims, scale, bound, pieces=(), kind=jnp.bfloat16):
    result = scale * jax.random.normal(key, dims, jnp.float32)
    if pieces:
        result = result * levels(key, dims, pieces, -0.22, 0.18)
    return jnp.clip(result, -bound, bound).astype(kind)


def gaussian_with(rng, extent, scale, most, cuts, heavy, kind=jnp.bfloat16):
    entries = scale * jax.random.normal(rng, extent, jnp.float32)
    if cuts:
        entries = entries * levels(rng, extent, cuts, -0.22, 0.18)
    return jnp.clip(raised(entries, jax.random.fold_in(rng, 3), *heavy), -most, most).astype(kind)


def setup_inputs(seed: int = 0) -> dict:
    arg_keys = jax.random.split(jax.random.key(seed), 20)
    return {
        "entering_states": gaussian_with(arg_keys[0], (TOKENS, D), 1.0, 6.0, ((0, 32),), (0, 1, 32, 2.75)),
        "bypass_states": gaussian(arg_keys[1], (TOKENS, D), 1.0, 6.0, ((0, 32),)),
        "mentor_states": draw_mentor_states(jax.random.fold_in(arg_keys[19], 71), 0),
        "occupancy_mask": draw_occupancy_mask(jax.random.fold_in(arg_keys[19], 71), 0),
        "bypass_merge_matrix": gaussian(arg_keys[4], (2 * D, D), (2 * D) ** -0.5, 0.125, ((0, 32),)),
        "bypass_merge_offset": gaussian(arg_keys[5], (D,), 0.3, 1.5, ((0, 32),)),
        "mixer_layernorm_scale": jnp.clip(1.0 + 0.15 * jax.random.normal(arg_keys[6], (D,), jnp.float32), 0.25, 1.75).astype(jnp.bfloat16),
        "mixer_layernorm_offset": gaussian(arg_keys[7], (D,), 0.3, 1.5, ((0, 32),)),
        "asking_map_matrix": gaussian(arg_keys[8], (D, D), (D * 2 // 5) ** -0.5, 0.3125, ((0, 16), (1, 2))),
        "lookup_map_matrix": gaussian(arg_keys[9], (D, D), (D * 2 // 5) ** -0.5, 0.3125, ((0, 16), (1, 2))),
        "content_map_matrix": gaussian(arg_keys[10], (D, D), D ** -0.5, 0.1875, ((0, 16), (1, 2))),
        "mixer_result_matrix": gaussian(arg_keys[11], (D, D), (D // 2) ** -0.5, 0.25, ((0, 2), (1, 16))),
        "mixer_result_offset": gaussian(arg_keys[12], (D,), 0.3, 1.5, ((0, 32),)),
        "perceptron_layernorm_scale": jnp.clip(1.0 + 0.15 * jax.random.normal(arg_keys[13], (D,), jnp.float32), 0.25, 1.75).astype(jnp.bfloat16),
        "perceptron_layernorm_offset": gaussian(arg_keys[14], (D,), 0.3, 1.5, ((0, 32),)),
        "expand_layer_matrix": gaussian(arg_keys[15], (D, FF), D ** -0.5, 0.1875, ((0, 16), (1, 2))),
        "expand_layer_offset": gaussian(arg_keys[16], (FF,), 0.3, 1.5, ((0, 32),)),
        "contract_layer_matrix": gaussian(arg_keys[17], (FF, D), FF ** -0.5, 0.09375, ((0, 2), (1, 16))),
        "contract_layer_offset": gaussian(arg_keys[18], (D,), 0.3, 1.5, ((0, 32),)),
    }


EPSILON = 1e-05

@jax.custom_vjp
def low(v):
    return lax.optimization_barrier(v.astype(jnp.bfloat16)).astype(jnp.float32)

@jax.custom_vjp
def low_back(v):
    return v

def low_keep(v):
    return (low(v), None)

def low_pass(kept, grad):
    return (grad,)

def back_keep(v):
    return (v, None)

def back_low(kept, grad):
    return (low(grad),)
low.defvjp(low_keep, low_pass)
low_back.defvjp(back_keep, back_low)

def matmul(left, right):
    return jnp.dot(left, right, precision=lax.Precision.HIGHEST, preferred_element_type=jnp.float32)

def layer_norm(value, gain, shift):
    centred = value - lax.optimization_barrier(jnp.mean(value, axis=-1, keepdims=True))
    spread = lax.optimization_barrier(jnp.mean(centred * centred, axis=-1, keepdims=True))
    return centred * lax.rsqrt(spread + EPSILON) * gain + shift

def attend(queries, keys_all, values):
    scale = float(D // HEADS) ** (-0.5)
    scores = low_back(jnp.einsum('qhd,khd->hqk', queries, keys_all, precision=lax.Precision.HIGHEST) * scale)
    weights = jax.nn.softmax(scores, axis=-1)
    return jnp.einsum('hqk,khd->qhd', low(weights), values, precision=lax.Precision.HIGHEST)

def forward(entering_states, bypass_states, bypass_merge_matrix, bypass_merge_offset, mixer_layernorm_scale, mixer_layernorm_offset, asking_map_matrix, lookup_map_matrix, content_map_matrix, mixer_result_matrix, mixer_result_offset, perceptron_layernorm_scale, perceptron_layernorm_offset, expand_layer_matrix, expand_layer_offset, contract_layer_matrix, contract_layer_offset):
    width = D // HEADS
    checked = jax.checkpoint(attend)
    joined = jnp.concatenate([entering_states, bypass_states], axis=-1)
    merged = low_back(matmul(joined, bypass_merge_matrix)) + bypass_merge_offset
    first = low(layer_norm(merged, mixer_layernorm_scale, mixer_layernorm_offset))
    queries = low(low_back(matmul(first, asking_map_matrix))).reshape(SERIES_PLACES, SEQ_LEN, HEADS, width)
    keys_all = low(low_back(matmul(first, lookup_map_matrix))).reshape(SERIES_PLACES, SEQ_LEN, HEADS, width)
    values = low(low_back(matmul(first, content_map_matrix))).reshape(SERIES_PLACES, SEQ_LEN, HEADS, width)
    attended = lax.map(lambda item: checked(item[0], item[1], item[2]), (queries, keys_all, values))
    attended = low(low_back(attended.reshape(SERIES_PLACES * SEQ_LEN, D)))
    after_attn = merged + low_back(matmul(attended, mixer_result_matrix)) + mixer_result_offset
    second = low(layer_norm(after_attn, perceptron_layernorm_scale, perceptron_layernorm_offset))
    hidden = low_back(matmul(second, expand_layer_matrix) + expand_layer_offset)
    active = low(jax.nn.gelu(hidden, approximate=False))
    return after_attn + low_back(matmul(active, contract_layer_matrix)) + contract_layer_offset

def reference(entering_states, bypass_states, mentor_states, occupancy_mask, bypass_merge_matrix, bypass_merge_offset, mixer_layernorm_scale, mixer_layernorm_offset, asking_map_matrix, lookup_map_matrix, content_map_matrix, mixer_result_matrix, mixer_result_offset, perceptron_layernorm_scale, perceptron_layernorm_offset, expand_layer_matrix, expand_layer_offset, contract_layer_matrix, contract_layer_offset):
    group_rows = SERIES_PLACES * SEQ_LEN
    params = tuple((item.astype(jnp.float32) for item in (bypass_merge_matrix, bypass_merge_offset, mixer_layernorm_scale, mixer_layernorm_offset, asking_map_matrix, lookup_map_matrix, content_map_matrix, mixer_result_matrix, mixer_result_offset, perceptron_layernorm_scale, perceptron_layernorm_offset, expand_layer_matrix, expand_layer_offset, contract_layer_matrix, contract_layer_offset)))
    occupied_lines = occupancy_mask.reshape(N_FSDP, SERIES_PLACES).astype(jnp.float32)
    row_live = jnp.repeat(occupied_lines, SEQ_LEN, axis=1)
    stacked = (entering_states.astype(jnp.float32).reshape(N_FSDP, group_rows, D), bypass_states.astype(jnp.float32).reshape(N_FSDP, group_rows, D), mentor_states.astype(jnp.float32).reshape(N_FSDP, group_rows, D), row_live)

    def group_step(carry, item):
        sums, energy = carry
        rows, short, target, alive_tokens = item
        outcome, pull = jax.vjp(forward, rows, short, *params)
        alive_tokens = alive_tokens[:, None]
        miss = outcome - target
        grads = pull(alive_tokens * miss)
        sums = tuple((left + right for left, right in zip(sums, grads[2:])))
        energy = energy + 0.5 * jnp.sum(alive_tokens * miss * miss)
        return ((sums, energy), ((outcome * alive_tokens).astype(jnp.bfloat16), grads[0], grads[1]))
    zeros_init = tuple((jnp.zeros_like(item) for item in params))
    (sums, energy), (block, grad_rows, grad_short) = lax.scan(group_step, (zeros_init, jnp.zeros((), jnp.float32)), stacked)
    loss_value = energy / (jnp.sum(row_live) * D)
    return (block.reshape(N_FSDP * group_rows, D), loss_value, grad_rows.reshape(N_FSDP * group_rows, D), grad_short.reshape(N_FSDP * group_rows, D), sums[0], sums[1], sums[2], sums[3], sums[4], sums[5], sums[6], sums[7], sums[8], sums[9], sums[10], sums[11], sums[12], sums[13], sums[14])
```

```python
import jax
import jax.numpy as jnp
from jax import lax
from jax.sharding import PartitionSpec as P

D = 1024
HEADS = 16
SEQ_LEN = 1104


EPSILON = 1e-05


def layer_norm(value, gain, shift):
    centred = value - jnp.mean(value, axis=-1, keepdims=True)
    spread = jnp.mean(centred * centred, axis=-1, keepdims=True)
    return centred * lax.rsqrt(spread + EPSILON) * gain + shift


def contract_rows(left, right):
    return lax.dot_general(
        left, right, (((0,), (0,)), ((), ())), preferred_element_type=jnp.float32
    )


def contract_cols(left, right):
    return lax.dot_general(
        left, right, (((1,), (1,)), ((), ())), preferred_element_type=jnp.float32
    )


def attend_forward(queries, keys_all, values):
    scale = float(queries.shape[-1]) ** (-0.5)
    scores = (
        jnp.einsum("qhd,khd->hqk", queries, keys_all, preferred_element_type=jnp.float32) * scale
    )
    peak_score = jnp.max(scores, axis=-1, keepdims=True)
    raised = jnp.exp(scores - peak_score)
    row_total = jnp.sum(raised, axis=-1, keepdims=True)
    weights_low = (raised / row_total).astype(jnp.bfloat16)
    output = jnp.einsum("hqk,khd->qhd", weights_low, values, preferred_element_type=jnp.float32)
    return (output.astype(jnp.bfloat16), peak_score + jnp.log(row_total))


def attend_backward(queries, keys_all, values, summary, upstream):
    scale = float(queries.shape[-1]) ** (-0.5)
    scores = (
        jnp.einsum("qhd,khd->hqk", queries, keys_all, preferred_element_type=jnp.float32) * scale
    )
    probs_full = jnp.exp(scores - summary)
    grad_probs = jnp.einsum("qhd,khd->hqk", upstream, values, preferred_element_type=jnp.float32)
    grad_values = jnp.einsum(
        "hqk,qhd->khd",
        probs_full.astype(jnp.bfloat16),
        upstream,
        preferred_element_type=jnp.float32,
    )
    centre = jnp.sum(probs_full * grad_probs, axis=-1, keepdims=True)
    grad_scores = (probs_full * (grad_probs - centre)).astype(jnp.bfloat16)
    grad_queries = (
        jnp.einsum("hqk,khd->qhd", grad_scores, keys_all, preferred_element_type=jnp.float32)
        * scale
    )
    grad_keys = (
        jnp.einsum("hqk,qhd->khd", grad_scores, queries, preferred_element_type=jnp.float32) * scale
    )
    return (
        grad_queries.astype(jnp.bfloat16),
        grad_keys.astype(jnp.bfloat16),
        grad_values.astype(jnp.bfloat16),
    )


def gelu_exact(value):
    return jax.nn.gelu(value, approximate=False)


def per_device_split(
    entering_states,
    bypass_states,
    mentor_states,
    occupancy_mask,
    bypass_merge_matrix,
    bypass_merge_offset,
    mixer_layernorm_scale,
    mixer_layernorm_offset,
    asking_map_matrix,
    lookup_map_matrix,
    content_map_matrix,
    mixer_result_matrix,
    mixer_result_offset,
    perceptron_layernorm_scale,
    perceptron_layernorm_offset,
    expand_layer_matrix,
    expand_layer_offset,
    contract_layer_matrix,
    contract_layer_offset,
):
    rows = entering_states.shape[0]
    width = D // HEADS
    position = lax.axis_index("tp")
    (
        merge_full,
        merge_add,
        gain_one,
        shift_one,
        output_add,
        gain_two,
        shift_two,
        hidden_add,
        down_add,
    ) = (
        lax.all_gather(bypass_merge_matrix, ("fsdp", "tp"), axis=0, tiled=True),
        lax.all_gather(bypass_merge_offset, ("fsdp", "tp"), axis=0, tiled=True),
        lax.all_gather(mixer_layernorm_scale, ("fsdp", "tp"), axis=0, tiled=True),
        lax.all_gather(mixer_layernorm_offset, ("fsdp", "tp"), axis=0, tiled=True),
        lax.all_gather(mixer_result_offset, ("fsdp", "tp"), axis=0, tiled=True),
        lax.all_gather(perceptron_layernorm_scale, ("fsdp", "tp"), axis=0, tiled=True),
        lax.all_gather(perceptron_layernorm_offset, ("fsdp", "tp"), axis=0, tiled=True),
        lax.all_gather(expand_layer_offset, ("fsdp", "tp"), axis=0, tiled=True),
        lax.all_gather(contract_layer_offset, ("fsdp", "tp"), axis=0, tiled=True),
    )
    query_full, key_full, value_full, output_full, hidden_full, down_full = (
        lax.all_gather(asking_map_matrix, "fsdp", axis=0, tiled=True),
        lax.all_gather(lookup_map_matrix, "fsdp", axis=0, tiled=True),
        lax.all_gather(content_map_matrix, "fsdp", axis=0, tiled=True),
        lax.all_gather(mixer_result_matrix, "fsdp", axis=1, tiled=True),
        lax.all_gather(expand_layer_matrix, "fsdp", axis=0, tiled=True),
        lax.all_gather(contract_layer_matrix, "fsdp", axis=1, tiled=True),
    )
    gain_one = gain_one.astype(jnp.float32)
    shift_one = shift_one.astype(jnp.float32)
    gain_two = gain_two.astype(jnp.float32)
    shift_two = shift_two.astype(jnp.float32)
    project = jnp.concatenate([query_full, key_full, value_full], axis=1)
    local_width = query_full.shape[1]
    local_heads = local_width // width
    local_hidden = hidden_full.shape[1]
    row_index = position * rows + jnp.arange(rows, dtype=jnp.int32)
    slot_of_row = row_index // SEQ_LEN
    series_place_total = occupancy_mask.shape[0]
    agreeing_lines = (
        slot_of_row[:, None] == jnp.arange(series_place_total, dtype=jnp.int32)[None, :]
    ).astype(jnp.float32)
    alive_tokens = jnp.sum(
        agreeing_lines * occupancy_mask.astype(jnp.float32)[None, :], axis=1, keepdims=True
    )
    joined = jnp.concatenate([entering_states, bypass_states], axis=1)
    merged = jnp.dot(joined, merge_full, preferred_element_type=jnp.float32) + merge_add.astype(
        jnp.float32
    )
    first = layer_norm(merged, gain_one, shift_one).astype(jnp.bfloat16)
    first_all = lax.all_gather(first, "tp", axis=0, tiled=True)
    group_rows = first_all.shape[0]
    slots = group_rows // SEQ_LEN
    projected = jnp.dot(first_all, project, preferred_element_type=jnp.float32).astype(jnp.bfloat16)
    shaped = projected.reshape(slots, SEQ_LEN, 3, local_heads, width)
    queries = shaped[:, :, 0]
    keys_all = shaped[:, :, 1]
    values = shaped[:, :, 2]
    attended, summary = lax.map(
        lambda item: attend_forward(item[0], item[1], item[2]), (queries, keys_all, values)
    )
    attended_flat = attended.reshape(group_rows, local_width)
    attention_term = jnp.dot(attended_flat, output_full, preferred_element_type=jnp.float32)
    after_attn = (
        merged
        + lax.psum_scatter(
            attention_term.astype(jnp.bfloat16), "tp", scatter_dimension=0, tiled=True
        ).astype(jnp.float32)
        + output_add.astype(jnp.float32)
    )
    second = layer_norm(after_attn, gain_two, shift_two).astype(jnp.bfloat16)
    second_all = lax.all_gather(second, "tp", axis=0, tiled=True)
    hidden_slice = lax.dynamic_slice_in_dim(
        hidden_add.astype(jnp.float32), position * local_hidden, local_hidden, 0
    )
    hidden = jnp.dot(second_all, hidden_full, preferred_element_type=jnp.float32) + hidden_slice
    active = gelu_exact(hidden).astype(jnp.bfloat16)
    feed_term = jnp.dot(active, down_full, preferred_element_type=jnp.float32)
    final = (
        after_attn
        + lax.psum_scatter(
            feed_term.astype(jnp.bfloat16), "tp", scatter_dimension=0, tiled=True
        ).astype(jnp.float32)
        + down_add.astype(jnp.float32)
    )
    missing = final - mentor_states.astype(jnp.float32)
    grad_final = alive_tokens * missing
    block_out = (final * alive_tokens).astype(jnp.bfloat16)
    energy, counted = lax.psum(
        (0.5 * jnp.sum(grad_final * missing), jnp.sum(alive_tokens)), ("fsdp", "tp")
    )
    loss_value = energy / (counted * D)
    grad_down_bias = jnp.sum(grad_final, axis=0)
    upstream = grad_final.astype(jnp.bfloat16)
    upstream_all = lax.all_gather(upstream, "tp", axis=0, tiled=True)
    grad_down = contract_rows(active, upstream_all)
    grad_active = contract_cols(upstream_all, down_full)
    gelu_value, gelu_pull = jax.vjp(gelu_exact, hidden)
    grad_hidden = gelu_pull(grad_active)[0].astype(jnp.bfloat16)
    grad_hidden_local = jnp.sum(grad_hidden.astype(jnp.float32), axis=0)
    grad_hidden_weight = contract_rows(second_all, grad_hidden)
    feed_back_term = contract_cols(grad_hidden, hidden_full)
    grad_second = lax.psum_scatter(
        feed_back_term.astype(jnp.bfloat16), "tp", scatter_dimension=0, tiled=True
    ).astype(jnp.float32)
    hidden_bias_term = lax.dynamic_update_slice_in_dim(
        jnp.zeros((hidden_add.shape[0],), jnp.float32),
        grad_hidden_local,
        position * local_hidden,
        0,
    )
    norm_value, second_pull = jax.vjp(layer_norm, after_attn, gain_two, shift_two)
    back_after, grad_gain_two, grad_shift_two = second_pull(grad_second)
    grad_after = grad_final + back_after
    grad_output_bias = jnp.sum(grad_after, axis=0)
    branch_all = lax.all_gather(grad_after.astype(jnp.bfloat16), "tp", axis=0, tiled=True)
    grad_output_weight = contract_rows(attended_flat, branch_all)
    grad_attended = contract_cols(branch_all, output_full).astype(jnp.bfloat16)
    upstream_heads = grad_attended.reshape(slots, SEQ_LEN, local_heads, width)
    grad_q_heads, grad_k_heads, grad_v_heads = lax.map(
        lambda item: attend_backward(item[0], item[1], item[2], item[3], item[4]),
        (queries, keys_all, values, summary, upstream_heads),
    )
    grad_projected = jnp.stack([grad_q_heads, grad_k_heads, grad_v_heads], axis=2).reshape(
        group_rows, 3 * local_width
    )
    grad_project = contract_rows(first_all, grad_projected)
    attention_back_term = contract_cols(grad_projected, project)
    grad_first = lax.psum_scatter(
        attention_back_term.astype(jnp.bfloat16), "tp", scatter_dimension=0, tiled=True
    ).astype(jnp.float32)
    first_value, first_pull = jax.vjp(layer_norm, merged, gain_one, shift_one)
    back_merged, grad_gain_one, grad_shift_one = first_pull(grad_first)
    grad_merged = grad_after + back_merged
    grad_merge_bias = jnp.sum(grad_merged, axis=0)
    merge_grad = grad_merged.astype(jnp.bfloat16)
    grad_merge_weight = contract_rows(joined, merge_grad)
    grad_joined = contract_cols(merge_grad, merge_full)
    model_width = entering_states.shape[1]
    grad_tokens = grad_joined[:, :model_width]
    grad_shortcut = grad_joined[:, model_width:]
    grad_query, grad_key, grad_value, grad_output, grad_hidden_full, grad_down_full = (
        lax.psum_scatter(
            grad_project[:, :local_width].astype(jnp.bfloat16),
            "fsdp",
            scatter_dimension=0,
            tiled=True,
        ).astype(jnp.float32),
        lax.psum_scatter(
            grad_project[:, local_width : 2 * local_width].astype(jnp.bfloat16),
            "fsdp",
            scatter_dimension=0,
            tiled=True,
        ).astype(jnp.float32),
        lax.psum_scatter(
            grad_project[:, 2 * local_width :].astype(jnp.bfloat16),
            "fsdp",
            scatter_dimension=0,
            tiled=True,
        ).astype(jnp.float32),
        lax.psum_scatter(
            grad_output_weight.astype(jnp.bfloat16), "fsdp", scatter_dimension=1, tiled=True
        ).astype(jnp.float32),
        lax.psum_scatter(
            grad_hidden_weight.astype(jnp.bfloat16), "fsdp", scatter_dimension=0, tiled=True
        ).astype(jnp.float32),
        lax.psum_scatter(
            grad_down.astype(jnp.bfloat16), "fsdp", scatter_dimension=1, tiled=True
        ).astype(jnp.float32),
    )
    (
        merge_weight_sum,
        merge_bias_sum,
        gain_one_sum,
        shift_one_sum,
        output_bias_sum,
        gain_two_sum,
        shift_two_sum,
        hidden_bias_sum,
        down_bias_sum,
    ) = (
        lax.psum_scatter(grad_merge_weight, ("fsdp", "tp"), scatter_dimension=0, tiled=True),
        lax.psum_scatter(grad_merge_bias, ("fsdp", "tp"), scatter_dimension=0, tiled=True),
        lax.psum_scatter(grad_gain_one, ("fsdp", "tp"), scatter_dimension=0, tiled=True),
        lax.psum_scatter(grad_shift_one, ("fsdp", "tp"), scatter_dimension=0, tiled=True),
        lax.psum_scatter(grad_output_bias, ("fsdp", "tp"), scatter_dimension=0, tiled=True),
        lax.psum_scatter(grad_gain_two, ("fsdp", "tp"), scatter_dimension=0, tiled=True),
        lax.psum_scatter(grad_shift_two, ("fsdp", "tp"), scatter_dimension=0, tiled=True),
        lax.psum_scatter(hidden_bias_term, ("fsdp", "tp"), scatter_dimension=0, tiled=True),
        lax.psum_scatter(grad_down_bias, ("fsdp", "tp"), scatter_dimension=0, tiled=True),
    )
    return (
        block_out,
        loss_value,
        grad_tokens,
        grad_shortcut,
        merge_weight_sum,
        merge_bias_sum,
        gain_one_sum,
        shift_one_sum,
        grad_query,
        grad_key,
        grad_value,
        grad_output,
        output_bias_sum,
        gain_two_sum,
        shift_two_sum,
        grad_hidden_full,
        hidden_bias_sum,
        grad_down_full,
        down_bias_sum,
    )


def one_sequence_plan(
    entering_states,
    bypass_states,
    mentor_states,
    occupancy_mask,
    bypass_merge_matrix,
    bypass_merge_offset,
    mixer_layernorm_scale,
    mixer_layernorm_offset,
    asking_map_matrix,
    lookup_map_matrix,
    content_map_matrix,
    mixer_result_matrix,
    mixer_result_offset,
    perceptron_layernorm_scale,
    perceptron_layernorm_offset,
    expand_layer_matrix,
    expand_layer_offset,
    contract_layer_matrix,
    contract_layer_offset,
):
    f32, bf16 = jnp.float32, jnp.bfloat16
    rows, d = entering_states.shape
    width = d // HEADS
    col = asking_map_matrix.shape[1]
    ffl = expand_layer_matrix.shape[1]
    r = asking_map_matrix.shape[0]
    nf = d // r
    nt = d // col
    everyone = ("z", "y", "c", "x")
    at = {axis: lax.axis_index(axis) for axis in everyone}
    small = (
        bypass_merge_offset,
        mixer_layernorm_scale,
        mixer_layernorm_offset,
        mixer_result_offset,
        perceptron_layernorm_scale,
        perceptron_layernorm_offset,
        contract_layer_offset,
        expand_layer_offset,
    )
    flat = jnp.concatenate(small)
    flat = jnp.pad(flat, (0, 16 * col - flat.shape[0])).reshape(16, col)
    early = jnp.concatenate(
        [
            bypass_merge_matrix.reshape(-1, col),
            asking_map_matrix,
            lookup_map_matrix,
            content_map_matrix,
            mixer_result_matrix.T,
            flat,
        ],
        axis=0,
    )
    early = lax.all_gather(early, everyone, axis=0, tiled=False)
    late = jnp.concatenate([expand_layer_matrix, contract_layer_matrix.T], axis=0)
    late = lax.all_gather(late, everyone, axis=0, tiled=False)
    mrows = bypass_merge_matrix.size // col
    merge_full = early[:, :mrows].reshape(-1, d)

    def columns(block, start, count):
        part = block.reshape((nf, nt) + block.shape[1:])[:, :, start : start + count]
        return part.transpose(0, 2, 1, 3).reshape(nf * count, -1)

    project = jnp.concatenate([columns(early, mrows + i * r, r) for i in range(3)], axis=1)
    output_t = columns(early, mrows + 3 * r, r)
    hidden_full = columns(late, 0, r)
    down_t = columns(late, r, r)
    vec = early[:, mrows + 4 * r :].reshape(nf * nt, -1)
    vectors, offset = [], 0
    for item in small:
        n = item.shape[0]
        vectors.append(vec[:, offset : offset + n].reshape(-1).astype(f32))
        offset += n
    merge_add, gain_one, shift_one, output_add, gain_two, shift_two, down_add, hidden_add = vectors

    alive = lax.dynamic_index_in_dim(occupancy_mask, at["x"], keepdims=False).astype(f32)
    joined = jnp.concatenate([entering_states, bypass_states], axis=1)
    merged = jnp.dot(joined, merge_full, preferred_element_type=f32) + merge_add
    first = layer_norm(merged, gain_one, shift_one).astype(bf16)
    projected = jnp.dot(first, project, preferred_element_type=f32).astype(bf16)
    shaped = projected.reshape(rows, 3, 2, HEADS // 2, width)
    queries, keys_all, values = (jnp.moveaxis(shaped[:, i], 1, 0) for i in range(3))
    attended, summary = lax.map(
        lambda item: attend_forward(item[0], item[1], item[2]), (queries, keys_all, values)
    )
    attended = jnp.moveaxis(attended, 0, 1).reshape(rows, d)
    after_attn = merged + contract_cols(attended, output_t) + output_add
    second = layer_norm(after_attn, gain_two, shift_two).astype(bf16)
    hidden = jnp.dot(second, hidden_full, preferred_element_type=f32) + hidden_add
    active = gelu_exact(hidden).astype(bf16)
    final = after_attn + contract_cols(active, down_t) + down_add
    missing = final - mentor_states.astype(f32)
    grad_final = alive * missing
    block_out = (final * alive).astype(bf16)
    energy, counted = lax.psum(
        (0.5 * jnp.sum(grad_final * missing), alive * float(rows)), everyone
    )
    loss_value = energy / (counted * d)
    grad_down_bias = jnp.sum(grad_final, axis=0)
    upstream = grad_final.astype(bf16)

    def exchange(value, axis):
        return lax.ppermute(value, axis, [(0, 1), (1, 0)])

    def pick(value, index, dim):
        return lax.dynamic_index_in_dim(value, index, dim, keepdims=False)

    def halve(value, axis, dim):
        here = at[axis]
        got = exchange(pick(value, 1 - here, dim), axis)
        return (pick(value, here, dim).astype(f32) + got.astype(f32)).astype(value.dtype)

    def line(value, dim):
        here = at["z"]
        total = pick(value, here, dim).astype(f32)
        for k in range(1, 4):
            target = lax.rem(here + k, 4)
            got = lax.ppermute(
                pick(value, target, dim), "z", [(i, (i + k) % 4) for i in range(4)]
            )
            total = total + got.astype(f32)
        return total

    def shared(value):
        value = halve(value, "c", 2)
        half = value.shape[-1] // 2
        left = halve(halve(value[..., :half], "x", 2), "y", 1)
        right = halve(halve(value[..., half:], "y", 1), "x", 1)
        return line(jnp.concatenate([left, right], axis=-1), 0)

    def blocks(value):
        return value.reshape(4, 2, 2, r, nt, -1).transpose(0, 1, 2, 4, 3, 5)

    grad_down = shared(blocks(contract_rows(upstream, active).astype(bf16)))
    grad_active = jnp.dot(upstream, down_t, preferred_element_type=f32)
    gelu_value, gelu_pull = jax.vjp(gelu_exact, hidden)
    grad_hidden = gelu_pull(grad_active)[0].astype(bf16)
    hidden_bias_term = jnp.sum(grad_hidden.astype(f32), axis=0)
    grad_hidden_weight = shared(blocks(contract_rows(second, grad_hidden).astype(bf16)))
    grad_second = contract_cols(grad_hidden, hidden_full)
    norm_value, second_pull = jax.vjp(layer_norm, after_attn, gain_two, shift_two)
    back_after, grad_gain_two, grad_shift_two = second_pull(grad_second)
    grad_after = grad_final + back_after
    grad_output_bias = jnp.sum(grad_after, axis=0)
    branch = grad_after.astype(bf16)
    grad_output_t = contract_rows(branch, attended).astype(bf16)
    grad_attended = jnp.dot(branch, output_t, preferred_element_type=f32).astype(bf16)
    upstream_heads = jnp.moveaxis(grad_attended.reshape(rows, 2, HEADS // 2, width), 1, 0)
    grad_qkv = lax.map(
        lambda item: attend_backward(item[0], item[1], item[2], item[3], item[4]),
        (queries, keys_all, values, summary, upstream_heads),
    )
    grad_projected = jnp.concatenate(
        [jnp.moveaxis(g, 0, 1).reshape(rows, d) for g in grad_qkv], axis=1
    )
    grad_project = contract_rows(first, grad_projected).astype(bf16)
    four = jnp.concatenate(
        [blocks(grad_project[:, i * d : (i + 1) * d]) for i in range(3)] + [blocks(grad_output_t)],
        axis=-1,
    )
    four = shared(four)
    grad_first = contract_cols(grad_projected, project)
    first_value, first_pull = jax.vjp(layer_norm, merged, gain_one, shift_one)
    back_merged, grad_gain_one, grad_shift_one = first_pull(grad_first)
    grad_merged = grad_after + back_merged
    grad_merge_bias = jnp.sum(grad_merged, axis=0)
    merge_grad = grad_merged.astype(bf16)
    grad_joined = contract_cols(merge_grad, merge_full)
    merge_weight = shared(
        contract_rows(joined, merge_grad).astype(bf16).reshape(4, 2, 2, nt, -1, d)
    )
    terms = (
        grad_merge_bias,
        grad_gain_one,
        grad_shift_one,
        grad_output_bias,
        grad_gain_two,
        grad_shift_two,
        grad_down_bias,
        hidden_bias_term,
    )
    stacked = jnp.concatenate([item.reshape(nf * nt, -1) for item in terms], axis=1)
    stacked = lax.psum_scatter(stacked, everyone, scatter_dimension=0, tiled=True).reshape(-1)
    sums, offset = [], 0
    for item in small:
        n = item.shape[0]
        sums.append(stacked[offset : offset + n])
        offset += n
    return (
        block_out,
        loss_value,
        grad_joined[:, :d],
        grad_joined[:, d:],
        merge_weight,
        sums[0],
        sums[1],
        sums[2],
        four[:, :col],
        four[:, col : 2 * col],
        four[:, 2 * col : 3 * col],
        four[:, 3 * col :].T,
        sums[3],
        sums[4],
        sums[5],
        grad_hidden_weight,
        sums[7],
        grad_down.T,
        sums[6],
    )


ARGUMENTS = (
    ("ft", None),
    ("ft", None),
    ("ft", None),
    ("f",),
    ("ft", None),
    ("ft",),
    ("ft",),
    ("ft",),
    ("f", "t"),
    ("f", "t"),
    ("f", "t"),
    ("t", "f"),
    ("ft",),
    ("ft",),
    ("ft",),
    ("f", "t"),
    ("ft",),
    ("t", "f"),
    ("ft",),
)
RESULTS = (
    ("ft", None),
    (),
    ("ft", None),
    ("ft", None),
    ("ft", None),
    ("ft",),
    ("ft",),
    ("ft",),
    ("f", "t"),
    ("f", "t"),
    ("f", "t"),
    ("t", "f"),
    ("ft",),
    ("ft",),
    ("ft",),
    ("f", "t"),
    ("ft",),
    ("t", "f"),
    ("ft",),
)


def solution(mesh):
    def whole(*args):
        rows = args[0].shape[0] // mesh.size
        if rows == SEQ_LEN and dict(mesh.shape) == {"fsdp": 16, "tp": 2}:
            plan = one_sequence_plan
            use = jax.sharding.Mesh(mesh.devices.reshape(4, 2, 2, 2), ("z", "y", "c", "x"))
            names = {"f": ("z", "y", "c"), "t": ("x",), "ft": ("z", "y", "c", "x")}
        else:
            plan = per_device_split
            use = mesh
            names = {"f": ("fsdp",), "t": ("tp",), "ft": ("fsdp", "tp")}

        def place(entry):
            return P(*(None if e is None else names[e] for e in entry))

        return jax.shard_map(
            plan,
            mesh=use,
            in_specs=tuple(place(e) for e in ARGUMENTS),
            out_specs=tuple(place(e) for e in RESULTS),
            check_vma=False,
        )(*args)

    return whole
```

```python
import functools
import math

import jax
import jax.numpy as jnp
from jax import lax
from jax.experimental import pallas as pl
from jax.experimental.pallas import tpu as pltpu
from jax.sharding import PartitionSpec as P

D = 1024
HEADS = 16
SEQ_LEN = 1104


EPSILON = 1e-05


def layer_norm(value, gain, shift):
    centred = value - jnp.mean(value, axis=-1, keepdims=True)
    spread = jnp.mean(centred * centred, axis=-1, keepdims=True)
    return centred * lax.rsqrt(spread + EPSILON) * gain + shift


def contract_rows(left, right):
    return lax.dot_general(
        left, right, (((0,), (0,)), ((), ())), preferred_element_type=jnp.float32
    )


def contract_cols(left, right):
    return lax.dot_general(
        left, right, (((1,), (1,)), ((), ())), preferred_element_type=jnp.float32
    )


def attend_forward(queries, keys_all, values):
    scale = float(queries.shape[-1]) ** (-0.5)
    scores = (
        jnp.einsum("qhd,khd->hqk", queries, keys_all, preferred_element_type=jnp.float32) * scale
    )
    peak_score = jnp.max(scores, axis=-1, keepdims=True)
    raised = jnp.exp(scores - peak_score)
    row_total = jnp.sum(raised, axis=-1, keepdims=True)
    weights_low = (raised / row_total).astype(jnp.bfloat16)
    output = jnp.einsum("hqk,khd->qhd", weights_low, values, preferred_element_type=jnp.float32)
    return (output.astype(jnp.bfloat16), peak_score + jnp.log(row_total))


def attend_backward(queries, keys_all, values, summary, upstream):
    scale = float(queries.shape[-1]) ** (-0.5)
    scores = (
        jnp.einsum("qhd,khd->hqk", queries, keys_all, preferred_element_type=jnp.float32) * scale
    )
    probs_full = jnp.exp(scores - summary)
    grad_probs = jnp.einsum("qhd,khd->hqk", upstream, values, preferred_element_type=jnp.float32)
    grad_values = jnp.einsum(
        "hqk,qhd->khd",
        probs_full.astype(jnp.bfloat16),
        upstream,
        preferred_element_type=jnp.float32,
    )
    centre = jnp.sum(probs_full * grad_probs, axis=-1, keepdims=True)
    grad_scores = (probs_full * (grad_probs - centre)).astype(jnp.bfloat16)
    grad_queries = (
        jnp.einsum("hqk,khd->qhd", grad_scores, keys_all, preferred_element_type=jnp.float32)
        * scale
    )
    grad_keys = (
        jnp.einsum("hqk,qhd->khd", grad_scores, queries, preferred_element_type=jnp.float32) * scale
    )
    return (
        grad_queries.astype(jnp.bfloat16),
        grad_keys.astype(jnp.bfloat16),
        grad_values.astype(jnp.bfloat16),
    )


def gelu_exact(value):
    return jax.nn.gelu(value, approximate=False)


def per_device_split(
    entering_states,
    bypass_states,
    mentor_states,
    occupancy_mask,
    bypass_merge_matrix,
    bypass_merge_offset,
    mixer_layernorm_scale,
    mixer_layernorm_offset,
    asking_map_matrix,
    lookup_map_matrix,
    content_map_matrix,
    mixer_result_matrix,
    mixer_result_offset,
    perceptron_layernorm_scale,
    perceptron_layernorm_offset,
    expand_layer_matrix,
    expand_layer_offset,
    contract_layer_matrix,
    contract_layer_offset,
):
    rows = entering_states.shape[0]
    width = D // HEADS
    position = lax.axis_index("tp")
    (
        merge_full,
        merge_add,
        gain_one,
        shift_one,
        output_add,
        gain_two,
        shift_two,
        hidden_add,
        down_add,
    ) = (
        lax.all_gather(bypass_merge_matrix, ("fsdp", "tp"), axis=0, tiled=True),
        lax.all_gather(bypass_merge_offset, ("fsdp", "tp"), axis=0, tiled=True),
        lax.all_gather(mixer_layernorm_scale, ("fsdp", "tp"), axis=0, tiled=True),
        lax.all_gather(mixer_layernorm_offset, ("fsdp", "tp"), axis=0, tiled=True),
        lax.all_gather(mixer_result_offset, ("fsdp", "tp"), axis=0, tiled=True),
        lax.all_gather(perceptron_layernorm_scale, ("fsdp", "tp"), axis=0, tiled=True),
        lax.all_gather(perceptron_layernorm_offset, ("fsdp", "tp"), axis=0, tiled=True),
        lax.all_gather(expand_layer_offset, ("fsdp", "tp"), axis=0, tiled=True),
        lax.all_gather(contract_layer_offset, ("fsdp", "tp"), axis=0, tiled=True),
    )
    query_full, key_full, value_full, output_full, hidden_full, down_full = (
        lax.all_gather(asking_map_matrix, "fsdp", axis=0, tiled=True),
        lax.all_gather(lookup_map_matrix, "fsdp", axis=0, tiled=True),
        lax.all_gather(content_map_matrix, "fsdp", axis=0, tiled=True),
        lax.all_gather(mixer_result_matrix, "fsdp", axis=1, tiled=True),
        lax.all_gather(expand_layer_matrix, "fsdp", axis=0, tiled=True),
        lax.all_gather(contract_layer_matrix, "fsdp", axis=1, tiled=True),
    )
    gain_one = gain_one.astype(jnp.float32)
    shift_one = shift_one.astype(jnp.float32)
    gain_two = gain_two.astype(jnp.float32)
    shift_two = shift_two.astype(jnp.float32)
    project = jnp.concatenate([query_full, key_full, value_full], axis=1)
    local_width = query_full.shape[1]
    local_heads = local_width // width
    local_hidden = hidden_full.shape[1]
    row_index = position * rows + jnp.arange(rows, dtype=jnp.int32)
    slot_of_row = row_index // SEQ_LEN
    series_place_total = occupancy_mask.shape[0]
    agreeing_lines = (
        slot_of_row[:, None] == jnp.arange(series_place_total, dtype=jnp.int32)[None, :]
    ).astype(jnp.float32)
    alive_tokens = jnp.sum(
        agreeing_lines * occupancy_mask.astype(jnp.float32)[None, :], axis=1, keepdims=True
    )
    joined = jnp.concatenate([entering_states, bypass_states], axis=1)
    merged = jnp.dot(joined, merge_full, preferred_element_type=jnp.float32) + merge_add.astype(
        jnp.float32
    )
    first = layer_norm(merged, gain_one, shift_one).astype(jnp.bfloat16)
    first_all = lax.all_gather(first, "tp", axis=0, tiled=True)
    group_rows = first_all.shape[0]
    slots = group_rows // SEQ_LEN
    projected = jnp.dot(first_all, project, preferred_element_type=jnp.float32).astype(jnp.bfloat16)
    shaped = projected.reshape(slots, SEQ_LEN, 3, local_heads, width)
    queries = shaped[:, :, 0]
    keys_all = shaped[:, :, 1]
    values = shaped[:, :, 2]
    attended, summary = lax.map(
        lambda item: attend_forward(item[0], item[1], item[2]), (queries, keys_all, values)
    )
    attended_flat = attended.reshape(group_rows, local_width)
    attention_term = jnp.dot(attended_flat, output_full, preferred_element_type=jnp.float32)
    after_attn = (
        merged
        + lax.psum_scatter(
            attention_term.astype(jnp.bfloat16), "tp", scatter_dimension=0, tiled=True
        ).astype(jnp.float32)
        + output_add.astype(jnp.float32)
    )
    second = layer_norm(after_attn, gain_two, shift_two).astype(jnp.bfloat16)
    second_all = lax.all_gather(second, "tp", axis=0, tiled=True)
    hidden_slice = lax.dynamic_slice_in_dim(
        hidden_add.astype(jnp.float32), position * local_hidden, local_hidden, 0
    )
    hidden = jnp.dot(second_all, hidden_full, preferred_element_type=jnp.float32) + hidden_slice
    active = gelu_exact(hidden).astype(jnp.bfloat16)
    feed_term = jnp.dot(active, down_full, preferred_element_type=jnp.float32)
    final = (
        after_attn
        + lax.psum_scatter(
            feed_term.astype(jnp.bfloat16), "tp", scatter_dimension=0, tiled=True
        ).astype(jnp.float32)
        + down_add.astype(jnp.float32)
    )
    missing = final - mentor_states.astype(jnp.float32)
    grad_final = alive_tokens * missing
    block_out = (final * alive_tokens).astype(jnp.bfloat16)
    energy, counted = lax.psum(
        (0.5 * jnp.sum(grad_final * missing), jnp.sum(alive_tokens)), ("fsdp", "tp")
    )
    loss_value = energy / (counted * D)
    grad_down_bias = jnp.sum(grad_final, axis=0)
    upstream = grad_final.astype(jnp.bfloat16)
    upstream_all = lax.all_gather(upstream, "tp", axis=0, tiled=True)
    grad_down = contract_rows(active, upstream_all)
    grad_active = contract_cols(upstream_all, down_full)
    gelu_value, gelu_pull = jax.vjp(gelu_exact, hidden)
    grad_hidden = gelu_pull(grad_active)[0].astype(jnp.bfloat16)
    grad_hidden_local = jnp.sum(grad_hidden.astype(jnp.float32), axis=0)
    grad_hidden_weight = contract_rows(second_all, grad_hidden)
    feed_back_term = contract_cols(grad_hidden, hidden_full)
    grad_second = lax.psum_scatter(
        feed_back_term.astype(jnp.bfloat16), "tp", scatter_dimension=0, tiled=True
    ).astype(jnp.float32)
    hidden_bias_term = lax.dynamic_update_slice_in_dim(
        jnp.zeros((hidden_add.shape[0],), jnp.float32),
        grad_hidden_local,
        position * local_hidden,
        0,
    )
    norm_value, second_pull = jax.vjp(layer_norm, after_attn, gain_two, shift_two)
    back_after, grad_gain_two, grad_shift_two = second_pull(grad_second)
    grad_after = grad_final + back_after
    grad_output_bias = jnp.sum(grad_after, axis=0)
    branch_all = lax.all_gather(grad_after.astype(jnp.bfloat16), "tp", axis=0, tiled=True)
    grad_output_weight = contract_rows(attended_flat, branch_all)
    grad_attended = contract_cols(branch_all, output_full).astype(jnp.bfloat16)
    upstream_heads = grad_attended.reshape(slots, SEQ_LEN, local_heads, width)
    grad_q_heads, grad_k_heads, grad_v_heads = lax.map(
        lambda item: attend_backward(item[0], item[1], item[2], item[3], item[4]),
        (queries, keys_all, values, summary, upstream_heads),
    )
    grad_projected = jnp.stack([grad_q_heads, grad_k_heads, grad_v_heads], axis=2).reshape(
        group_rows, 3 * local_width
    )
    grad_project = contract_rows(first_all, grad_projected)
    attention_back_term = contract_cols(grad_projected, project)
    grad_first = lax.psum_scatter(
        attention_back_term.astype(jnp.bfloat16), "tp", scatter_dimension=0, tiled=True
    ).astype(jnp.float32)
    first_value, first_pull = jax.vjp(layer_norm, merged, gain_one, shift_one)
    back_merged, grad_gain_one, grad_shift_one = first_pull(grad_first)
    grad_merged = grad_after + back_merged
    grad_merge_bias = jnp.sum(grad_merged, axis=0)
    merge_grad = grad_merged.astype(jnp.bfloat16)
    grad_merge_weight = contract_rows(joined, merge_grad)
    grad_joined = contract_cols(merge_grad, merge_full)
    model_width = entering_states.shape[1]
    grad_tokens = grad_joined[:, :model_width]
    grad_shortcut = grad_joined[:, model_width:]
    grad_query, grad_key, grad_value, grad_output, grad_hidden_full, grad_down_full = (
        lax.psum_scatter(
            grad_project[:, :local_width].astype(jnp.bfloat16),
            "fsdp",
            scatter_dimension=0,
            tiled=True,
        ).astype(jnp.float32),
        lax.psum_scatter(
            grad_project[:, local_width : 2 * local_width].astype(jnp.bfloat16),
            "fsdp",
            scatter_dimension=0,
            tiled=True,
        ).astype(jnp.float32),
        lax.psum_scatter(
            grad_project[:, 2 * local_width :].astype(jnp.bfloat16),
            "fsdp",
            scatter_dimension=0,
            tiled=True,
        ).astype(jnp.float32),
        lax.psum_scatter(
            grad_output_weight.astype(jnp.bfloat16), "fsdp", scatter_dimension=1, tiled=True
        ).astype(jnp.float32),
        lax.psum_scatter(
            grad_hidden_weight.astype(jnp.bfloat16), "fsdp", scatter_dimension=0, tiled=True
        ).astype(jnp.float32),
        lax.psum_scatter(
            grad_down.astype(jnp.bfloat16), "fsdp", scatter_dimension=1, tiled=True
        ).astype(jnp.float32),
    )
    (
        merge_weight_sum,
        merge_bias_sum,
        gain_one_sum,
        shift_one_sum,
        output_bias_sum,
        gain_two_sum,
        shift_two_sum,
        hidden_bias_sum,
        down_bias_sum,
    ) = (
        lax.psum_scatter(grad_merge_weight, ("fsdp", "tp"), scatter_dimension=0, tiled=True),
        lax.psum_scatter(grad_merge_bias, ("fsdp", "tp"), scatter_dimension=0, tiled=True),
        lax.psum_scatter(grad_gain_one, ("fsdp", "tp"), scatter_dimension=0, tiled=True),
        lax.psum_scatter(grad_shift_one, ("fsdp", "tp"), scatter_dimension=0, tiled=True),
        lax.psum_scatter(grad_output_bias, ("fsdp", "tp"), scatter_dimension=0, tiled=True),
        lax.psum_scatter(grad_gain_two, ("fsdp", "tp"), scatter_dimension=0, tiled=True),
        lax.psum_scatter(grad_shift_two, ("fsdp", "tp"), scatter_dimension=0, tiled=True),
        lax.psum_scatter(hidden_bias_term, ("fsdp", "tp"), scatter_dimension=0, tiled=True),
        lax.psum_scatter(grad_down_bias, ("fsdp", "tp"), scatter_dimension=0, tiled=True),
    )
    return (
        block_out,
        loss_value,
        grad_tokens,
        grad_shortcut,
        merge_weight_sum,
        merge_bias_sum,
        gain_one_sum,
        shift_one_sum,
        grad_query,
        grad_key,
        grad_value,
        grad_output,
        output_bias_sum,
        gain_two_sum,
        shift_two_sum,
        grad_hidden_full,
        hidden_bias_sum,
        grad_down_full,
        down_bias_sum,
    )


LOG2E = math.log2(math.e)
PAIR = 128
CHUNK = 368


def nn(a, b):
    return lax.dot_general(a, b, (((1,), (0,)), ((), ())), preferred_element_type=jnp.float32)


def nt(a, b):
    return lax.dot_general(a, b, (((1,), (1,)), ((), ())), preferred_element_type=jnp.float32)


def tn(a, b):
    return lax.dot_general(a, b, (((0,), (0,)), ((), ())), preferred_element_type=jnp.float32)


def vmem(mib):
    return pltpu.CompilerParams(vmem_limit_bytes=mib * 2**20)


def attention_forward_kernel(q_ref, k_ref, v_ref, o_ref, l_ref):
    count = q_ref.shape[0]
    scale = (PAIR // 2) ** -0.5 * LOG2E
    low = lax.broadcasted_iota(jnp.int32, (1, PAIR), 1) < PAIR // 2
    keys, values = k_ref[...], v_ref[...]
    zero = jnp.zeros_like(keys)
    heads = (jnp.where(low, keys, zero), jnp.where(low, zero, keys))
    wide = jnp.concatenate([values, jnp.ones_like(values)], axis=1)
    for start in range(0, count, CHUNK):
        part = slice(start, min(start + CHUNK, count))
        queries = q_ref[part, :]
        outs, sums = [], []
        for head in heads:
            scores = nt(queries, head)
            peak = jnp.max(scores, axis=1, keepdims=True) * scale
            raised = jnp.exp2(scores * scale - peak).astype(jnp.bfloat16)
            both = nn(raised, wide)
            total = both[:, PAIR:]
            outs.append(both[:, :PAIR] / total)
            sums.append(peak + jnp.log2(total))
        o_ref[part, :] = jnp.where(low, outs[0], outs[1]).astype(jnp.bfloat16)
        l_ref[part, :] = jnp.where(low, sums[0], sums[1])


def attention_backward_kernel(q_ref, k_ref, v_ref, o_ref, l_ref, u_ref, out_ref, total_ref):
    count = q_ref.shape[0]
    plain = (PAIR // 2) ** -0.5
    scale = plain * LOG2E
    low = lax.broadcasted_iota(jnp.int32, (1, PAIR), 1) < PAIR // 2
    queries, upstream = q_ref[...], u_ref[...]
    product = upstream.astype(jnp.float32) * o_ref[...].astype(jnp.float32)
    left = jnp.sum(jnp.where(low, product, 0.0), axis=1, keepdims=True)
    right = jnp.sum(jnp.where(low, 0.0, product), axis=1, keepdims=True)
    centres = jnp.transpose(jnp.where(low, left, right))
    logs = jnp.transpose(l_ref[...])
    for head in range(2):

        def own(value):
            zero = jnp.zeros_like(value)
            return jnp.where(low, value, zero) if head == 0 else jnp.where(low, zero, value)

        row = head * (PAIR // 2)
        own_queries, own_upstream = own(queries), own(upstream)
        log_row, centre = logs[row : row + 1, :], centres[row : row + 1, :]
        for start in range(0, count, CHUNK):
            part = slice(start, min(start + CHUNK, count))
            keys, values = k_ref[part, :], v_ref[part, :]
            probs = jnp.exp2(nt(keys, own_queries) * scale - log_row)
            slopes = (probs * (nt(values, own_upstream) - centre)).astype(jnp.bfloat16)
            grad_v = nn(probs.astype(jnp.bfloat16), own_upstream).astype(jnp.bfloat16)
            grad_k = (nn(slopes, own_queries) * plain).astype(jnp.bfloat16)
            grad_q = tn(slopes, own(keys))
            if head == 0:
                out_ref[1, part, :] = grad_k
                out_ref[2, part, :] = grad_v
            else:
                out_ref[1, part, :] = jnp.where(low, out_ref[1, part, :], grad_k)
                out_ref[2, part, :] = jnp.where(low, out_ref[2, part, :], grad_v)
            if head == 0 and start == 0:
                total_ref[...] = grad_q
            else:
                total_ref[...] += grad_q
    out_ref[0] = (total_ref[...] * plain).astype(jnp.bfloat16)


def attention_cost(rows, pairs, products):
    return pl.CostEstimate(
        flops=products * 2 * rows * rows * PAIR * 2 * pairs,
        bytes_accessed=8 * rows * PAIR * pairs * 2,
        transcendentals=rows * rows * 2 * pairs,
    )


def attention_forward(projected):
    rows, columns = projected.shape
    pairs = columns // 3 // PAIR

    def block(offset):
        return pl.BlockSpec((rows, PAIR), lambda j: (0, offset + j))

    return pl.pallas_call(
        attention_forward_kernel,
        grid=(pairs,),
        in_specs=[block(0), block(pairs), block(2 * pairs)],
        out_specs=[block(0), block(0)],
        out_shape=[
            jax.ShapeDtypeStruct((rows, pairs * PAIR), jnp.bfloat16),
            jax.ShapeDtypeStruct((rows, pairs * PAIR), jnp.float32),
        ],
        compiler_params=vmem(48),
        cost_estimate=attention_cost(rows, pairs, 2),
        name="attention_forward",
    )(projected, projected, projected)


def attention_backward(projected, attended, logs, upstream):
    rows, columns = projected.shape
    pairs = columns // 3 // PAIR

    def block(offset):
        return pl.BlockSpec((rows, PAIR), lambda j: (0, offset + j))

    return pl.pallas_call(
        attention_backward_kernel,
        grid=(pairs,),
        in_specs=[block(0), block(pairs), block(2 * pairs), block(0), block(0), block(0)],
        out_specs=pl.BlockSpec((3, rows, PAIR), lambda j: (0, 0, j)),
        out_shape=jax.ShapeDtypeStruct((3, rows, pairs * PAIR), jnp.bfloat16),
        scratch_shapes=[pltpu.VMEM((rows, PAIR), jnp.float32)],
        compiler_params=vmem(48),
        cost_estimate=attention_cost(rows, pairs, 5),
        name="attention_backward",
    )(projected, projected, projected, attended, logs, upstream)


def one_sequence_plan(
    entering_states,
    bypass_states,
    mentor_states,
    occupancy_mask,
    bypass_merge_matrix,
    bypass_merge_offset,
    mixer_layernorm_scale,
    mixer_layernorm_offset,
    asking_map_matrix,
    lookup_map_matrix,
    content_map_matrix,
    mixer_result_matrix,
    mixer_result_offset,
    perceptron_layernorm_scale,
    perceptron_layernorm_offset,
    expand_layer_matrix,
    expand_layer_offset,
    contract_layer_matrix,
    contract_layer_offset,
):
    f32, bf16 = jnp.float32, jnp.bfloat16
    rows, d = entering_states.shape
    col = asking_map_matrix.shape[1]
    ffl = expand_layer_matrix.shape[1]
    r = asking_map_matrix.shape[0]
    nf = d // r
    nt = d // col
    everyone = ("z", "y", "c", "x")
    at = {axis: lax.axis_index(axis) for axis in everyone}
    small = (
        bypass_merge_offset,
        mixer_layernorm_scale,
        mixer_layernorm_offset,
        mixer_result_offset,
        perceptron_layernorm_scale,
        perceptron_layernorm_offset,
        contract_layer_offset,
        expand_layer_offset,
    )
    flat = jnp.concatenate(small)
    flat = jnp.pad(flat, (0, 16 * col - flat.shape[0])).reshape(16, col)
    early = jnp.concatenate(
        [
            bypass_merge_matrix.reshape(-1, col),
            asking_map_matrix,
            lookup_map_matrix,
            content_map_matrix,
            mixer_result_matrix.T,
            flat,
        ],
        axis=0,
    )
    early = lax.all_gather(early, everyone, axis=0, tiled=False)
    late = jnp.concatenate([expand_layer_matrix, contract_layer_matrix.T], axis=0)
    late = lax.all_gather(late, everyone, axis=0, tiled=False)
    mrows = bypass_merge_matrix.size // col
    merge_full = early[:, :mrows].reshape(-1, d)

    def columns(block, start, count):
        part = block.reshape((nf, nt) + block.shape[1:])[:, :, start : start + count]
        return part.transpose(0, 2, 1, 3).reshape(nf * count, -1)

    project = jnp.concatenate([columns(early, mrows + i * r, r) for i in range(3)], axis=1)
    output_t = columns(early, mrows + 3 * r, r)
    hidden_full = columns(late, 0, r)
    down_t = columns(late, r, r)
    vec = early[:, mrows + 4 * r :].reshape(nf * nt, -1)
    vectors, offset = [], 0
    for item in small:
        n = item.shape[0]
        vectors.append(vec[:, offset : offset + n].reshape(-1).astype(f32))
        offset += n
    merge_add, gain_one, shift_one, output_add, gain_two, shift_two, down_add, hidden_add = vectors

    alive = lax.dynamic_index_in_dim(occupancy_mask, at["x"], keepdims=False).astype(f32)
    joined = jnp.concatenate([entering_states, bypass_states], axis=1)
    merged = jnp.dot(joined, merge_full, preferred_element_type=f32) + merge_add
    first = layer_norm(merged, gain_one, shift_one).astype(bf16)
    projected = jnp.dot(first, project, preferred_element_type=f32).astype(bf16)
    attended, summary = attention_forward(projected)
    after_attn = merged + contract_cols(attended, output_t) + output_add
    second = layer_norm(after_attn, gain_two, shift_two).astype(bf16)
    hidden = jnp.dot(second, hidden_full, preferred_element_type=f32) + hidden_add
    active = gelu_exact(hidden).astype(bf16)
    final = after_attn + contract_cols(active, down_t) + down_add
    missing = final - mentor_states.astype(f32)
    grad_final = alive * missing
    block_out = (final * alive).astype(bf16)
    energy, counted = lax.psum(
        (0.5 * jnp.sum(grad_final * missing), alive * float(rows)), everyone
    )
    loss_value = energy / (counted * d)
    grad_down_bias = jnp.sum(grad_final, axis=0)
    upstream = grad_final.astype(bf16)

    def exchange(value, axis):
        return lax.ppermute(value, axis, [(0, 1), (1, 0)])

    def pick(value, index, dim):
        return lax.dynamic_index_in_dim(value, index, dim, keepdims=False)

    def halve(value, axis, dim):
        here = at[axis]
        got = exchange(pick(value, 1 - here, dim), axis)
        return (pick(value, here, dim).astype(f32) + got.astype(f32)).astype(value.dtype)

    def line(value, dim):
        here = at["z"]
        total = pick(value, here, dim).astype(f32)
        for k in range(1, 4):
            target = lax.rem(here + k, 4)
            got = lax.ppermute(
                pick(value, target, dim), "z", [(i, (i + k) % 4) for i in range(4)]
            )
            total = total + got.astype(f32)
        return total

    def shared(value):
        value = halve(value, "c", 2)
        half = value.shape[-1] // 2
        left = halve(halve(value[..., :half], "x", 2), "y", 1)
        right = halve(halve(value[..., half:], "y", 1), "x", 1)
        return line(jnp.concatenate([left, right], axis=-1), 0)

    def blocks(value):
        return value.reshape(4, 2, 2, r, nt, -1).transpose(0, 1, 2, 4, 3, 5)

    grad_down = shared(blocks(contract_rows(upstream, active).astype(bf16)))
    grad_active = jnp.dot(upstream, down_t, preferred_element_type=f32)
    gelu_value, gelu_pull = jax.vjp(gelu_exact, hidden)
    grad_hidden = gelu_pull(grad_active)[0].astype(bf16)
    hidden_bias_term = jnp.sum(grad_hidden.astype(f32), axis=0)
    grad_hidden_weight = shared(blocks(contract_rows(second, grad_hidden).astype(bf16)))
    grad_second = contract_cols(grad_hidden, hidden_full)
    norm_value, second_pull = jax.vjp(layer_norm, after_attn, gain_two, shift_two)
    back_after, grad_gain_two, grad_shift_two = second_pull(grad_second)
    grad_after = grad_final + back_after
    grad_output_bias = jnp.sum(grad_after, axis=0)
    branch = grad_after.astype(bf16)
    grad_output_t = contract_rows(branch, attended).astype(bf16)
    grad_attended = jnp.dot(branch, output_t, preferred_element_type=f32).astype(bf16)
    grad_qkv = attention_backward(projected, attended, summary, grad_attended)
    grad_projected = jnp.concatenate([grad_qkv[i] for i in range(3)], axis=1)
    grad_project = contract_rows(first, grad_projected).astype(bf16)
    four = jnp.concatenate(
        [blocks(grad_project[:, i * d : (i + 1) * d]) for i in range(3)] + [blocks(grad_output_t)],
        axis=-1,
    )
    four = shared(four)
    grad_first = contract_cols(grad_projected, project)
    first_value, first_pull = jax.vjp(layer_norm, merged, gain_one, shift_one)
    back_merged, grad_gain_one, grad_shift_one = first_pull(grad_first)
    grad_merged = grad_after + back_merged
    grad_merge_bias = jnp.sum(grad_merged, axis=0)
    merge_grad = grad_merged.astype(bf16)
    grad_joined = contract_cols(merge_grad, merge_full)
    merge_weight = shared(
        contract_rows(joined, merge_grad).astype(bf16).reshape(4, 2, 2, nt, -1, d)
    )
    terms = (
        grad_merge_bias,
        grad_gain_one,
        grad_shift_one,
        grad_output_bias,
        grad_gain_two,
        grad_shift_two,
        grad_down_bias,
        hidden_bias_term,
    )
    stacked = jnp.concatenate([item.reshape(nf * nt, -1) for item in terms], axis=1)
    stacked = lax.psum_scatter(stacked, everyone, scatter_dimension=0, tiled=True).reshape(-1)
    sums, offset = [], 0
    for item in small:
        n = item.shape[0]
        sums.append(stacked[offset : offset + n])
        offset += n
    return (
        block_out,
        loss_value,
        grad_joined[:, :d],
        grad_joined[:, d:],
        merge_weight,
        sums[0],
        sums[1],
        sums[2],
        four[:, :col],
        four[:, col : 2 * col],
        four[:, 2 * col : 3 * col],
        four[:, 3 * col :].T,
        sums[3],
        sums[4],
        sums[5],
        grad_hidden_weight,
        sums[7],
        grad_down.T,
        sums[6],
    )


ARGUMENTS = (
    ("ft", None),
    ("ft", None),
    ("ft", None),
    ("f",),
    ("ft", None),
    ("ft",),
    ("ft",),
    ("ft",),
    ("f", "t"),
    ("f", "t"),
    ("f", "t"),
    ("t", "f"),
    ("ft",),
    ("ft",),
    ("ft",),
    ("f", "t"),
    ("ft",),
    ("t", "f"),
    ("ft",),
)
RESULTS = (
    ("ft", None),
    (),
    ("ft", None),
    ("ft", None),
    ("ft", None),
    ("ft",),
    ("ft",),
    ("ft",),
    ("f", "t"),
    ("f", "t"),
    ("f", "t"),
    ("t", "f"),
    ("ft",),
    ("ft",),
    ("ft",),
    ("f", "t"),
    ("ft",),
    ("t", "f"),
    ("ft",),
)


def solution(mesh):
    def whole(*args):
        rows = args[0].shape[0] // mesh.size
        if rows == SEQ_LEN and dict(mesh.shape) == {"fsdp": 16, "tp": 2}:
            plan = one_sequence_plan
            use = jax.sharding.Mesh(mesh.devices.reshape(4, 2, 2, 2), ("z", "y", "c", "x"))
            names = {"f": ("z", "y", "c"), "t": ("x",), "ft": ("z", "y", "c", "x")}
        else:
            plan = per_device_split
            use = mesh
            names = {"f": ("fsdp",), "t": ("tp",), "ft": ("fsdp", "tp")}

        def place(entry):
            return P(*(None if e is None else names[e] for e in entry))

        return jax.shard_map(
            plan,
            mesh=use,
            in_specs=tuple(place(e) for e in ARGUMENTS),
            out_specs=tuple(place(e) for e in RESULTS),
            check_vma=False,
        )(*args)

    return whole
```

```python
import functools
import math

import jax
import jax.numpy as jnp
from jax import lax
from jax.experimental import pallas as pl
from jax.experimental.pallas import tpu as pltpu
from jax.sharding import PartitionSpec as P

D = 1024
HEADS = 16
SEQ_LEN = 1104


EPSILON = 1e-05


def layer_norm(value, gain, shift):
    centred = value - jnp.mean(value, axis=-1, keepdims=True)
    spread = jnp.mean(centred * centred, axis=-1, keepdims=True)
    return centred * lax.rsqrt(spread + EPSILON) * gain + shift


def contract_rows(left, right):
    return lax.dot_general(
        left, right, (((0,), (0,)), ((), ())), preferred_element_type=jnp.float32
    )


def contract_cols(left, right):
    return lax.dot_general(
        left, right, (((1,), (1,)), ((), ())), preferred_element_type=jnp.float32
    )


def attend_forward(queries, keys_all, values):
    scale = float(queries.shape[-1]) ** (-0.5)
    scores = (
        jnp.einsum("qhd,khd->hqk", queries, keys_all, preferred_element_type=jnp.float32) * scale
    )
    peak_score = jnp.max(scores, axis=-1, keepdims=True)
    raised = jnp.exp(scores - peak_score)
    row_total = jnp.sum(raised, axis=-1, keepdims=True)
    weights_low = (raised / row_total).astype(jnp.bfloat16)
    output = jnp.einsum("hqk,khd->qhd", weights_low, values, preferred_element_type=jnp.float32)
    return (output.astype(jnp.bfloat16), peak_score + jnp.log(row_total))


def attend_backward(queries, keys_all, values, summary, upstream):
    scale = float(queries.shape[-1]) ** (-0.5)
    scores = (
        jnp.einsum("qhd,khd->hqk", queries, keys_all, preferred_element_type=jnp.float32) * scale
    )
    probs_full = jnp.exp(scores - summary)
    grad_probs = jnp.einsum("qhd,khd->hqk", upstream, values, preferred_element_type=jnp.float32)
    grad_values = jnp.einsum(
        "hqk,qhd->khd",
        probs_full.astype(jnp.bfloat16),
        upstream,
        preferred_element_type=jnp.float32,
    )
    centre = jnp.sum(probs_full * grad_probs, axis=-1, keepdims=True)
    grad_scores = (probs_full * (grad_probs - centre)).astype(jnp.bfloat16)
    grad_queries = (
        jnp.einsum("hqk,khd->qhd", grad_scores, keys_all, preferred_element_type=jnp.float32)
        * scale
    )
    grad_keys = (
        jnp.einsum("hqk,qhd->khd", grad_scores, queries, preferred_element_type=jnp.float32) * scale
    )
    return (
        grad_queries.astype(jnp.bfloat16),
        grad_keys.astype(jnp.bfloat16),
        grad_values.astype(jnp.bfloat16),
    )


def gelu_exact(value):
    return jax.nn.gelu(value, approximate=False)


def per_device_split(
    entering_states,
    bypass_states,
    mentor_states,
    occupancy_mask,
    bypass_merge_matrix,
    bypass_merge_offset,
    mixer_layernorm_scale,
    mixer_layernorm_offset,
    asking_map_matrix,
    lookup_map_matrix,
    content_map_matrix,
    mixer_result_matrix,
    mixer_result_offset,
    perceptron_layernorm_scale,
    perceptron_layernorm_offset,
    expand_layer_matrix,
    expand_layer_offset,
    contract_layer_matrix,
    contract_layer_offset,
):
    rows = entering_states.shape[0]
    width = D // HEADS
    position = lax.axis_index("tp")
    (
        merge_full,
        merge_add,
        gain_one,
        shift_one,
        output_add,
        gain_two,
        shift_two,
        hidden_add,
        down_add,
    ) = (
        lax.all_gather(bypass_merge_matrix, ("fsdp", "tp"), axis=0, tiled=True),
        lax.all_gather(bypass_merge_offset, ("fsdp", "tp"), axis=0, tiled=True),
        lax.all_gather(mixer_layernorm_scale, ("fsdp", "tp"), axis=0, tiled=True),
        lax.all_gather(mixer_layernorm_offset, ("fsdp", "tp"), axis=0, tiled=True),
        lax.all_gather(mixer_result_offset, ("fsdp", "tp"), axis=0, tiled=True),
        lax.all_gather(perceptron_layernorm_scale, ("fsdp", "tp"), axis=0, tiled=True),
        lax.all_gather(perceptron_layernorm_offset, ("fsdp", "tp"), axis=0, tiled=True),
        lax.all_gather(expand_layer_offset, ("fsdp", "tp"), axis=0, tiled=True),
        lax.all_gather(contract_layer_offset, ("fsdp", "tp"), axis=0, tiled=True),
    )
    query_full, key_full, value_full, output_full, hidden_full, down_full = (
        lax.all_gather(asking_map_matrix, "fsdp", axis=0, tiled=True),
        lax.all_gather(lookup_map_matrix, "fsdp", axis=0, tiled=True),
        lax.all_gather(content_map_matrix, "fsdp", axis=0, tiled=True),
        lax.all_gather(mixer_result_matrix, "fsdp", axis=1, tiled=True),
        lax.all_gather(expand_layer_matrix, "fsdp", axis=0, tiled=True),
        lax.all_gather(contract_layer_matrix, "fsdp", axis=1, tiled=True),
    )
    gain_one = gain_one.astype(jnp.float32)
    shift_one = shift_one.astype(jnp.float32)
    gain_two = gain_two.astype(jnp.float32)
    shift_two = shift_two.astype(jnp.float32)
    project = jnp.concatenate([query_full, key_full, value_full], axis=1)
    local_width = query_full.shape[1]
    local_heads = local_width // width
    local_hidden = hidden_full.shape[1]
    row_index = position * rows + jnp.arange(rows, dtype=jnp.int32)
    slot_of_row = row_index // SEQ_LEN
    series_place_total = occupancy_mask.shape[0]
    agreeing_lines = (
        slot_of_row[:, None] == jnp.arange(series_place_total, dtype=jnp.int32)[None, :]
    ).astype(jnp.float32)
    alive_tokens = jnp.sum(
        agreeing_lines * occupancy_mask.astype(jnp.float32)[None, :], axis=1, keepdims=True
    )
    joined = jnp.concatenate([entering_states, bypass_states], axis=1)
    merged = jnp.dot(joined, merge_full, preferred_element_type=jnp.float32) + merge_add.astype(
        jnp.float32
    )
    first = layer_norm(merged, gain_one, shift_one).astype(jnp.bfloat16)
    first_all = lax.all_gather(first, "tp", axis=0, tiled=True)
    group_rows = first_all.shape[0]
    slots = group_rows // SEQ_LEN
    projected = jnp.dot(first_all, project, preferred_element_type=jnp.float32).astype(jnp.bfloat16)
    shaped = projected.reshape(slots, SEQ_LEN, 3, local_heads, width)
    queries = shaped[:, :, 0]
    keys_all = shaped[:, :, 1]
    values = shaped[:, :, 2]
    attended, summary = lax.map(
        lambda item: attend_forward(item[0], item[1], item[2]), (queries, keys_all, values)
    )
    attended_flat = attended.reshape(group_rows, local_width)
    attention_term = jnp.dot(attended_flat, output_full, preferred_element_type=jnp.float32)
    after_attn = (
        merged
        + lax.psum_scatter(
            attention_term.astype(jnp.bfloat16), "tp", scatter_dimension=0, tiled=True
        ).astype(jnp.float32)
        + output_add.astype(jnp.float32)
    )
    second = layer_norm(after_attn, gain_two, shift_two).astype(jnp.bfloat16)
    second_all = lax.all_gather(second, "tp", axis=0, tiled=True)
    hidden_slice = lax.dynamic_slice_in_dim(
        hidden_add.astype(jnp.float32), position * local_hidden, local_hidden, 0
    )
    hidden = jnp.dot(second_all, hidden_full, preferred_element_type=jnp.float32) + hidden_slice
    active = gelu_exact(hidden).astype(jnp.bfloat16)
    feed_term = jnp.dot(active, down_full, preferred_element_type=jnp.float32)
    final = (
        after_attn
        + lax.psum_scatter(
            feed_term.astype(jnp.bfloat16), "tp", scatter_dimension=0, tiled=True
        ).astype(jnp.float32)
        + down_add.astype(jnp.float32)
    )
    missing = final - mentor_states.astype(jnp.float32)
    grad_final = alive_tokens * missing
    block_out = (final * alive_tokens).astype(jnp.bfloat16)
    energy, counted = lax.psum(
        (0.5 * jnp.sum(grad_final * missing), jnp.sum(alive_tokens)), ("fsdp", "tp")
    )
    loss_value = energy / (counted * D)
    grad_down_bias = jnp.sum(grad_final, axis=0)
    upstream = grad_final.astype(jnp.bfloat16)
    upstream_all = lax.all_gather(upstream, "tp", axis=0, tiled=True)
    grad_down = contract_rows(active, upstream_all)
    grad_active = contract_cols(upstream_all, down_full)
    gelu_value, gelu_pull = jax.vjp(gelu_exact, hidden)
    grad_hidden = gelu_pull(grad_active)[0].astype(jnp.bfloat16)
    grad_hidden_local = jnp.sum(grad_hidden.astype(jnp.float32), axis=0)
    grad_hidden_weight = contract_rows(second_all, grad_hidden)
    feed_back_term = contract_cols(grad_hidden, hidden_full)
    grad_second = lax.psum_scatter(
        feed_back_term.astype(jnp.bfloat16), "tp", scatter_dimension=0, tiled=True
    ).astype(jnp.float32)
    hidden_bias_term = lax.dynamic_update_slice_in_dim(
        jnp.zeros((hidden_add.shape[0],), jnp.float32),
        grad_hidden_local,
        position * local_hidden,
        0,
    )
    norm_value, second_pull = jax.vjp(layer_norm, after_attn, gain_two, shift_two)
    back_after, grad_gain_two, grad_shift_two = second_pull(grad_second)
    grad_after = grad_final + back_after
    grad_output_bias = jnp.sum(grad_after, axis=0)
    branch_all = lax.all_gather(grad_after.astype(jnp.bfloat16), "tp", axis=0, tiled=True)
    grad_output_weight = contract_rows(attended_flat, branch_all)
    grad_attended = contract_cols(branch_all, output_full).astype(jnp.bfloat16)
    upstream_heads = grad_attended.reshape(slots, SEQ_LEN, local_heads, width)
    grad_q_heads, grad_k_heads, grad_v_heads = lax.map(
        lambda item: attend_backward(item[0], item[1], item[2], item[3], item[4]),
        (queries, keys_all, values, summary, upstream_heads),
    )
    grad_projected = jnp.stack([grad_q_heads, grad_k_heads, grad_v_heads], axis=2).reshape(
        group_rows, 3 * local_width
    )
    grad_project = contract_rows(first_all, grad_projected)
    attention_back_term = contract_cols(grad_projected, project)
    grad_first = lax.psum_scatter(
        attention_back_term.astype(jnp.bfloat16), "tp", scatter_dimension=0, tiled=True
    ).astype(jnp.float32)
    first_value, first_pull = jax.vjp(layer_norm, merged, gain_one, shift_one)
    back_merged, grad_gain_one, grad_shift_one = first_pull(grad_first)
    grad_merged = grad_after + back_merged
    grad_merge_bias = jnp.sum(grad_merged, axis=0)
    merge_grad = grad_merged.astype(jnp.bfloat16)
    grad_merge_weight = contract_rows(joined, merge_grad)
    grad_joined = contract_cols(merge_grad, merge_full)
    model_width = entering_states.shape[1]
    grad_tokens = grad_joined[:, :model_width]
    grad_shortcut = grad_joined[:, model_width:]
    grad_query, grad_key, grad_value, grad_output, grad_hidden_full, grad_down_full = (
        lax.psum_scatter(
            grad_project[:, :local_width].astype(jnp.bfloat16),
            "fsdp",
            scatter_dimension=0,
            tiled=True,
        ).astype(jnp.float32),
        lax.psum_scatter(
            grad_project[:, local_width : 2 * local_width].astype(jnp.bfloat16),
            "fsdp",
            scatter_dimension=0,
            tiled=True,
        ).astype(jnp.float32),
        lax.psum_scatter(
            grad_project[:, 2 * local_width :].astype(jnp.bfloat16),
            "fsdp",
            scatter_dimension=0,
            tiled=True,
        ).astype(jnp.float32),
        lax.psum_scatter(
            grad_output_weight.astype(jnp.bfloat16), "fsdp", scatter_dimension=1, tiled=True
        ).astype(jnp.float32),
        lax.psum_scatter(
            grad_hidden_weight.astype(jnp.bfloat16), "fsdp", scatter_dimension=0, tiled=True
        ).astype(jnp.float32),
        lax.psum_scatter(
            grad_down.astype(jnp.bfloat16), "fsdp", scatter_dimension=1, tiled=True
        ).astype(jnp.float32),
    )
    (
        merge_weight_sum,
        merge_bias_sum,
        gain_one_sum,
        shift_one_sum,
        output_bias_sum,
        gain_two_sum,
        shift_two_sum,
        hidden_bias_sum,
        down_bias_sum,
    ) = (
        lax.psum_scatter(grad_merge_weight, ("fsdp", "tp"), scatter_dimension=0, tiled=True),
        lax.psum_scatter(grad_merge_bias, ("fsdp", "tp"), scatter_dimension=0, tiled=True),
        lax.psum_scatter(grad_gain_one, ("fsdp", "tp"), scatter_dimension=0, tiled=True),
        lax.psum_scatter(grad_shift_one, ("fsdp", "tp"), scatter_dimension=0, tiled=True),
        lax.psum_scatter(grad_output_bias, ("fsdp", "tp"), scatter_dimension=0, tiled=True),
        lax.psum_scatter(grad_gain_two, ("fsdp", "tp"), scatter_dimension=0, tiled=True),
        lax.psum_scatter(grad_shift_two, ("fsdp", "tp"), scatter_dimension=0, tiled=True),
        lax.psum_scatter(hidden_bias_term, ("fsdp", "tp"), scatter_dimension=0, tiled=True),
        lax.psum_scatter(grad_down_bias, ("fsdp", "tp"), scatter_dimension=0, tiled=True),
    )
    return (
        block_out,
        loss_value,
        grad_tokens,
        grad_shortcut,
        merge_weight_sum,
        merge_bias_sum,
        gain_one_sum,
        shift_one_sum,
        grad_query,
        grad_key,
        grad_value,
        grad_output,
        output_bias_sum,
        gain_two_sum,
        shift_two_sum,
        grad_hidden_full,
        hidden_bias_sum,
        grad_down_full,
        down_bias_sum,
    )


LOG2E = math.log2(math.e)
PAIR = 128
CHUNK = 368


def nn(a, b):
    return lax.dot_general(a, b, (((1,), (0,)), ((), ())), preferred_element_type=jnp.float32)


def nt(a, b):
    return lax.dot_general(a, b, (((1,), (1,)), ((), ())), preferred_element_type=jnp.float32)


def tn(a, b):
    return lax.dot_general(a, b, (((0,), (0,)), ((), ())), preferred_element_type=jnp.float32)


def vmem():
    return pltpu.CompilerParams(vmem_limit_bytes=60 * 2**20)


def attention_forward_kernel(q_ref, k_ref, v_ref, o_ref, l_ref):
    count = q_ref.shape[0]
    scale = (PAIR // 2) ** -0.5 * LOG2E
    low = lax.broadcasted_iota(jnp.int32, (1, PAIR), 1) < PAIR // 2
    keys, values = k_ref[...], v_ref[...]
    zero = jnp.zeros_like(keys)
    heads = (jnp.where(low, keys, zero), jnp.where(low, zero, keys))
    wide = jnp.concatenate([values, jnp.ones_like(values)], axis=1)
    for start in range(0, count, CHUNK):
        part = slice(start, min(start + CHUNK, count))
        queries = q_ref[part, :]
        outs, sums = [], []
        for head in heads:
            scores = nt(queries, head)
            peak = jnp.max(scores, axis=1, keepdims=True) * scale
            raised = jnp.exp2(scores * scale - peak).astype(jnp.bfloat16)
            both = nn(raised, wide)
            total = both[:, PAIR:]
            outs.append(both[:, :PAIR] / total)
            sums.append(peak + jnp.log2(total))
        o_ref[part, :] = jnp.where(low, outs[0], outs[1]).astype(jnp.bfloat16)
        l_ref[part, :] = jnp.where(low, sums[0], sums[1])


def attention_backward_kernel(q_ref, k_ref, v_ref, o_ref, l_ref, u_ref, out_ref, total_ref):
    count = q_ref.shape[0]
    plain = (PAIR // 2) ** -0.5
    scale = plain * LOG2E
    low = lax.broadcasted_iota(jnp.int32, (1, PAIR), 1) < PAIR // 2
    queries, upstream = q_ref[...], u_ref[...]
    product = upstream.astype(jnp.float32) * o_ref[...].astype(jnp.float32)
    left = jnp.sum(jnp.where(low, product, 0.0), axis=1, keepdims=True)
    right = jnp.sum(jnp.where(low, 0.0, product), axis=1, keepdims=True)
    centres = jnp.transpose(jnp.where(low, left, right))
    logs = jnp.transpose(l_ref[...])
    for head in range(2):

        def own(value):
            zero = jnp.zeros_like(value)
            return jnp.where(low, value, zero) if head == 0 else jnp.where(low, zero, value)

        row = head * (PAIR // 2)
        own_queries, own_upstream = own(queries), own(upstream)
        log_row, centre = logs[row : row + 1, :], centres[row : row + 1, :]
        for start in range(0, count, CHUNK):
            part = slice(start, min(start + CHUNK, count))
            keys, values = k_ref[part, :], v_ref[part, :]
            probs = jnp.exp2(nt(keys, own_queries) * scale - log_row)
            slopes = (probs * (nt(values, own_upstream) - centre)).astype(jnp.bfloat16)
            grad_v = nn(probs.astype(jnp.bfloat16), own_upstream).astype(jnp.bfloat16)
            grad_k = (nn(slopes, own_queries) * plain).astype(jnp.bfloat16)
            grad_q = tn(slopes, own(keys))
            if head == 0:
                out_ref[1, part, :] = grad_k
                out_ref[2, part, :] = grad_v
            else:
                out_ref[1, part, :] = jnp.where(low, out_ref[1, part, :], grad_k)
                out_ref[2, part, :] = jnp.where(low, out_ref[2, part, :], grad_v)
            if head == 0 and start == 0:
                total_ref[...] = grad_q
            else:
                total_ref[...] += grad_q
    out_ref[0] = (total_ref[...] * plain).astype(jnp.bfloat16)


def gelu_both(value):
    t = 1.0 / (1.0 + 0.3275911 * math.sqrt(0.5) * jnp.abs(value))
    bell = jnp.exp2(value * value * (-0.5 * LOG2E))
    poly = 0.5 * 1.061405429 * t - 0.5 * 1.453152027
    poly = poly * t + 0.5 * 1.421413741
    poly = poly * t - 0.5 * 0.284496736
    poly = poly * t + 0.5 * 0.254829592
    rest = poly * t * bell
    below = jnp.where(value >= 0, 1.0 - rest, rest)
    return value * below, below + value * bell * (1.0 / math.sqrt(2.0 * math.pi))


def normalized(value):
    centred = value - jnp.mean(value, axis=-1, keepdims=True)
    spread = jnp.mean(centred * centred, axis=-1, keepdims=True)
    inverse = lax.rsqrt(spread + EPSILON)
    return centred * inverse, inverse


def place_at(where_ref, hi, lo, y_rel, c_rel, rows):
    y = jnp.bitwise_xor(where_ref[0], y_rel)
    c = jnp.bitwise_xor(where_ref[1], c_rel)
    return pl.multiple_of(((hi * 2 + lo) * 4 + y * 2 + c) * rows, rows)


BITS = (0, 1)


def once(block, index):
    return pl.BlockSpec(block, index, pipeline_mode=pl.Buffered(1))


def call(kernel, grid, where, ins, outs, scratch, name, after=(), aliases=()):
    first, count = len(ins), len(after)

    def ordered_kernel(where_ref, *refs):
        kernel(where_ref, *refs[:first], *refs[first + count :])

    anywhere = pl.BlockSpec(memory_space=pl.ANY)
    return pl.pallas_call(
        ordered_kernel,
        grid_spec=pltpu.PrefetchScalarGridSpec(
            num_scalar_prefetch=1,
            grid=grid,
            in_specs=[spec for _, spec in ins] + [anywhere] * count,
            out_specs=[spec for _, _, spec in outs],
            scratch_shapes=scratch,
        ),
        out_shape=[jax.ShapeDtypeStruct(s, t) for s, t, _ in outs],
        input_output_aliases={1 + i: o for i, o in aliases},
        compiler_params=vmem(),
        cost_estimate=pl.CostEstimate(flops=0, bytes_accessed=0, transcendentals=0),
        name=name,
    )(where, *(x for x, _ in ins), *after)


def resident(shape):
    return once(shape, lambda *_: (0,) * len(shape))


def attention_forward(where, projected):
    rows, columns = projected.shape
    pairs = columns // 3 // PAIR

    def block(offset):
        return pl.BlockSpec((rows, PAIR), lambda j, s: (0, offset + j))

    return call(
        lambda where_ref, *refs: attention_forward_kernel(*refs),
        (pairs,),
        where,
        [(projected, block(0)), (projected, block(pairs)), (projected, block(2 * pairs))],
        [
            ((rows, pairs * PAIR), jnp.bfloat16, block(0)),
            ((rows, pairs * PAIR), jnp.float32, block(0)),
        ],
        [],
        "attention_forward",
    )


def attention_backward(where, projected, attended, logs, upstream, index, of, grads):
    rows, columns = projected.shape
    pairs = columns // 3 // PAIR
    here = index * (pairs // of)

    def block(offset):
        return pl.BlockSpec((rows, PAIR), lambda j, s: (0, offset + here + j))

    ins = [
        (projected, block(0)),
        (projected, block(pairs)),
        (projected, block(2 * pairs)),
        (attended, block(0)),
        (logs, block(0)),
        (upstream, block(0)),
    ]
    aliases = ()
    if grads is not None:
        ins.append((grads, pl.BlockSpec(memory_space=pl.ANY)))
        aliases = ((6, 0),)

    def kernel(where_ref, *refs):
        attention_backward_kernel(*refs[:6], *refs[-2:])

    return call(
        kernel,
        (pairs // of,),
        where,
        ins,
        [((3, rows, pairs * PAIR), jnp.bfloat16, pl.BlockSpec((3, rows, PAIR), lambda j, s: (0, 0, here + j)))],
        [pltpu.VMEM((rows, PAIR), jnp.float32)],
        "attention_backward",
        (),
        aliases,
    )[0]


def gate(where, values, after):
    anywhere = pl.BlockSpec(memory_space=pl.ANY)
    return call(
        lambda *refs: None,
        (1,),
        where,
        [(v, anywhere) for v in values],
        [(v.shape, v.dtype, anywhere) for v in values],
        [],
        "gate",
        after,
        tuple((i, i) for i in range(len(values))),
    )


def pile_kernel(slot, axis, where, mine, other, out):
    here = 0 if slot is None else where[slot]
    there = 1 - here
    if axis == 0:
        out[here] = mine[...]
        out[there] = other[...]
    else:
        for i in range(out.shape[0]):
            out[i, here] = mine[i]
            out[i, there] = other[i]


def pile(where, slot, mine, other, axis, after=()):
    shape = mine.shape[:axis] + (2,) + mine.shape[axis:]
    return call(
        functools.partial(pile_kernel, slot, axis),
        (1,),
        where,
        [(mine, resident(mine.shape)), (other, resident(mine.shape))],
        [(shape, mine.dtype, resident(shape))],
        [],
        "pile",
        after,
    )[0]


def merge_kernel(where, ent, byp, full, out):
    half = ent.shape[1]
    weight = full[...].reshape(2 * half, half)
    out[...] = nn(ent[...], weight[:half, :]) + nn(byp[...], weight[half:, :])


def merge_forward(where, ent, byp, gathered, r):
    rows, d = ent.shape
    part = pl.BlockSpec((CHUNK, d), lambda i, w: (i, 0))
    return call(
        merge_kernel,
        (rows // CHUNK,),
        where,
        [(ent, part), (byp, part), (gathered, resident((2, 2, 2, 2, 2, r, d)))],
        [((rows, d), jnp.float32, part)],
        [],
        "merge_forward",
    )[0]


def project_kernel(rows, where, raw, vec, b00, b01, b10, b11, v00, v01, v10, v11, merged, first, out, natural):
    w, x_rel = pl.program_id(0), pl.program_id(1)

    @pl.when((w == 0) & (x_rel == 0))
    def _():
        for start in range(0, raw.shape[0], CHUNK):
            part = slice(start, start + CHUNK)
            total = raw[part, :] + vec[0:1, :]
            merged[part, :] = total
            norm, _ = normalized(total)
            first[part, :] = (norm * vec[1:2, :] + vec[2:3, :]).astype(jnp.bfloat16)

    @pl.when(w < 2)
    def _():
        fill_by_core_and_y(where, natural, ((b00, b01), (b10, b11)), rows)

    @pl.when((w == 2) & (x_rel == 0))
    def _():
        fill_by_core(where, natural, (v00, v10), rows)

    @pl.when((w == 2) & (x_rel == 1))
    def _():
        fill_by_core(where, natural, (v01, v11), rows)

    out[...] = nn(first[...], natural[...]).astype(jnp.bfloat16)


def project_forward(where, raw, vec, early, late, r, col):
    rows, d = raw.shape
    f32, bf16 = jnp.float32, jnp.bfloat16
    by_x = pl.BlockSpec(
        (pl.squeezed, 2, 2, r, col),
        lambda w, x, s: (jnp.where(w < 2, x, 1), 0, 0, jnp.minimum(w, 1), 0),
    )
    by_y = once((2, 2, 2, r, col), lambda w, x, s: (0, 0, 0, 0, 0))
    return call(
        functools.partial(project_kernel, r),
        (3, 2),
        where,
        [(raw, resident((rows, d))), (vec, resident(vec.shape))]
        + [(p, by_x) for p in early]
        + [(p, by_y) for p in late],
        [
            ((rows, d), f32, resident((rows, d))),
            ((rows, d), bf16, resident((rows, d))),
            ((rows, 6 * col), bf16, pl.BlockSpec((rows, col), lambda w, x, s: (0, w * 2 + x))),
            ((3, 2, d, col), bf16, pl.BlockSpec((pl.squeezed, pl.squeezed, d, col), lambda w, x, s: (w, x, 0, 0))),
        ],
        [],
        "project_forward",
    )


def result_kernel(rows, where, attended, merged, vec, v00, v01, v10, v11, after, second, natural, total):
    step = pl.program_id(0)

    @pl.when(step == 0)
    def _():
        fill_by_core(where, natural, (v00, v10), rows)
        total[...] = nt(attended[...], natural[...])

    @pl.when(step == 1)
    def _():
        fill_by_core(where, natural, (v01, v11), rows)
        for start in range(0, after.shape[0], CHUNK):
            here = slice(start, start + CHUNK)
            part = nt(attended[here, :], natural[...])
            value = merged[here, :] + vec[3:4, :] + (total[here, :] + part)
            after[here, :] = value
            norm, _ = normalized(value)
            second[here, :] = (norm * vec[4:5, :] + vec[5:6, :]).astype(jnp.bfloat16)


def result_forward(where, attended, merged, vec, late, r, col):
    rows, d = merged.shape
    by_y = once((2, 2, 2, r, col), lambda x, s: (0, 0, 0, 1, 0))
    return call(
        functools.partial(result_kernel, r),
        (2,),
        where,
        [
            (attended, pl.BlockSpec((rows, col), lambda x, s: (0, x))),
            (merged, resident((rows, d))),
            (vec, resident(vec.shape)),
        ]
        + [(p, by_y) for p in late],
        [
            ((rows, d), jnp.float32, resident((rows, d))),
            ((rows, d), jnp.bfloat16, resident((rows, d))),
            ((2, d, col), jnp.bfloat16, pl.BlockSpec((pl.squeezed, d, col), lambda x, s: (x, 0, 0))),
        ],
        [pltpu.VMEM((rows, d), jnp.float32)],
        "result_forward",
    )


def fill_by_core(where, full, refs, rows):
    for c_rel, ref in enumerate(refs):
        for y_rel in BITS:
            for hi in BITS:
                for lo in BITS:
                    at = place_at(where, hi, lo, y_rel, c_rel, rows)
                    full[pl.ds(at, rows), :] = ref[y_rel, hi, lo]


def fill_by_core_and_y(where, full, refs, rows):
    for c_rel, pair in enumerate(refs):
        for y_rel, ref in enumerate(pair):
            for hi in BITS:
                for lo in BITS:
                    at = place_at(where, hi, lo, y_rel, c_rel, rows)
                    full[pl.ds(at, rows), :] = ref[hi, lo]


def spill_by_core(where, full, refs, rows):
    for c_rel, ref in enumerate(refs):
        for y_rel in BITS:
            for hi in BITS:
                for lo in BITS:
                    at = place_at(where, hi, lo, y_rel, c_rel, rows)
                    ref[y_rel, hi, lo] = full[pl.ds(at, rows), :]


def expand_kernel(rows, where, second, bias, w0, w1, active, slope, full):
    fill_by_core(where, full, (w0, w1), rows)
    for start in range(0, second.shape[0], CHUNK):
        part = slice(start, start + CHUNK)
        hidden = nn(second[part, :], full[...]) + bias[...]
        value, rate = gelu_both(hidden)
        active[part, :] = value.astype(jnp.bfloat16)
        slope[part, :] = rate.astype(jnp.bfloat16)


def expand_forward(where, second, bias, pieces, block=512):
    rows, d = second.shape
    *_, r, half = pieces[0].shape
    weight = pl.BlockSpec((2, 2, 2, r, block), lambda j, s: (0, 0, 0, 0, j))
    out = pl.BlockSpec((rows, block), lambda j, s: (0, j))
    return call(
        functools.partial(expand_kernel, r),
        (half // block,),
        where,
        [(second, resident((rows, d))), (bias, pl.BlockSpec((1, block), lambda j, s: (0, j)))]
        + [(p, weight) for p in pieces],
        [((rows, half), jnp.bfloat16, out)] * 2,
        [pltpu.VMEM((d, block), jnp.bfloat16)],
        "expand_forward",
    )


def contract_kernel(rows, steps, where, alive, a0, a1, after, mentor, vec, w00, w01, w10, w11,
                    out, upstream, grad, sums, energy, full, total):
    step = pl.program_id(0)
    fill_by_core_and_y(where, full, ((w00, w01), (w10, w11)), rows)
    count = after.shape[0]

    @pl.when(step == 0)
    def _():
        total[...] = nt(a0[...], full[...])

    @pl.when((step > 0) & (step < steps))
    def _():
        total[...] += nt(a0[...], full[...])

    @pl.when((step >= steps) & (step < 2 * steps - 1))
    def _():
        total[...] += nt(a1[...], full[...])

    @pl.when(step == 2 * steps - 1)
    def _():
        live = alive[0]
        column, squares = 0.0, 0.0
        for start in range(0, count, CHUNK):
            part = slice(start, start + CHUNK)
            final = after[part, :] + (total[part, :] + nt(a1[part, :], full[...])) + vec[6:7, :]
            missing = final - mentor[part, :].astype(jnp.float32)
            slope = live * missing
            out[part, :] = (live * final).astype(jnp.bfloat16)
            upstream[part, :] = slope.astype(jnp.bfloat16)
            grad[part, :] = slope
            column += jnp.sum(slope, axis=0, keepdims=True)
            squares += jnp.sum(slope * missing, axis=0, keepdims=True)
        sums[...] = jnp.broadcast_to(column, sums.shape)
        energy[...] = jnp.broadcast_to(0.5 * jnp.sum(squares, axis=1, keepdims=True), energy.shape)


def contract_forward(where, alive, active, after, mentor, vec, pieces, block=1024):
    rows, d = after.shape
    *_, r, half = pieces[0].shape
    steps = half // block
    weight = pl.BlockSpec((pl.squeezed, 2, 2, r, block), lambda j, s: (j // steps, 0, 0, 0, j % steps))
    f32, bf16 = jnp.float32, jnp.bfloat16
    whole = resident((rows, d))
    return call(
        functools.partial(contract_kernel, r, steps),
        (2 * steps,),
        where,
        [
            (alive, pl.BlockSpec(memory_space=pltpu.SMEM)),
            (active[0], pl.BlockSpec((rows, block), lambda j, s: (0, jnp.minimum(j, steps - 1)))),
            (active[1], pl.BlockSpec((rows, block), lambda j, s: (0, jnp.maximum(j - steps, 0)))),
            (after, whole),
            (mentor, whole),
            (vec, resident(vec.shape)),
        ]
        + [(p, weight) for p in pieces],
        [
            ((rows, d), bf16, whole),
            ((rows, d), bf16, whole),
            ((rows, d), f32, whole),
            ((8, d), f32, resident((8, d))),
            ((8, 128), f32, resident((8, 128))),
        ],
        [pltpu.VMEM((d, block), bf16), pltpu.VMEM((rows, d), f32)],
        "contract_forward",
    )


def feed_backward_kernel(rows, where, upstream, second, active, slope, v00, v01, v10, v11, w0, w1,
                         grad_second, e0, e1, d0, d1, bias, down, up, result):
    step = pl.program_id(0)
    fill_by_core_and_y(where, down, ((v00, v01), (v10, v11)), rows)
    fill_by_core(where, up, (w0, w1), rows)
    grad_active = nn(upstream[...], down[...])
    grad_hidden = grad_active * slope[...].astype(jnp.float32)
    bias[...] = jnp.broadcast_to(jnp.sum(grad_hidden, axis=0, keepdims=True), bias.shape)
    grad_hidden = grad_hidden.astype(jnp.bfloat16)
    result[...] = tn(upstream[...], active[...]).astype(jnp.bfloat16)
    spill_by_core(where, result, (d0, d1), rows)
    back = nt(grad_hidden, up[...])

    @pl.when(step == 0)
    def _():
        grad_second[...] = back

    @pl.when(step > 0)
    def _():
        grad_second[...] += back

    result[...] = tn(second[...], grad_hidden).astype(jnp.bfloat16)
    spill_by_core(where, result, (e0, e1), rows)


def feed_backward(where, upstream, second, active, slope, down, up, x_rel, block=512):
    rows, d = upstream.shape
    *_, r, half = up[0].shape
    f32, bf16 = jnp.float32, jnp.bfloat16
    whole = resident((rows, d))
    part = pl.BlockSpec((rows, block), lambda j, s: (0, j))
    piece = pl.BlockSpec((2, 2, 2, r, block), lambda j, s: (0, 0, 0, 0, j))
    quarter = pl.BlockSpec((pl.squeezed, 2, 2, r, block), lambda j, s: (x_rel, 0, 0, 0, j))
    return call(
        functools.partial(feed_backward_kernel, r),
        (half // block,),
        where,
        [(upstream, whole), (second, whole), (active, part), (slope, part)]
        + [(p, quarter) for p in down]
        + [(p, piece) for p in up],
        [((rows, d), f32, whole)]
        + [((2, 2, 2, r, half), bf16, piece)] * 4
        + [((8, half), f32, pl.BlockSpec((8, block), lambda j, s: (0, j)))],
        [pltpu.VMEM((d, block), bf16)] * 3,
        "feed_backward",
    )


def norm_backward_kernel(count, gain_row, where, value, base, vec, *refs):
    grads, extra, (total, low, sums) = refs[:count], refs[count:-3], refs[-3:]
    upstream = grads[0][...]
    for ref in grads[1:]:
        upstream = upstream + ref[...]
    norm, inverse = normalized(value[...])
    e = upstream * vec[gain_row : gain_row + 1, :]
    mean_e = jnp.mean(e, axis=-1, keepdims=True)
    mean_en = jnp.mean(e * norm, axis=-1, keepdims=True)
    result = base[...] + inverse * (e - mean_e - norm * mean_en)
    total[...] = result
    low[...] = result.astype(jnp.bfloat16)

    @pl.when(pl.program_id(0) == 0)
    def _():
        sums[...] = jnp.zeros_like(sums)
        if extra:
            column, energy, alive, own, other = extra
            d = sums.shape[1]
            sums[3:4, :] = column[0:1, :]
            sums[4:5, :] = jnp.broadcast_to(energy[0:1, 0:1], (1, d))
            sums[5:6, :] = jnp.full((1, d), alive[0] * (value.shape[0] * pl.num_programs(0)), jnp.float32)
            here = where[2] == 0
            for i in BITS:
                part = slice(i * d, (i + 1) * d)
                sums[8 + i : 9 + i, :] = jnp.where(here, own[0:1, part], other[0:1, part])
                sums[10 + i : 11 + i, :] = jnp.where(here, other[0:1, part], own[0:1, part])

    for row, item in enumerate((upstream * norm, upstream, result)):
        sums[row : row + 1, :] += jnp.sum(item, axis=0, keepdims=True)


def norm_backward(where, value, base, vec, gain_row, grads, extra=()):
    rows, d = value.shape
    part = pl.BlockSpec((CHUNK, d), lambda i, s: (i, 0))
    height = 16 if extra else 8
    carried = [
        (x, pl.BlockSpec(memory_space=pltpu.SMEM) if x.ndim == 1 else resident(x.shape)) for x in extra
    ]
    return call(
        functools.partial(norm_backward_kernel, len(grads), gain_row),
        (rows // CHUNK,),
        where,
        [(value, part), (base, part), (vec, resident(vec.shape))] + [(g, part) for g in grads] + carried,
        [
            ((rows, d), jnp.float32, part),
            ((rows, d), jnp.bfloat16, part),
            ((height, d), jnp.float32, resident((height, d))),
        ],
        [],
        "norm_backward",
    )


def result_backward_kernel(rows, where, branch, attended, weight, grad, o0, o1, full):
    grad[...] = nn(branch[...], weight[...]).astype(jnp.bfloat16)
    full[...] = tn(branch[...], attended[...]).astype(jnp.bfloat16)
    spill_by_core(where, full, (o0, o1), rows)


def result_backward(where, branch, attended, natural, r):
    rows, d = branch.shape
    col = natural.shape[-1]
    bf16 = jnp.bfloat16
    part = pl.BlockSpec((rows, col), lambda x, s: (0, x))
    piece = pl.BlockSpec((pl.squeezed, 2, 2, 2, r, col), lambda x, s: (x, 0, 0, 0, 0, 0))
    return call(
        functools.partial(result_backward_kernel, r),
        (2,),
        where,
        [
            (branch, resident((rows, d))),
            (attended, part),
            (natural, pl.BlockSpec((pl.squeezed, d, col), lambda x, s: (x, 0, 0))),
        ],
        [((rows, d), bf16, part)] + [((2, 2, 2, 2, r, col), bf16, piece)] * 2,
        [pltpu.VMEM((d, col), bf16)],
        "result_backward",
    )


def project_weight_kernel(rows, where, first, grad, o0, o1, full):
    full[...] = tn(first[...], grad[...]).astype(jnp.bfloat16)
    spill_by_core(where, full, (o0, o1), rows)


def project_weight(where, first, grads, r, col):
    rows, d = first.shape
    bf16 = jnp.bfloat16
    part = pl.BlockSpec((pl.squeezed, rows, col), lambda w, x, s: (w, 0, x))
    piece = pl.BlockSpec((pl.squeezed, pl.squeezed, 2, 2, 2, r, col), lambda w, x, s: (w, x, 0, 0, 0, 0, 0))
    return call(
        functools.partial(project_weight_kernel, r),
        (3, 2),
        where,
        [(first, resident((rows, d))), (grads, part)],
        [((3, 2, 2, 2, 2, r, col), bf16, piece)] * 2,
        [pltpu.VMEM((d, col), bf16)],
        "project_weight",
    )


def project_backward_kernel(where, grad, weight, out):
    part = nt(grad[...], weight[...])
    begin = (pl.program_id(0) == 0) & (pl.program_id(1) == 0)

    @pl.when(begin)
    def _():
        out[...] = part

    @pl.when(jnp.logical_not(begin))
    def _():
        out[...] += part


def project_backward(where, grads, natural):
    _, rows, d = grads.shape
    col = natural.shape[-1]
    return call(
        project_backward_kernel,
        (3, 2),
        where,
        [
            (grads, pl.BlockSpec((pl.squeezed, rows, col), lambda w, x, s: (w, 0, x))),
            (natural, pl.BlockSpec((pl.squeezed, pl.squeezed, d, col), lambda w, x, s: (w, x, 0, 0))),
        ],
        [((rows, d), jnp.float32, resident((rows, d)))],
        [],
        "project_backward",
    )[0]


def merge_weight_kernel(where, ent, byp, grad, o0, o1, full):
    half = ent.shape[1]
    full[:half, :] = tn(ent[...], grad[...]).astype(jnp.bfloat16)
    full[half:, :] = tn(byp[...], grad[...]).astype(jnp.bfloat16)
    for c_rel, ref in enumerate((o0, o1)):
        for x_rel in BITS:
            x = jnp.bitwise_xor(where[2], x_rel)
            for y_rel in BITS:
                for hi in BITS:
                    for lo in BITS:
                        at = place_at(where, hi, lo, y_rel, c_rel, 128) + x * 64
                        ref[x_rel, y_rel, hi, lo] = full[pl.ds(pl.multiple_of(at, 64), 64), :]


def merge_weight(where, ent, byp, grad, r, part):
    rows, d = ent.shape
    half = d // 2
    bf16 = jnp.bfloat16
    whole = resident((rows, d))
    piece = resident((2, 2, 2, 2, r, half))
    return call(
        merge_weight_kernel,
        (1,),
        where,
        [(ent, whole), (byp, whole), (grad, once((rows, half), lambda j, s: (0, part)))],
        [((2, 2, 2, 2, r, half), bf16, piece)] * 2,
        [pltpu.VMEM((2 * d, half), bf16)],
        "merge_weight",
    )


def merge_backward_kernel(where, grad, full, left, right):
    half = left.shape[1]
    weight = full[...].reshape(2 * half, half)
    left[...] = nt(grad[...], weight[:half, :])
    right[...] = nt(grad[...], weight[half:, :])


def merge_backward(where, grad, gathered, r, after):
    rows, d = grad.shape
    part = pl.BlockSpec((CHUNK, d), lambda i, w: (i, 0))
    return call(
        merge_backward_kernel,
        (rows // CHUNK,),
        where,
        [(grad, part), (gathered, resident((2, 2, 2, 2, 2, r, d)))],
        [((rows, d), jnp.float32, part)] * 2,
        [],
        "merge_backward",
        after,
    )


def swap(value, axis):
    return lax.ppermute(value, axis, [(0, 1), (1, 0)])


def swap_line(value, bit):
    return lax.ppermute(value, "z", [(i, i ^ bit) for i in range(4)])


def plus(*parts):
    total = parts[0].astype(jnp.float32)
    for part in parts[1:]:
        total = total + part.astype(jnp.float32)
    return total


def send(value, axis):
    return swap(value.astype(jnp.bfloat16), axis)


def line_parts(total, index, dim):
    mine = lax.dynamic_index_in_dim(total, index, dim, keepdims=False)
    other = lax.dynamic_index_in_dim(total, 1 - index, dim, keepdims=False)
    return mine, other.astype(jnp.bfloat16)


def one_sequence_plan(
    entering_states,
    bypass_states,
    mentor_states,
    occupancy_mask,
    bypass_merge_matrix,
    bypass_merge_offset,
    mixer_layernorm_scale,
    mixer_layernorm_offset,
    asking_map_matrix,
    lookup_map_matrix,
    content_map_matrix,
    mixer_result_matrix,
    mixer_result_offset,
    perceptron_layernorm_scale,
    perceptron_layernorm_offset,
    expand_layer_matrix,
    expand_layer_offset,
    contract_layer_matrix,
    contract_layer_offset,
):
    f32, bf16 = jnp.float32, jnp.bfloat16
    rows, d = entering_states.shape
    r, col = asking_map_matrix.shape
    half = expand_layer_matrix.shape[1]
    everyone = ("z", "y", "c", "x")
    z, y, c, x = (lax.axis_index(axis) for axis in everyone)
    hi, lo = z // 2, z % 2
    device = ((z * 2 + y) * 2 + c) * 2 + x
    where = jnp.stack([y, c, x, hi, lo]).astype(jnp.int32)
    small = (
        bypass_merge_offset,
        mixer_layernorm_scale,
        mixer_layernorm_offset,
        mixer_result_offset,
        perceptron_layernorm_scale,
        perceptron_layernorm_offset,
        contract_layer_offset,
        expand_layer_offset,
    )
    flat = jnp.concatenate(small)
    flat = jnp.pad(flat, (0, 16 * d - flat.shape[0])).reshape(16, d)
    pack = lax.all_gather(jnp.concatenate([bypass_merge_matrix, flat]), everyone, axis=0, tiled=False)
    gathered = pack.reshape((2,) * 5 + pack.shape[1:])

    matrices = (
        jnp.concatenate([asking_map_matrix, lookup_map_matrix]),
        jnp.concatenate([content_map_matrix, mixer_result_matrix.T]),
        expand_layer_matrix,
        contract_layer_matrix.T,
    )
    orders = (("x", "y"), ("y", "x"), ("y", "x"), ("x", "y"))
    far = [swap_line(m, 2) for m in matrices[:2]]
    early = [pile(where, 3, m, f, 0) for m, f in zip(matrices[:2], far)]
    near = [swap_line(m, 1) for m in early]
    late = gate(where, matrices[2:], early)
    far = [swap_line(m, 2) for m in late]
    early = [pile(where, 4, m, f, 1) for m, f in zip(early, near)]
    third = [swap(m, o[0]) for m, o in zip(early, orders[:2])]
    late = [pile(where, 3, m, f, 0, after=early) for m, f in zip(late, far)]
    near = [swap_line(m, 1) for m in late]
    early = [pile(where, None, m, f, 0, after=late) for m, f in zip(early, third)]
    fourth = [swap(m, o[1]) for m, o in zip(early, orders[:2])]
    late = [pile(where, 4, m, f, 1, after=early) for m, f in zip(late, near)]
    third = [swap(m, o[0]) for m, o in zip(late, orders[2:])]
    own = gate(where, [early[0], fourth[0], early[1], fourth[1]], late)
    away = [swap(m, "c") for m in own]
    early = [(own[0], own[1], away[0], away[1]), (own[2], own[3], away[2], away[3])]
    raw = merge_forward(where, entering_states, bypass_states, gathered, r)
    late = [pile(where, None, m, f, 0, after=(raw,)) for m, f in zip(late, third)]
    fourth = [swap(m, o[1]) for m, o in zip(late, orders[2:])]

    rest = pack[:, r].astype(f32)
    count = pack.shape[0]
    vec = rest[:, : 7 * d // count].reshape(count, 7, d // count).transpose(1, 0, 2).reshape(7, d)
    vec = jnp.pad(vec, ((0, 1), (0, 0)))
    hidden_add = rest[:, 7 * d // count : 7 * d // count + 2 * half // count].reshape(2, 1, half)
    alive = lax.dynamic_index_in_dim(occupancy_mask, x, keepdims=True).astype(f32)

    merged, first, projected, project_natural = project_forward(where, raw, vec, early[0], early[1], r, col)
    attended, logs = attention_forward(where, projected)
    own = gate(where, [late[0], fourth[0], late[1], fourth[1]], (attended,))
    away = [swap(m, "c") for m in own]
    expand_pieces = ((own[0], away[0]), (own[1], away[1]))
    contract_pieces = (own[2], own[3], away[2], away[3])
    after_attn, second, result_natural = result_forward(where, attended, merged, vec, early[1], r, col)
    active, slope = [], []
    for x_rel in BITS:
        bias = lax.dynamic_index_in_dim(hidden_add, jnp.bitwise_xor(x, x_rel), keepdims=False)
        value, rate = expand_forward(where, second, bias, expand_pieces[x_rel])
        active.append(value)
        slope.append(rate)
    block_out, upstream, grad_final, down_bias, energy = contract_forward(
        where, alive, active, after_attn, mentor_states, vec, contract_pieces
    )

    def feed(x_rel):
        return feed_backward(
            where, upstream, second, active[x_rel], slope[x_rel], contract_pieces, expand_pieces[x_rel], x_rel
        )

    gs1, e1, e1s, d1, d1s, hb1 = feed(1)
    e1c, d1c = swap(e1s, "c"), swap(d1s, "c")
    gs0, e0, e0s, d0, d0s, hb0 = feed(0)
    e0c, d0c = swap(e0s, "c"), swap(d0s, "c")
    e1, d1 = gate(where, [e1, d1], (gs0,))
    e1x = send(plus(e1, e1c), "x")
    d1y = send(plus(d1[1], d1c[1]), "y")
    grad_after, branch, sums_two = norm_backward(
        where, after_attn, grad_final, vec, 4, [gs0, gs1], (down_bias, energy, alive, hb0, hb1)
    )
    parcel = lax.all_gather(sums_two, everyone, axis=0, tiled=False)
    e0, d0 = gate(where, [e0, d0], (branch,))
    d0y = send(plus(d0[1], d0c[1]), "y")
    grad_attended, o0, o1 = result_backward(where, branch, attended, result_natural, r)

    def attend(part, grads):
        return attention_backward(where, projected, attended, logs, grad_attended, part, 2, grads)

    grads = attend(0, None)
    e0, d0, d1, grads = gate(where, [e0, d0, d1, grads], ())
    e_far = send(plus(e0[1], e0c[1], e1x[1]), "y")
    d_far = send(plus(d1[0], d1c[0], d1y), "x")
    grads = attend(1, grads)
    e0, d0, grads = gate(where, [e0, d0, grads], ())
    own = jnp.sum(parcel, axis=0)
    e_mine, e_other = line_parts(plus(e0[0], e0c[0], e1x[0], e_far), lo, 1)
    d_mine, d_other = line_parts(plus(d0[0], d0c[0], d0y, d_far), lo, 1)
    e_near, d_near = swap_line(e_other, 1), swap_line(d_other, 1)
    p0, p1 = project_weight(where, first, grads, r, col)
    qk_c = swap(p1[:2], "c")
    vo0, vo1 = jnp.stack([p0[2], o0]), jnp.stack([p1[2], o1])
    vo_c = swap(vo1, "c")
    grad_first = project_backward(where, grads, project_natural)
    p0, vo0 = gate(where, [p0, vo0], (grad_first,))
    qk_x = send(plus(p0[:2, 1], qk_c[:, 1]), "x")
    vo_y = send(plus(vo0[:, :, 1], vo_c[:, :, 1]), "y")
    e_mine, e_other = line_parts(plus(e_mine, e_near), hi, 0)
    d_mine, d_other = line_parts(plus(d_mine, d_near), hi, 0)
    e_end, d_end = swap_line(e_other, 2), swap_line(d_other, 2)
    grad_merged, merge_grad, sums_one = norm_backward(where, merged, grad_after, vec, 1, [grad_first])
    l0, l1 = merge_weight(where, entering_states, bypass_states, merge_grad, r, 0)
    l_c = swap(l1, "c")
    p0, vo0 = gate(where, [p0, vo0], (l0,))
    qk = plus(p0[:2, 0], qk_c[:, 0], qk_x)
    vo = plus(vo0[:, :, 0], vo_c[:, :, 0], vo_y)
    qk_y, vo_x = send(qk[:, 1], "y"), send(vo[:, 1], "x")
    r0, r1 = merge_weight(where, entering_states, bypass_states, merge_grad, r, 1)
    r_c = swap(r1, "c")
    l0, r0 = gate(where, [l0, r0], ())
    l_sum = plus(l0[1], l_c[1]).astype(bf16)
    l_x = swap(l_sum, "x")
    r_sum = plus(r0[:, 1], r_c[:, 1]).astype(bf16)
    r_y = swap(r_sum, "y")
    grad_expand, grad_contract = plus(e_mine, e_end), plus(d_mine, d_end)
    grad_tokens, grad_shortcut = merge_backward(
        where, merge_grad, gathered, r, (r_sum[0, 0, 0, :16, :128], l_sum[0, 0, 0, :16, :128])
    )
    l0, r0 = gate(where, [l0, r0], (grad_tokens,))
    qk = plus(qk[:, 0], qk_y)
    vo = plus(vo[:, 0], vo_x)
    four = jnp.concatenate([qk[0], qk[1], vo[0], vo[1]], axis=-1)
    four, other = line_parts(four, lo, 1)
    four_near = swap_line(other, 1)
    left = plus(l0[0], l_c[0], l_x)
    right = plus(r0[:, 0], r_c[:, 0], r_y)
    left_y, right_x = send(left[1], "y"), send(right[1], "x")
    four, other = line_parts(plus(four, four_near), hi, 0)
    four_far = swap_line(other, 2)
    grad_merge = jnp.concatenate([plus(left[0], left_y), plus(right[0], right_x)], axis=-1)
    grad_merge, other = line_parts(grad_merge, lo, 1)
    grad_merge, other = line_parts(plus(grad_merge, swap_line(other, 1)), hi, 0)
    four = plus(four, four_far)
    grad_merge = plus(grad_merge, swap_line(other, 2))
    grad_query, grad_key, grad_value, grad_result = (four[:, i * col : (i + 1) * col] for i in range(4))

    (three,) = gate(where, [sums_one], (grad_tokens,))
    for axis in ("c", "x", "y"):
        three = three + swap(three, axis)
    for bit in (1, 2):
        three = three + swap_line(three, bit)
    share = d // count
    three = lax.dynamic_slice_in_dim(three, device * share, share, 1)
    four_rows = lax.dynamic_slice_in_dim(own[:4], device * share, share, 1)
    loss_value = own[4, 0] / (own[5, 0] * d)
    share = 2 * half // count
    hidden_row = lax.dynamic_slice_in_dim(own[8:12].reshape(-1), device * share, share, 0)
    sums = (three[2], three[0], three[1], four_rows[2], four_rows[0], four_rows[1], four_rows[3], hidden_row)
    return (
        block_out,
        loss_value,
        grad_tokens,
        grad_shortcut,
        grad_merge,
        sums[0],
        sums[1],
        sums[2],
        grad_query,
        grad_key,
        grad_value,
        grad_result.T,
        sums[3],
        sums[4],
        sums[5],
        grad_expand,
        sums[7],
        grad_contract.T,
        sums[6],
    )


ARGUMENTS = (
    ("ft", None),
    ("ft", None),
    ("ft", None),
    ("f",),
    ("ft", None),
    ("ft",),
    ("ft",),
    ("ft",),
    ("f", "t"),
    ("f", "t"),
    ("f", "t"),
    ("t", "f"),
    ("ft",),
    ("ft",),
    ("ft",),
    ("f", "t"),
    ("ft",),
    ("t", "f"),
    ("ft",),
)
RESULTS = (
    ("ft", None),
    (),
    ("ft", None),
    ("ft", None),
    ("ft", None),
    ("ft",),
    ("ft",),
    ("ft",),
    ("f", "t"),
    ("f", "t"),
    ("f", "t"),
    ("t", "f"),
    ("ft",),
    ("ft",),
    ("ft",),
    ("f", "t"),
    ("ft",),
    ("t", "f"),
    ("ft",),
)


def solution(mesh):
    def whole(*args):
        rows = args[0].shape[0] // mesh.size
        if rows == SEQ_LEN and dict(mesh.shape) == {"fsdp": 16, "tp": 2}:
            plan = one_sequence_plan
            use = jax.sharding.Mesh(mesh.devices.reshape(4, 2, 2, 2), ("z", "y", "c", "x"))
            names = {"f": ("z", "y", "c"), "t": ("x",), "ft": ("z", "y", "c", "x")}
        else:
            plan = per_device_split
            use = mesh
            names = {"f": ("fsdp",), "t": ("tp",), "ft": ("fsdp", "tp")}

        def place(entry):
            return P(*(None if e is None else names[e] for e in entry))

        return jax.shard_map(
            plan,
            mesh=use,
            in_specs=tuple(place(e) for e in ARGUMENTS),
            out_specs=tuple(place(e) for e in RESULTS),
            check_vma=False,
        )(*args)

    return whole
```

```python
import functools
import math

import jax
import jax.numpy as jnp
from jax import lax
from jax.experimental import pallas as pl
from jax.experimental.pallas import tpu as pltpu
from jax.sharding import PartitionSpec as P

D = 1024
HEADS = 16
SEQ_LEN = 1104


EPSILON = 1e-05


def layer_norm(value, gain, shift):
    centred = value - jnp.mean(value, axis=-1, keepdims=True)
    spread = jnp.mean(centred * centred, axis=-1, keepdims=True)
    return centred * lax.rsqrt(spread + EPSILON) * gain + shift


def contract_rows(left, right):
    return lax.dot_general(
        left, right, (((0,), (0,)), ((), ())), preferred_element_type=jnp.float32
    )


def contract_cols(left, right):
    return lax.dot_general(
        left, right, (((1,), (1,)), ((), ())), preferred_element_type=jnp.float32
    )


def attend_forward(queries, keys_all, values):
    scale = float(queries.shape[-1]) ** (-0.5)
    scores = (
        jnp.einsum("qhd,khd->hqk", queries, keys_all, preferred_element_type=jnp.float32) * scale
    )
    peak_score = jnp.max(scores, axis=-1, keepdims=True)
    raised = jnp.exp(scores - peak_score)
    row_total = jnp.sum(raised, axis=-1, keepdims=True)
    weights_low = (raised / row_total).astype(jnp.bfloat16)
    output = jnp.einsum("hqk,khd->qhd", weights_low, values, preferred_element_type=jnp.float32)
    return (output.astype(jnp.bfloat16), peak_score + jnp.log(row_total))


def attend_backward(queries, keys_all, values, summary, upstream):
    scale = float(queries.shape[-1]) ** (-0.5)
    scores = (
        jnp.einsum("qhd,khd->hqk", queries, keys_all, preferred_element_type=jnp.float32) * scale
    )
    probs_full = jnp.exp(scores - summary)
    grad_probs = jnp.einsum("qhd,khd->hqk", upstream, values, preferred_element_type=jnp.float32)
    grad_values = jnp.einsum(
        "hqk,qhd->khd",
        probs_full.astype(jnp.bfloat16),
        upstream,
        preferred_element_type=jnp.float32,
    )
    centre = jnp.sum(probs_full * grad_probs, axis=-1, keepdims=True)
    grad_scores = (probs_full * (grad_probs - centre)).astype(jnp.bfloat16)
    grad_queries = (
        jnp.einsum("hqk,khd->qhd", grad_scores, keys_all, preferred_element_type=jnp.float32)
        * scale
    )
    grad_keys = (
        jnp.einsum("hqk,qhd->khd", grad_scores, queries, preferred_element_type=jnp.float32) * scale
    )
    return (
        grad_queries.astype(jnp.bfloat16),
        grad_keys.astype(jnp.bfloat16),
        grad_values.astype(jnp.bfloat16),
    )


def gelu_exact(value):
    return jax.nn.gelu(value, approximate=False)


def per_device_split(
    entering_states,
    bypass_states,
    mentor_states,
    occupancy_mask,
    bypass_merge_matrix,
    bypass_merge_offset,
    mixer_layernorm_scale,
    mixer_layernorm_offset,
    asking_map_matrix,
    lookup_map_matrix,
    content_map_matrix,
    mixer_result_matrix,
    mixer_result_offset,
    perceptron_layernorm_scale,
    perceptron_layernorm_offset,
    expand_layer_matrix,
    expand_layer_offset,
    contract_layer_matrix,
    contract_layer_offset,
):
    rows = entering_states.shape[0]
    width = D // HEADS
    position = lax.axis_index("tp")
    (
        merge_full,
        merge_add,
        gain_one,
        shift_one,
        output_add,
        gain_two,
        shift_two,
        hidden_add,
        down_add,
    ) = (
        lax.all_gather(bypass_merge_matrix, ("fsdp", "tp"), axis=0, tiled=True),
        lax.all_gather(bypass_merge_offset, ("fsdp", "tp"), axis=0, tiled=True),
        lax.all_gather(mixer_layernorm_scale, ("fsdp", "tp"), axis=0, tiled=True),
        lax.all_gather(mixer_layernorm_offset, ("fsdp", "tp"), axis=0, tiled=True),
        lax.all_gather(mixer_result_offset, ("fsdp", "tp"), axis=0, tiled=True),
        lax.all_gather(perceptron_layernorm_scale, ("fsdp", "tp"), axis=0, tiled=True),
        lax.all_gather(perceptron_layernorm_offset, ("fsdp", "tp"), axis=0, tiled=True),
        lax.all_gather(expand_layer_offset, ("fsdp", "tp"), axis=0, tiled=True),
        lax.all_gather(contract_layer_offset, ("fsdp", "tp"), axis=0, tiled=True),
    )
    query_full, key_full, value_full, output_full, hidden_full, down_full = (
        lax.all_gather(asking_map_matrix, "fsdp", axis=0, tiled=True),
        lax.all_gather(lookup_map_matrix, "fsdp", axis=0, tiled=True),
        lax.all_gather(content_map_matrix, "fsdp", axis=0, tiled=True),
        lax.all_gather(mixer_result_matrix, "fsdp", axis=1, tiled=True),
        lax.all_gather(expand_layer_matrix, "fsdp", axis=0, tiled=True),
        lax.all_gather(contract_layer_matrix, "fsdp", axis=1, tiled=True),
    )
    gain_one = gain_one.astype(jnp.float32)
    shift_one = shift_one.astype(jnp.float32)
    gain_two = gain_two.astype(jnp.float32)
    shift_two = shift_two.astype(jnp.float32)
    project = jnp.concatenate([query_full, key_full, value_full], axis=1)
    local_width = query_full.shape[1]
    local_heads = local_width // width
    local_hidden = hidden_full.shape[1]
    row_index = position * rows + jnp.arange(rows, dtype=jnp.int32)
    slot_of_row = row_index // SEQ_LEN
    series_place_total = occupancy_mask.shape[0]
    agreeing_lines = (
        slot_of_row[:, None] == jnp.arange(series_place_total, dtype=jnp.int32)[None, :]
    ).astype(jnp.float32)
    alive_tokens = jnp.sum(
        agreeing_lines * occupancy_mask.astype(jnp.float32)[None, :], axis=1, keepdims=True
    )
    joined = jnp.concatenate([entering_states, bypass_states], axis=1)
    merged = jnp.dot(joined, merge_full, preferred_element_type=jnp.float32) + merge_add.astype(
        jnp.float32
    )
    first = layer_norm(merged, gain_one, shift_one).astype(jnp.bfloat16)
    first_all = lax.all_gather(first, "tp", axis=0, tiled=True)
    group_rows = first_all.shape[0]
    slots = group_rows // SEQ_LEN
    projected = jnp.dot(first_all, project, preferred_element_type=jnp.float32).astype(jnp.bfloat16)
    shaped = projected.reshape(slots, SEQ_LEN, 3, local_heads, width)
    queries = shaped[:, :, 0]
    keys_all = shaped[:, :, 1]
    values = shaped[:, :, 2]
    attended, summary = lax.map(
        lambda item: attend_forward(item[0], item[1], item[2]), (queries, keys_all, values)
    )
    attended_flat = attended.reshape(group_rows, local_width)
    attention_term = jnp.dot(attended_flat, output_full, preferred_element_type=jnp.float32)
    after_attn = (
        merged
        + lax.psum_scatter(
            attention_term.astype(jnp.bfloat16), "tp", scatter_dimension=0, tiled=True
        ).astype(jnp.float32)
        + output_add.astype(jnp.float32)
    )
    second = layer_norm(after_attn, gain_two, shift_two).astype(jnp.bfloat16)
    second_all = lax.all_gather(second, "tp", axis=0, tiled=True)
    hidden_slice = lax.dynamic_slice_in_dim(
        hidden_add.astype(jnp.float32), position * local_hidden, local_hidden, 0
    )
    hidden = jnp.dot(second_all, hidden_full, preferred_element_type=jnp.float32) + hidden_slice
    active = gelu_exact(hidden).astype(jnp.bfloat16)
    feed_term = jnp.dot(active, down_full, preferred_element_type=jnp.float32)
    final = (
        after_attn
        + lax.psum_scatter(
            feed_term.astype(jnp.bfloat16), "tp", scatter_dimension=0, tiled=True
        ).astype(jnp.float32)
        + down_add.astype(jnp.float32)
    )
    missing = final - mentor_states.astype(jnp.float32)
    grad_final = alive_tokens * missing
    block_out = (final * alive_tokens).astype(jnp.bfloat16)
    energy, counted = lax.psum(
        (0.5 * jnp.sum(grad_final * missing), jnp.sum(alive_tokens)), ("fsdp", "tp")
    )
    loss_value = energy / (counted * D)
    grad_down_bias = jnp.sum(grad_final, axis=0)
    upstream = grad_final.astype(jnp.bfloat16)
    upstream_all = lax.all_gather(upstream, "tp", axis=0, tiled=True)
    grad_down = contract_rows(active, upstream_all)
    grad_active = contract_cols(upstream_all, down_full)
    gelu_value, gelu_pull = jax.vjp(gelu_exact, hidden)
    grad_hidden = gelu_pull(grad_active)[0].astype(jnp.bfloat16)
    grad_hidden_local = jnp.sum(grad_hidden.astype(jnp.float32), axis=0)
    grad_hidden_weight = contract_rows(second_all, grad_hidden)
    feed_back_term = contract_cols(grad_hidden, hidden_full)
    grad_second = lax.psum_scatter(
        feed_back_term.astype(jnp.bfloat16), "tp", scatter_dimension=0, tiled=True
    ).astype(jnp.float32)
    hidden_bias_term = lax.dynamic_update_slice_in_dim(
        jnp.zeros((hidden_add.shape[0],), jnp.float32),
        grad_hidden_local,
        position * local_hidden,
        0,
    )
    norm_value, second_pull = jax.vjp(layer_norm, after_attn, gain_two, shift_two)
    back_after, grad_gain_two, grad_shift_two = second_pull(grad_second)
    grad_after = grad_final + back_after
    grad_output_bias = jnp.sum(grad_after, axis=0)
    branch_all = lax.all_gather(grad_after.astype(jnp.bfloat16), "tp", axis=0, tiled=True)
    grad_output_weight = contract_rows(attended_flat, branch_all)
    grad_attended = contract_cols(branch_all, output_full).astype(jnp.bfloat16)
    upstream_heads = grad_attended.reshape(slots, SEQ_LEN, local_heads, width)
    grad_q_heads, grad_k_heads, grad_v_heads = lax.map(
        lambda item: attend_backward(item[0], item[1], item[2], item[3], item[4]),
        (queries, keys_all, values, summary, upstream_heads),
    )
    grad_projected = jnp.stack([grad_q_heads, grad_k_heads, grad_v_heads], axis=2).reshape(
        group_rows, 3 * local_width
    )
    grad_project = contract_rows(first_all, grad_projected)
    attention_back_term = contract_cols(grad_projected, project)
    grad_first = lax.psum_scatter(
        attention_back_term.astype(jnp.bfloat16), "tp", scatter_dimension=0, tiled=True
    ).astype(jnp.float32)
    first_value, first_pull = jax.vjp(layer_norm, merged, gain_one, shift_one)
    back_merged, grad_gain_one, grad_shift_one = first_pull(grad_first)
    grad_merged = grad_after + back_merged
    grad_merge_bias = jnp.sum(grad_merged, axis=0)
    merge_grad = grad_merged.astype(jnp.bfloat16)
    grad_merge_weight = contract_rows(joined, merge_grad)
    grad_joined = contract_cols(merge_grad, merge_full)
    model_width = entering_states.shape[1]
    grad_tokens = grad_joined[:, :model_width]
    grad_shortcut = grad_joined[:, model_width:]
    grad_query, grad_key, grad_value, grad_output, grad_hidden_full, grad_down_full = (
        lax.psum_scatter(
            grad_project[:, :local_width].astype(jnp.bfloat16),
            "fsdp",
            scatter_dimension=0,
            tiled=True,
        ).astype(jnp.float32),
        lax.psum_scatter(
            grad_project[:, local_width : 2 * local_width].astype(jnp.bfloat16),
            "fsdp",
            scatter_dimension=0,
            tiled=True,
        ).astype(jnp.float32),
        lax.psum_scatter(
            grad_project[:, 2 * local_width :].astype(jnp.bfloat16),
            "fsdp",
            scatter_dimension=0,
            tiled=True,
        ).astype(jnp.float32),
        lax.psum_scatter(
            grad_output_weight.astype(jnp.bfloat16), "fsdp", scatter_dimension=1, tiled=True
        ).astype(jnp.float32),
        lax.psum_scatter(
            grad_hidden_weight.astype(jnp.bfloat16), "fsdp", scatter_dimension=0, tiled=True
        ).astype(jnp.float32),
        lax.psum_scatter(
            grad_down.astype(jnp.bfloat16), "fsdp", scatter_dimension=1, tiled=True
        ).astype(jnp.float32),
    )
    (
        merge_weight_sum,
        merge_bias_sum,
        gain_one_sum,
        shift_one_sum,
        output_bias_sum,
        gain_two_sum,
        shift_two_sum,
        hidden_bias_sum,
        down_bias_sum,
    ) = (
        lax.psum_scatter(grad_merge_weight, ("fsdp", "tp"), scatter_dimension=0, tiled=True),
        lax.psum_scatter(grad_merge_bias, ("fsdp", "tp"), scatter_dimension=0, tiled=True),
        lax.psum_scatter(grad_gain_one, ("fsdp", "tp"), scatter_dimension=0, tiled=True),
        lax.psum_scatter(grad_shift_one, ("fsdp", "tp"), scatter_dimension=0, tiled=True),
        lax.psum_scatter(grad_output_bias, ("fsdp", "tp"), scatter_dimension=0, tiled=True),
        lax.psum_scatter(grad_gain_two, ("fsdp", "tp"), scatter_dimension=0, tiled=True),
        lax.psum_scatter(grad_shift_two, ("fsdp", "tp"), scatter_dimension=0, tiled=True),
        lax.psum_scatter(hidden_bias_term, ("fsdp", "tp"), scatter_dimension=0, tiled=True),
        lax.psum_scatter(grad_down_bias, ("fsdp", "tp"), scatter_dimension=0, tiled=True),
    )
    return (
        block_out,
        loss_value,
        grad_tokens,
        grad_shortcut,
        merge_weight_sum,
        merge_bias_sum,
        gain_one_sum,
        shift_one_sum,
        grad_query,
        grad_key,
        grad_value,
        grad_output,
        output_bias_sum,
        gain_two_sum,
        shift_two_sum,
        grad_hidden_full,
        hidden_bias_sum,
        grad_down_full,
        down_bias_sum,
    )


LOG2E = math.log2(math.e)
PAIR = 128
CHUNK = 368


def nn(a, b):
    return lax.dot_general(a, b, (((1,), (0,)), ((), ())), preferred_element_type=jnp.float32)


def nt(a, b):
    return lax.dot_general(a, b, (((1,), (1,)), ((), ())), preferred_element_type=jnp.float32)


def tn(a, b):
    return lax.dot_general(a, b, (((0,), (0,)), ((), ())), preferred_element_type=jnp.float32)


def vmem():
    return pltpu.CompilerParams(vmem_limit_bytes=60 * 2**20)


def attention_forward_kernel(q_ref, k_ref, v_ref, o_ref, l_ref):
    count = q_ref.shape[0]
    scale = (PAIR // 2) ** -0.5 * LOG2E
    low = lax.broadcasted_iota(jnp.int32, (1, PAIR), 1) < PAIR // 2
    keys, values = k_ref[...], v_ref[...]
    zero = jnp.zeros_like(keys)
    heads = (jnp.where(low, keys, zero), jnp.where(low, zero, keys))
    wide = jnp.concatenate([values, jnp.ones_like(values)], axis=1)
    for start in range(0, count, CHUNK):
        part = slice(start, min(start + CHUNK, count))
        queries = q_ref[part, :]
        outs, sums = [], []
        for head in heads:
            scores = nt(queries, head)
            peak = jnp.max(scores, axis=1, keepdims=True) * scale
            raised = jnp.exp2(scores * scale - peak).astype(jnp.bfloat16)
            both = nn(raised, wide)
            total = both[:, PAIR:]
            outs.append(both[:, :PAIR] / total)
            sums.append(peak + jnp.log2(total))
        o_ref[part, :] = jnp.where(low, outs[0], outs[1]).astype(jnp.bfloat16)
        l_ref[part, :] = jnp.where(low, sums[0], sums[1])


def attention_backward_kernel(q_ref, k_ref, v_ref, o_ref, l_ref, u_ref, out_ref, total_ref):
    count = q_ref.shape[0]
    plain = (PAIR // 2) ** -0.5
    scale = plain * LOG2E
    low = lax.broadcasted_iota(jnp.int32, (1, PAIR), 1) < PAIR // 2
    queries, upstream = q_ref[...], u_ref[...]
    product = upstream.astype(jnp.float32) * o_ref[...].astype(jnp.float32)
    left = jnp.sum(jnp.where(low, product, 0.0), axis=1, keepdims=True)
    right = jnp.sum(jnp.where(low, 0.0, product), axis=1, keepdims=True)
    centres = jnp.transpose(jnp.where(low, left, right))
    logs = jnp.transpose(l_ref[...])
    for head in range(2):

        def own(value):
            zero = jnp.zeros_like(value)
            return jnp.where(low, value, zero) if head == 0 else jnp.where(low, zero, value)

        row = head * (PAIR // 2)
        own_queries, own_upstream = own(queries), own(upstream)
        log_row, centre = logs[row : row + 1, :], centres[row : row + 1, :]
        for start in range(0, count, CHUNK):
            part = slice(start, min(start + CHUNK, count))
            keys, values = k_ref[part, :], v_ref[part, :]
            probs = jnp.exp2(nt(keys, own_queries) * scale - log_row)
            slopes = (probs * (nt(values, own_upstream) - centre)).astype(jnp.bfloat16)
            grad_v = nn(probs.astype(jnp.bfloat16), own_upstream).astype(jnp.bfloat16)
            grad_k = (nn(slopes, own_queries) * plain).astype(jnp.bfloat16)
            grad_q = tn(slopes, own(keys))
            if head == 0:
                out_ref[1, part, :] = grad_k
                out_ref[2, part, :] = grad_v
            else:
                out_ref[1, part, :] = jnp.where(low, out_ref[1, part, :], grad_k)
                out_ref[2, part, :] = jnp.where(low, out_ref[2, part, :], grad_v)
            if head == 0 and start == 0:
                total_ref[...] = grad_q
            else:
                total_ref[...] += grad_q
    out_ref[0] = (total_ref[...] * plain).astype(jnp.bfloat16)


def gelu_both(value):
    t = 1.0 / (1.0 + 0.3275911 * math.sqrt(0.5) * jnp.abs(value))
    bell = jnp.exp2(value * value * (-0.5 * LOG2E))
    poly = 0.5 * 1.061405429 * t - 0.5 * 1.453152027
    poly = poly * t + 0.5 * 1.421413741
    poly = poly * t - 0.5 * 0.284496736
    poly = poly * t + 0.5 * 0.254829592
    rest = poly * t * bell
    below = jnp.where(value >= 0, 1.0 - rest, rest)
    return value * below, below + value * bell * (1.0 / math.sqrt(2.0 * math.pi))


def normalized(value):
    centred = value - jnp.mean(value, axis=-1, keepdims=True)
    spread = jnp.mean(centred * centred, axis=-1, keepdims=True)
    inverse = lax.rsqrt(spread + EPSILON)
    return centred * inverse, inverse


def place_at(where_ref, hi, lo, y_rel, c_rel, rows):
    y = jnp.bitwise_xor(where_ref[0], y_rel)
    c = jnp.bitwise_xor(where_ref[1], c_rel)
    return pl.multiple_of(((hi * 2 + lo) * 4 + y * 2 + c) * rows, rows)


BITS = (0, 1)


def once(block, index):
    return pl.BlockSpec(block, index, pipeline_mode=pl.Buffered(1))


def call(kernel, grid, where, ins, outs, scratch, name, after=(), aliases=()):
    first, count = len(ins), len(after)

    def ordered_kernel(where_ref, *refs):
        kernel(where_ref, *refs[:first], *refs[first + count :])

    anywhere = pl.BlockSpec(memory_space=pl.ANY)
    return pl.pallas_call(
        ordered_kernel,
        grid_spec=pltpu.PrefetchScalarGridSpec(
            num_scalar_prefetch=1,
            grid=grid,
            in_specs=[spec for _, spec in ins] + [anywhere] * count,
            out_specs=[spec for _, _, spec in outs],
            scratch_shapes=scratch,
        ),
        out_shape=[jax.ShapeDtypeStruct(s, t) for s, t, _ in outs],
        input_output_aliases={1 + i: o for i, o in aliases},
        compiler_params=vmem(),
        cost_estimate=pl.CostEstimate(flops=0, bytes_accessed=0, transcendentals=0),
        name=name,
    )(where, *(x for x, _ in ins), *after)


def resident(shape):
    return once(shape, lambda *_: (0,) * len(shape))


def attention_forward(where, projected):
    rows, columns = projected.shape
    pairs = columns // 3 // PAIR

    def block(offset):
        return pl.BlockSpec((rows, PAIR), lambda j, s: (0, offset + j))

    return call(
        lambda where_ref, *refs: attention_forward_kernel(*refs),
        (pairs,),
        where,
        [(projected, block(0)), (projected, block(pairs)), (projected, block(2 * pairs))],
        [
            ((rows, pairs * PAIR), jnp.bfloat16, block(0)),
            ((rows, pairs * PAIR), jnp.float32, block(0)),
        ],
        [],
        "attention_forward",
    )


def attention_backward(where, projected, attended, logs, upstream, index, of, grads):
    rows, columns = projected.shape
    pairs = columns // 3 // PAIR
    here = index * (pairs // of)

    def block(offset):
        return pl.BlockSpec((rows, PAIR), lambda j, s: (0, offset + here + j))

    ins = [
        (projected, block(0)),
        (projected, block(pairs)),
        (projected, block(2 * pairs)),
        (attended, block(0)),
        (logs, block(0)),
        (upstream, block(0)),
    ]
    aliases = ()
    if grads is not None:
        ins.append((grads, pl.BlockSpec(memory_space=pl.ANY)))
        aliases = ((6, 0),)

    def kernel(where_ref, *refs):
        attention_backward_kernel(*refs[:6], *refs[-2:])

    return call(
        kernel,
        (pairs // of,),
        where,
        ins,
        [((3, rows, pairs * PAIR), jnp.bfloat16, pl.BlockSpec((3, rows, PAIR), lambda j, s: (0, 0, here + j)))],
        [pltpu.VMEM((rows, PAIR), jnp.float32)],
        "attention_backward",
        (),
        aliases,
    )[0]


def gate(where, values, after):
    anywhere = pl.BlockSpec(memory_space=pl.ANY)
    return call(
        lambda *refs: None,
        (1,),
        where,
        [(v, anywhere) for v in values],
        [(v.shape, v.dtype, anywhere) for v in values],
        [],
        "gate",
        after,
        tuple((i, i) for i in range(len(values))),
    )


def fold_kernel(jobs, carried, waited, where, *refs):
    sources = iter(refs)
    total = sum(len(parts) for pieces, _ in jobs for parts in pieces)
    targets = iter(refs[total + carried + waited :])
    for pieces, results in jobs:
        held = [[next(sources) for _ in parts] for parts in pieces]
        for kind, select in results:
            out, begin = next(targets), 0
            at = tuple(slice(None) if t is None else jnp.bitwise_xor(where[t[0]], t[1]) for t in select)
            for parts in held:
                value = parts[0][at + (Ellipsis,)].astype(jnp.float32)
                for part in parts[1:]:
                    value = value + part[at + (Ellipsis,)].astype(jnp.float32)
                end = begin + value.shape[-1]
                out[..., begin:end] = value.astype(out.dtype)
                begin = end


def fold(where, jobs, carry=(), after=()):
    ins, outs, plan = [], [], []
    for pieces, results in jobs:
        columns = 0
        for parts in pieces:
            for array, lead in parts:
                fixed = lead + (None, None)
                block = tuple(n if t is None else pl.squeezed for n, t in zip(array.shape, fixed))
                index = tuple(0 if t is None else t for t in fixed)
                ins.append((array, once(block, lambda i, s, index=index: index)))
            columns += array.shape[-1]
        shape = tuple(n for n, t in zip(array.shape, fixed) if t is None)[:-1] + (columns,)
        for kind, select in results:
            made = tuple(n for n, t in zip(shape, select) if t is None) + shape[len(select) :]
            outs.append((made, kind, resident(made)))
        plan.append((pieces, results))
    anywhere = pl.BlockSpec(memory_space=pl.ANY)
    count, made = len(ins), len(outs)
    ins += [(c, anywhere) for c in carry]
    outs += [(c.shape, c.dtype, anywhere) for c in carry]
    return call(
        functools.partial(fold_kernel, plan, len(carry), 0),
        (1,),
        where,
        ins,
        outs,
        [],
        "fold",
        after,
        tuple((count + i, made + i) for i in range(len(carry))),
    )


def pile_kernel(slot, axis, where, mine, other, *outs):
    here = 0 if slot is None else where[slot]
    there = 1 - here
    lead = outs[0].shape[:axis]
    rows = outs[0].shape[-2]
    for number, out in enumerate(outs):
        part = slice(number * rows, (number + 1) * rows)
        for i in range(math.prod(lead)):
            at = ()
            for size in reversed(lead):
                at = (i % size,) + at
                i //= size
            out[at + (here,)] = mine[at + (Ellipsis, part, slice(None))]
            out[at + (there,)] = other[at + (Ellipsis, part, slice(None))]


def pile(where, slot, mine, other, axis, parts=1):
    shape = mine.shape[:axis] + (2,) + mine.shape[axis:-2] + (mine.shape[-2] // parts, mine.shape[-1])
    made = call(
        functools.partial(pile_kernel, slot, axis),
        (1,),
        where,
        [(mine, resident(mine.shape)), (other, resident(mine.shape))],
        [(shape, mine.dtype, resident(shape))] * parts,
        [],
        "pile",
    )
    return made if parts > 1 else made[0]


def merge_kernel(where, ent, byp, full, out):
    half = ent.shape[1]
    weight = full[...].reshape(2 * half, half)
    out[...] = nn(ent[...], weight[:half, :]) + nn(byp[...], weight[half:, :])


def merge_forward(where, ent, byp, gathered, r):
    rows, d = ent.shape
    part = pl.BlockSpec((CHUNK, d), lambda i, w: (i, 0))
    return call(
        merge_kernel,
        (rows // CHUNK,),
        where,
        [(ent, part), (byp, part), (gathered, resident((2, 2, 2, 2, 2, r, d)))],
        [((rows, d), jnp.float32, part)],
        [],
        "merge_forward",
    )[0]


def weight_block(r, col, number):
    def index(*args):
        which, x_rel = number(*args[:-1])
        return 0, 0, 0, 0, jnp.bitwise_xor(x_rel, args[-1][2]), 1 + which // 2, which % 2

    return pl.BlockSpec((2, 2, 2, 2, pl.squeezed, r, col), index)


def project_kernel(where, raw, vec, weight, merged, first, out):
    @pl.when((pl.program_id(0) == 0) & (pl.program_id(1) == 0))
    def _():
        for start in range(0, raw.shape[0], CHUNK):
            part = slice(start, start + CHUNK)
            total = raw[part, :] + vec[0:1, :]
            merged[part, :] = total
            norm, _ = normalized(total)
            first[part, :] = (norm * vec[1:2, :] + vec[2:3, :]).astype(jnp.bfloat16)

    out[...] = nn(first[...], weight[...].reshape(first.shape[1], -1)).astype(jnp.bfloat16)


def project_forward(where, raw, vec, gathered, r, col):
    rows, d = raw.shape
    f32, bf16 = jnp.float32, jnp.bfloat16
    return call(
        project_kernel,
        (3, 2),
        where,
        [
            (raw, resident((rows, d))),
            (vec, resident(vec.shape)),
            (gathered, weight_block(r, col, lambda w, x: (w, x))),
        ],
        [
            ((rows, d), f32, resident((rows, d))),
            ((rows, d), bf16, resident((rows, d))),
            ((rows, 6 * col), bf16, pl.BlockSpec((rows, col), lambda w, x, s: (0, w * 2 + x))),
        ],
        [],
        "project_forward",
    )


def result_kernel(where, attended, merged, vec, weight, after, second, total):
    step = pl.program_id(0)
    natural = weight[...].reshape(after.shape[1], -1)

    @pl.when(step == 0)
    def _():
        total[...] = nt(attended[...], natural)

    @pl.when(step == 1)
    def _():
        for start in range(0, after.shape[0], CHUNK):
            here = slice(start, start + CHUNK)
            part = nt(attended[here, :], natural)
            value = merged[here, :] + vec[3:4, :] + (total[here, :] + part)
            after[here, :] = value
            norm, _ = normalized(value)
            second[here, :] = (norm * vec[4:5, :] + vec[5:6, :]).astype(jnp.bfloat16)


def result_forward(where, attended, merged, vec, gathered, r, col):
    rows, d = merged.shape
    return call(
        result_kernel,
        (2,),
        where,
        [
            (attended, pl.BlockSpec((rows, col), lambda x, s: (0, x))),
            (merged, resident((rows, d))),
            (vec, resident(vec.shape)),
            (gathered, weight_block(r, col, lambda x: (3, x))),
        ],
        [
            ((rows, d), jnp.float32, resident((rows, d))),
            ((rows, d), jnp.bfloat16, resident((rows, d))),
        ],
        [pltpu.VMEM((rows, d), jnp.float32)],
        "result_forward",
    )


def fill_by_core(where, full, refs, rows):
    for c_rel, ref in enumerate(refs):
        for y_rel in BITS:
            for hi in BITS:
                for lo in BITS:
                    at = place_at(where, hi, lo, y_rel, c_rel, rows)
                    full[pl.ds(at, rows), :] = ref[y_rel, hi, lo]


def spill_by_core(where, full, refs, rows):
    for c_rel, ref in enumerate(refs):
        for y_rel in BITS:
            for hi in BITS:
                for lo in BITS:
                    at = place_at(where, hi, lo, y_rel, c_rel, rows)
                    ref[y_rel, hi, lo] = full[pl.ds(at, rows), :]


def expand_kernel(rows, where, second, bias, w0, w1, active, slope, full):
    fill_by_core(where, full, (w0, w1), rows)
    for start in range(0, second.shape[0], CHUNK):
        part = slice(start, start + CHUNK)
        hidden = nn(second[part, :], full[...]) + bias[...]
        value, rate = gelu_both(hidden)
        active[part, :] = value.astype(jnp.bfloat16)
        slope[part, :] = rate.astype(jnp.bfloat16)


def expand_forward(where, second, bias, pieces, block=512):
    rows, d = second.shape
    *_, r, half = pieces[0].shape
    weight = pl.BlockSpec((2, 2, 2, r, block), lambda j, s: (0, 0, 0, 0, j))
    out = pl.BlockSpec((rows, block), lambda j, s: (0, j))
    return call(
        functools.partial(expand_kernel, r),
        (half // block,),
        where,
        [(second, resident((rows, d))), (bias, pl.BlockSpec((1, block), lambda j, s: (0, j)))]
        + [(p, weight) for p in pieces],
        [((rows, half), jnp.bfloat16, out)] * 2,
        [pltpu.VMEM((d, block), jnp.bfloat16)],
        "expand_forward",
    )


def contract_kernel(steps, where, alive, a0, a1, after, mentor, vec, weight, out, upstream, sums, energy, total):
    step = pl.program_id(0)
    count, d = after.shape
    full = weight[...].reshape(d, -1)

    @pl.when(step == 0)
    def _():
        total[...] = nt(a0[...], full)

    @pl.when((step > 0) & (step < steps))
    def _():
        total[...] += nt(a0[...], full)

    @pl.when((step >= steps) & (step < 2 * steps - 1))
    def _():
        total[...] += nt(a1[...], full)

    @pl.when(step == 2 * steps - 1)
    def _():
        live = alive[0]
        column, squares = 0.0, 0.0
        for start in range(0, count, CHUNK):
            part = slice(start, start + CHUNK)
            final = after[part, :] + (total[part, :] + nt(a1[part, :], full)) + vec[6:7, :]
            missing = final - mentor[part, :].astype(jnp.float32)
            slope = live * missing
            out[part, :] = (live * final).astype(jnp.bfloat16)
            upstream[part, :] = slope.astype(jnp.bfloat16)
            column += jnp.sum(slope, axis=0, keepdims=True)
            squares += jnp.sum(slope * missing, axis=0, keepdims=True)
        sums[...] = jnp.broadcast_to(column, sums.shape)
        energy[...] = jnp.broadcast_to(0.5 * jnp.sum(squares, axis=1, keepdims=True), energy.shape)


def contract_forward(where, alive, active, after, mentor, vec, weights, block=1024):
    rows, d = after.shape
    *_, r, half = weights.shape
    steps = half // block
    weight = pl.BlockSpec(
        (2, 2, 2, 2, pl.squeezed, r, block),
        lambda j, s: (0, 0, 0, 0, jnp.bitwise_xor(j // steps, s[2]), 0, j % steps),
    )
    f32, bf16 = jnp.float32, jnp.bfloat16
    whole = resident((rows, d))
    return call(
        functools.partial(contract_kernel, steps),
        (2 * steps,),
        where,
        [
            (alive, pl.BlockSpec(memory_space=pltpu.SMEM)),
            (active[0], pl.BlockSpec((rows, block), lambda j, s: (0, jnp.minimum(j, steps - 1)))),
            (active[1], pl.BlockSpec((rows, block), lambda j, s: (0, jnp.maximum(j - steps, 0)))),
            (after, whole),
            (mentor, whole),
            (vec, resident(vec.shape)),
            (weights, weight),
        ],
        [
            ((rows, d), bf16, whole),
            ((rows, d), bf16, whole),
            ((8, d), f32, resident((8, d))),
            ((8, 128), f32, resident((8, 128))),
        ],
        [pltpu.VMEM((rows, d), f32)],
        "contract_forward",
    )


def feed_backward_kernel(rows, where, upstream, second, active, slope, weight, w0, w1,
                         grad_second, e0, e1, d0, d1, bias, up, result, total):
    step, last = pl.program_id(0), pl.num_programs(0) - 1
    fill_by_core(where, up, (w0, w1), rows)
    grad_active = nn(upstream[...], weight[...].reshape(up.shape))
    grad_hidden = grad_active * slope[...].astype(jnp.float32)
    bias[...] = jnp.broadcast_to(jnp.sum(grad_hidden, axis=0, keepdims=True), bias.shape)
    grad_hidden = grad_hidden.astype(jnp.bfloat16)
    result[...] = tn(upstream[...], active[...]).astype(jnp.bfloat16)
    spill_by_core(where, result, (d0, d1), rows)
    back = nt(grad_hidden, up[...])

    @pl.when(step == 0)
    def _():
        total[...] = back

    @pl.when((step > 0) & (step < last))
    def _():
        total[...] += back

    @pl.when(step == last)
    def _():
        grad_second[...] = (total[...] + back).astype(jnp.bfloat16)

    result[...] = tn(second[...], grad_hidden).astype(jnp.bfloat16)
    spill_by_core(where, result, (e0, e1), rows)


def feed_backward(where, upstream, second, active, slope, down, up, x_rel, block=512):
    rows, d = upstream.shape
    *_, r, half = up[0].shape
    f32, bf16 = jnp.float32, jnp.bfloat16
    whole = resident((rows, d))
    part = pl.BlockSpec((rows, block), lambda j, s: (0, j))
    piece = pl.BlockSpec((2, 2, 2, r, block), lambda j, s: (0, 0, 0, 0, j))
    weight = pl.BlockSpec(
        (2, 2, 2, 2, pl.squeezed, r, block),
        lambda j, s: (0, 0, 0, 0, jnp.bitwise_xor(x_rel, s[2]), 0, j),
    )
    return call(
        functools.partial(feed_backward_kernel, r),
        (half // block,),
        where,
        [(upstream, whole), (second, whole), (active, part), (slope, part), (down, weight)]
        + [(p, piece) for p in up],
        [((rows, d), bf16, whole)]
        + [((2, 2, 2, r, half), bf16, piece)] * 4
        + [((8, half), f32, pl.BlockSpec((8, block), lambda j, s: (0, j)))],
        [pltpu.VMEM((d, block), bf16)] * 2 + [pltpu.VMEM((rows, d), f32)],
        "feed_backward",
    )


def norm_backward_kernel(count, gain_row, last, where, value, base, vec, *refs):
    outs = 2 if last else 3
    grads, extra, (*total, low, sums) = refs[:count], refs[count:-outs], refs[-outs:]

    @pl.when(pl.program_id(0) == 0)
    def _():
        sums[...] = jnp.zeros_like(sums)
        if extra:
            column, energy, alive, own, other = extra
            d = sums.shape[1]
            sums[3:4, :] = column[0:1, :]
            sums[4:5, :] = jnp.broadcast_to(energy[0:1, 0:1], (1, d))
            sums[5:6, :] = jnp.full((1, d), alive[0] * (value.shape[0] * pl.num_programs(0)), jnp.float32)
            here = where[2] == 0
            for i in BITS:
                part = slice(i * d, (i + 1) * d)
                sums[8 + i : 9 + i, :] = jnp.where(here, own[0:1, part], other[0:1, part])
                sums[10 + i : 11 + i, :] = jnp.where(here, other[0:1, part], own[0:1, part])

    upstream = grads[0][...].astype(jnp.float32)
    for ref in grads[1:]:
        upstream = upstream + ref[...].astype(jnp.float32)
    norm, inverse = normalized(value[...])
    e = upstream * vec[gain_row : gain_row + 1, :]
    mean_e = jnp.mean(e, axis=-1, keepdims=True)
    mean_en = jnp.mean(e * norm, axis=-1, keepdims=True)
    result = base[...].astype(jnp.float32) + inverse * (e - mean_e - norm * mean_en)
    for ref in total:
        ref[...] = result
    low[...] = result.astype(jnp.bfloat16)
    for row, item in enumerate((upstream * norm, upstream, result)):
        sums[row : row + 1, :] += jnp.sum(item, axis=0, keepdims=True)


def norm_backward(where, value, base, vec, gain_row, grads, extra=(), last=False):
    rows, d = value.shape
    part = pl.BlockSpec((CHUNK, d), lambda i, s: (i, 0))
    height = 16 if extra else 8
    carried = [
        (x, pl.BlockSpec(memory_space=pltpu.SMEM) if x.ndim == 1 else resident(x.shape)) for x in extra
    ]
    return call(
        functools.partial(norm_backward_kernel, len(grads), gain_row, last),
        (rows // CHUNK,),
        where,
        [(value, part), (base, part), (vec, resident(vec.shape))] + [(g, part) for g in grads] + carried,
        [((rows, d), jnp.float32, part)] * (0 if last else 1)
        + [
            ((rows, d), jnp.bfloat16, part),
            ((height, d), jnp.float32, resident((height, d))),
        ],
        [],
        "norm_backward",
    )


def result_backward_kernel(rows, where, branch, attended, weight, grad, o0, o1, full):
    grad[...] = nn(branch[...], weight[...].reshape(branch.shape[1], -1)).astype(jnp.bfloat16)
    full[...] = tn(branch[...], attended[...]).astype(jnp.bfloat16)
    spill_by_core(where, full, (o0, o1), rows)


def result_backward(where, branch, attended, gathered, r, col):
    rows, d = branch.shape
    bf16 = jnp.bfloat16
    part = pl.BlockSpec((rows, col), lambda x, s: (0, x))
    piece = pl.BlockSpec((pl.squeezed, pl.squeezed, 2, 2, 2, r, col), lambda x, s: (1, x, 0, 0, 0, 0, 0))
    return call(
        functools.partial(result_backward_kernel, r),
        (2,),
        where,
        [
            (branch, resident((rows, d))),
            (attended, part),
            (gathered, weight_block(r, col, lambda x: (3, x))),
        ],
        [((rows, d), bf16, part)] + [((2, 2, 2, 2, 2, r, col), bf16, piece)] * 2,
        [pltpu.VMEM((d, col), bf16)],
        "result_backward",
    )


def project_weight_kernel(rows, where, first, grad, _, __, a0, a1, b0, b1, full):
    full[...] = tn(first[...], grad[...]).astype(jnp.bfloat16)

    @pl.when(pl.program_id(0) < 2)
    def _():
        spill_by_core(where, full, (a0, a1), rows)

    @pl.when(pl.program_id(0) == 2)
    def _():
        spill_by_core(where, full, (b0, b1), rows)


def project_weight(where, first, grads, with_result, r, col):
    rows, d = first.shape
    bf16 = jnp.bfloat16
    part = pl.BlockSpec((pl.squeezed, rows, col), lambda w, x, s: (w, 0, x))
    block = (pl.squeezed, pl.squeezed, 2, 2, 2, r, col)
    front = pl.BlockSpec(
        block, lambda w, x, s: (jnp.minimum(w, 1), jnp.where(w < 2, x, 1), 0, 0, 0, 0, 0)
    )
    back = pl.BlockSpec(block, lambda w, x, s: (0, jnp.where(w < 2, 0, x), 0, 0, 0, 0, 0))
    anywhere = pl.BlockSpec(memory_space=pl.ANY)
    return call(
        functools.partial(project_weight_kernel, r),
        (3, 2),
        where,
        [(first, resident((rows, d))), (grads, part)] + [(p, anywhere) for p in with_result],
        [((2, 2, 2, 2, 2, r, col), bf16, front)] * 2 + [((2, 2, 2, 2, 2, r, col), bf16, back)] * 2,
        [pltpu.VMEM((d, col), bf16)],
        "project_weight",
        (),
        ((2, 2), (3, 3)),
    )


def project_backward_kernel(where, grad, weight, out, total):
    part = nt(grad[...], weight[...].reshape(out.shape[1], -1))
    step = pl.program_id(0) * pl.num_programs(1) + pl.program_id(1)
    last = pl.num_programs(0) * pl.num_programs(1) - 1

    @pl.when(step == 0)
    def _():
        total[...] = part

    @pl.when((step > 0) & (step < last))
    def _():
        total[...] += part

    @pl.when(step == last)
    def _():
        out[...] = (total[...] + part).astype(jnp.bfloat16)


def project_backward(where, grads, gathered, r, col):
    _, rows, d = grads.shape
    return call(
        project_backward_kernel,
        (3, 2),
        where,
        [
            (grads, pl.BlockSpec((pl.squeezed, rows, col), lambda w, x, s: (w, 0, x))),
            (gathered, weight_block(r, col, lambda w, x: (w, x))),
        ],
        [((rows, d), jnp.bfloat16, resident((rows, d)))],
        [pltpu.VMEM((rows, d), jnp.float32)],
        "project_backward",
    )[0]


def merge_weight_kernel(where, ent, byp, grad, o0, o1, full):
    half = ent.shape[1]
    full[:half, :] = tn(ent[...], grad[...]).astype(jnp.bfloat16)
    full[half:, :] = tn(byp[...], grad[...]).astype(jnp.bfloat16)
    for c_rel, ref in enumerate((o0, o1)):
        for x_rel in BITS:
            x = jnp.bitwise_xor(where[2], x_rel)
            for y_rel in BITS:
                for hi in BITS:
                    for lo in BITS:
                        at = place_at(where, hi, lo, y_rel, c_rel, 128) + x * 64
                        ref[x_rel, y_rel, hi, lo] = full[pl.ds(pl.multiple_of(at, 64), 64), :]


def merge_weight(where, ent, byp, grad, r):
    rows, d = ent.shape
    half = d // 2
    bf16 = jnp.bfloat16
    whole = resident((rows, d))
    piece = pl.BlockSpec((pl.squeezed, 2, 2, 2, 2, r, half), lambda j, s: (j, 0, 0, 0, 0, 0, 0))
    return call(
        merge_weight_kernel,
        (2,),
        where,
        [(ent, whole), (byp, whole), (grad, pl.BlockSpec((rows, half), lambda j, s: (0, j)))],
        [((2, 2, 2, 2, 2, r, half), bf16, piece)] * 2,
        [pltpu.VMEM((2 * d, half), bf16)],
        "merge_weight",
    )


def merge_backward_kernel(where, grad, full, left, right):
    half = left.shape[1]
    weight = full[...].reshape(2 * half, half)
    left[...] = nt(grad[...], weight[:half, :])
    right[...] = nt(grad[...], weight[half:, :])


def merge_backward(where, grad, gathered, r, after):
    rows, d = grad.shape
    part = pl.BlockSpec((CHUNK, d), lambda i, w: (i, 0))
    return call(
        merge_backward_kernel,
        (rows // CHUNK,),
        where,
        [(grad, part), (gathered, resident((2, 2, 2, 2, 2, r, d)))],
        [((rows, d), jnp.float32, part)] * 2,
        [],
        "merge_backward",
        after,
    )


def swap(value, axis):
    return lax.ppermute(value, axis, [(0, 1), (1, 0)])


def swap_line(value, bit):
    return lax.ppermute(value, "z", [(i, i ^ bit) for i in range(4)])


def plus(*parts):
    total = parts[0].astype(jnp.float32)
    for part in parts[1:]:
        total = total + part.astype(jnp.float32)
    return total


def send(value, axis):
    return swap(value.astype(jnp.bfloat16), axis)


def line_parts(total, index, dim):
    mine = lax.dynamic_index_in_dim(total, index, dim, keepdims=False)
    other = lax.dynamic_index_in_dim(total, 1 - index, dim, keepdims=False)
    return mine, other.astype(jnp.bfloat16)


def one_sequence_plan(
    entering_states,
    bypass_states,
    mentor_states,
    occupancy_mask,
    bypass_merge_matrix,
    bypass_merge_offset,
    mixer_layernorm_scale,
    mixer_layernorm_offset,
    asking_map_matrix,
    lookup_map_matrix,
    content_map_matrix,
    mixer_result_matrix,
    mixer_result_offset,
    perceptron_layernorm_scale,
    perceptron_layernorm_offset,
    expand_layer_matrix,
    expand_layer_offset,
    contract_layer_matrix,
    contract_layer_offset,
):
    f32, bf16 = jnp.float32, jnp.bfloat16
    rows, d = entering_states.shape
    r, col = asking_map_matrix.shape
    half = expand_layer_matrix.shape[1]
    everyone = ("z", "y", "c", "x")
    z, y, c, x = (lax.axis_index(axis) for axis in everyone)
    hi, lo = z // 2, z % 2
    device = ((z * 2 + y) * 2 + c) * 2 + x
    where = jnp.stack([y, c, x, hi, lo]).astype(jnp.int32)
    small = (
        bypass_merge_offset,
        mixer_layernorm_scale,
        mixer_layernorm_offset,
        mixer_result_offset,
        perceptron_layernorm_scale,
        perceptron_layernorm_offset,
        contract_layer_offset,
        expand_layer_offset,
    )
    flat = jnp.concatenate(small)
    flat = jnp.pad(flat, (0, 8 * d - flat.shape[0])).reshape(8, d)
    pack = jnp.concatenate(
        [
            bypass_merge_matrix,
            jnp.concatenate([asking_map_matrix, lookup_map_matrix], axis=1),
            jnp.concatenate([content_map_matrix, mixer_result_matrix.T], axis=1),
            flat,
        ]
    )
    pack = lax.all_gather(pack, everyone, axis=0, tiled=False)
    gathered = pack.reshape((2,) * 5 + pack.shape[1:])

    down = lax.all_gather(contract_layer_matrix.T, everyone, axis=0, tiled=False)
    down = down.reshape((2,) * 5 + down.shape[1:])

    up = expand_layer_matrix
    up = pile(where, 3, up, swap_line(up, 2), 0)
    up = pile(where, 4, up, swap_line(up, 1), 1)
    up_block = pile(where, None, up, swap(up, "y"), 0)
    (gathered,) = gate(where, [gathered], (up_block,))
    raw = merge_forward(where, entering_states, bypass_states, gathered, r)

    rest = pack[:, 3 * r].astype(f32)
    count = pack.shape[0]
    vec = rest[:, : 7 * d // count].reshape(count, 7, d // count).transpose(1, 0, 2).reshape(7, d)
    vec = jnp.pad(vec, ((0, 1), (0, 0)))
    hidden_add = rest[:, 7 * d // count : 7 * d // count + 2 * half // count].reshape(2, 1, half)
    alive = lax.dynamic_index_in_dim(occupancy_mask, x, keepdims=True).astype(f32)

    merged, first, projected = project_forward(where, raw, vec, gathered, r, col)
    up_other, projected = gate(where, [swap(up_block, "x"), projected], ())
    up_away = [swap(up_block, "c"), swap(up_other, "c")]
    attended, logs = attention_forward(where, projected)
    *up_away, attended, logs = gate(where, up_away + [attended, logs], ())
    expand_pieces = ((up_block, up_away[0]), (up_other, up_away[1]))
    after_attn, second = result_forward(where, attended, merged, vec, gathered, r, col)
    bias = lax.dynamic_index_in_dim(hidden_add, x, keepdims=False)
    other_bias = lax.dynamic_index_in_dim(hidden_add, 1 - x, keepdims=False)
    active, slope = [None, None], [None, None]
    active[0], slope[0] = expand_forward(where, second, bias, expand_pieces[0])
    active[1], slope[1] = expand_forward(where, second, other_bias, expand_pieces[1])
    block_out, upstream, down_bias, energy = contract_forward(
        where, alive, active, after_attn, mentor_states, vec, down
    )

    def feed(x_rel):
        return feed_backward(
            where, upstream, second, active[x_rel], slope[x_rel], down, expand_pieces[x_rel], x_rel
        )

    none2, none3 = (None,) * 2, (None,) * 3
    by_lo = [(f32, (None, (4, 0))), (bf16, (None, (4, 1)))]
    by_hi = [(f32, ((3, 0),)), (bf16, ((3, 1),))]

    gs1, e1, e1s, d1, d1s, hb1 = feed(1)
    e1c, d1c = swap(e1s, "c"), swap(d1s, "c")
    gs0, e0, e0s, d0, d0s, hb0 = feed(0)
    e1x, d1y, gs0, e0s, d0s = fold(
        where,
        [
            ([[(e1, none3), (e1c, none3)]], [(bf16, ())]),
            ([[(d1, (1,) + none2), (d1c, (1,) + none2)]], [(bf16, ())]),
        ],
        (gs0, e0s, d0s),
    )
    e1x, d1y, e0c, d0c = swap(e1x, "x"), swap(d1y, "y"), swap(e0s, "c"), swap(d0s, "c")
    grad_after, branch, sums_two = norm_backward(
        where, after_attn, upstream, vec, 4, [gs0, gs1], (down_bias, energy, alive, hb0, hb1)
    )
    parcel = lax.all_gather(sums_two, everyone, axis=0, tiled=False)
    d0y, branch = fold(
        where, [([[(d0, (1,) + none2), (d0c, (1,) + none2)]], [(bf16, ())])], (branch,), (e0c,)
    )
    d0y = swap(d0y, "y")
    grad_attended, o0, o1 = result_backward(where, branch, attended, gathered, r, col)

    def attend(part, grads):
        return attention_backward(where, projected, attended, logs, grad_attended, part, 2, grads)

    grads = attend(0, None)
    e_far, d_far, grads = fold(
        where,
        [
            ([[(a, (1,) + none2) for a in (e0, e0c, e1x)]], [(bf16, ())]),
            ([[(d1, (0,) + none2), (d1c, (0,) + none2), (d1y, none2)]], [(bf16, ())]),
        ],
        (grads,),
        (d0y,),
    )
    e_far, d_far = swap(e_far, "y"), swap(d_far, "x")
    grads = attend(1, grads)
    front = (0,) + none2
    ends, ends_z, grads = fold(
        where,
        [
            (
                [
                    [(e0, front), (e0c, front), (e1x, front), (e_far, none2)],
                    [(d0, front), (d0c, front), (d0y, none2), (d_far, none2)],
                ],
                by_lo,
            )
        ],
        (grads,),
        (parcel,),
    )
    ends_z = swap_line(ends_z, 1)
    p0, p1, vo0, vo1 = project_weight(where, first, grads, (o0, o1), r, col)
    qk_c, vo_c = swap(p1, "c"), swap(vo1, "c")
    grad_first = project_backward(where, grads, gathered, r, col)
    qk_x, vo_y, ends, ends_z, grad_first = fold(
        where,
        [
            ([[(a, (None, 1) + none3) for a in (p0, qk_c)]], [(bf16, ())]),
            ([[(a, (None, None, 1) + none2) for a in (vo0, vo_c)]], [(bf16, ())]),
            ([[(a, (None,)) for a in (ends, ends_z)]], by_hi),
        ],
        (grad_first,),
    )
    qk_x, vo_y, ends_z = swap(qk_x, "x"), swap(vo_y, "y"), swap_line(ends_z, 2)
    merge_grad, three = norm_backward(where, merged, grad_after, vec, 1, [grad_first], last=True)
    m0, m1 = merge_weight(where, entering_states, bypass_states, merge_grad, r)
    three_c = swap(three, "c")
    ends, qk_y, vo_x, three, merge_grad, m1 = fold(
        where,
        [
            ([[(a, ()) for a in (ends, ends_z)]], [(f32, ())]),
            ([[(a, (None, 0, 1) + none2) for a in (p0, qk_c)] + [(qk_x, (None, 1) + none2)]], [(bf16, ())]),
            ([[(a, (None, 1, 0) + none2) for a in (vo0, vo_c)] + [(vo_y, (None, 1) + none2)]], [(bf16, ())]),
            ([[(three, ()), (three_c, ())]], [(f32, ())]),
        ],
        (merge_grad, m1),
    )
    qk_y, vo_x, m_c, three_x = swap(qk_y, "y"), swap(vo_x, "x"), swap(m1, "c"), swap(three, "x")
    grad_tokens, grad_shortcut = merge_backward(where, merge_grad, gathered, r, ())
    four_pieces = [
        [(a, (i, 0, 0) + none2) for a in (p0, qk_c)] + [(qk_x, (i, 0) + none2), (qk_y, (i,) + none2)]
        for i in BITS
    ] + [
        [(a, (i, 0, 0) + none2) for a in (vo0, vo_c)] + [(vo_y, (i, 0) + none2), (vo_x, (i,) + none2)]
        for i in BITS
    ]
    four, four_z, l_x, r_y, three, grad_tokens = fold(
        where,
        [
            (four_pieces, by_lo),
            ([[(a, (0, 1) + none3) for a in (m0, m_c)]], [(bf16, ())]),
            ([[(a, (1, None, 1) + none2) for a in (m0, m_c)]], [(bf16, ())]),
            ([[(three, ()), (three_x, ())]], [(f32, ())]),
        ],
        (grad_tokens,),
    )
    l_x, r_y, three_y, four_z = swap(l_x, "x"), swap(r_y, "y"), swap(three, "y"), swap_line(four_z, 1)
    l_y, r_x, three, four, four_z = fold(
        where,
        [
            ([[(a, (0, 0, 1) + none2) for a in (m0, m_c)] + [(l_x, (1,) + none2)]], [(bf16, ())]),
            ([[(a, (1, 1, 0) + none2) for a in (m0, m_c)] + [(r_y, (1,) + none2)]], [(bf16, ())]),
            ([[(three, ()), (three_y, ())]], [(f32, ())]),
            ([[(a, (None,)) for a in (four, four_z)]], by_hi),
        ],
    )
    l_y, r_x, three_z, four_z = swap(l_y, "y"), swap(r_x, "x"), swap_line(three, 1), swap_line(four_z, 2)
    grad_merge, merge_z, four, three = fold(
        where,
        [
            (
                [
                    [(a, (0, 0, 0) + none2) for a in (m0, m_c)] + [(l_x, (0,) + none2), (l_y, none2)],
                    [(a, (1, 0, 0) + none2) for a in (m0, m_c)] + [(r_y, (0,) + none2), (r_x, none2)],
                ],
                by_lo,
            ),
            ([[(a, ()) for a in (four, four_z)]], [(f32, ())]),
            ([[(a, ()) for a in (three, three_z)]], [(f32, ())]),
        ],
    )
    merge_z, three_z = swap_line(merge_z, 1), swap_line(three, 2)
    grad_merge, merge_z, three = fold(
        where,
        [
            ([[(a, (None,)) for a in (grad_merge, merge_z)]], by_hi),
            ([[(a, ()) for a in (three, three_z)]], [(f32, ())]),
        ],
    )
    (grad_merge,) = fold(where, [([[(a, ()) for a in (grad_merge, swap_line(merge_z, 2))]], [(f32, ())])])
    grad_expand, grad_contract = ends[:, :half], ends[:, half:]
    grad_query, grad_key, grad_value, grad_result = (four[:, i * col : (i + 1) * col] for i in range(4))
    own = jnp.sum(parcel, axis=0)

    share = d // count
    three = lax.dynamic_slice_in_dim(three, device * share, share, 1)
    four_rows = lax.dynamic_slice_in_dim(own[:4], device * share, share, 1)
    loss_value = own[4, 0] / (own[5, 0] * d)
    share = 2 * half // count
    hidden_row = lax.dynamic_slice_in_dim(own[8:12].reshape(-1), device * share, share, 0)
    sums = (three[2], three[0], three[1], four_rows[2], four_rows[0], four_rows[1], four_rows[3], hidden_row)
    return (
        block_out,
        loss_value,
        grad_tokens,
        grad_shortcut,
        grad_merge,
        sums[0],
        sums[1],
        sums[2],
        grad_query,
        grad_key,
        grad_value,
        grad_result.T,
        sums[3],
        sums[4],
        sums[5],
        grad_expand,
        sums[7],
        grad_contract.T,
        sums[6],
    )


ARGUMENTS = (
    ("ft", None),
    ("ft", None),
    ("ft", None),
    ("f",),
    ("ft", None),
    ("ft",),
    ("ft",),
    ("ft",),
    ("f", "t"),
    ("f", "t"),
    ("f", "t"),
    ("t", "f"),
    ("ft",),
    ("ft",),
    ("ft",),
    ("f", "t"),
    ("ft",),
    ("t", "f"),
    ("ft",),
)
RESULTS = (
    ("ft", None),
    (),
    ("ft", None),
    ("ft", None),
    ("ft", None),
    ("ft",),
    ("ft",),
    ("ft",),
    ("f", "t"),
    ("f", "t"),
    ("f", "t"),
    ("t", "f"),
    ("ft",),
    ("ft",),
    ("ft",),
    ("f", "t"),
    ("ft",),
    ("t", "f"),
    ("ft",),
)


def solution(mesh):
    def whole(*args):
        rows = args[0].shape[0] // mesh.size
        if rows == SEQ_LEN and dict(mesh.shape) == {"fsdp": 16, "tp": 2}:
            plan = one_sequence_plan
            use = jax.sharding.Mesh(mesh.devices.reshape(4, 2, 2, 2), ("z", "y", "c", "x"))
            names = {"f": ("z", "y", "c"), "t": ("x",), "ft": ("z", "y", "c", "x")}
        else:
            plan = per_device_split
            use = mesh
            names = {"f": ("fsdp",), "t": ("tp",), "ft": ("fsdp", "tp")}

        def place(entry):
            return P(*(None if e is None else names[e] for e in entry))

        return jax.shard_map(
            plan,
            mesh=use,
            in_specs=tuple(place(e) for e in ARGUMENTS),
            out_specs=tuple(place(e) for e in RESULTS),
            check_vma=False,
        )(*args)

    return whole
```

```python
import functools
import math

import jax
import jax.numpy as jnp
from jax import lax
from jax.experimental import pallas as pl
from jax.experimental.pallas import tpu as pltpu
from jax.sharding import PartitionSpec as P

D = 1024
HEADS = 16
SEQ_LEN = 1104


EPSILON = 1e-05


def layer_norm(value, gain, shift):
    centred = value - jnp.mean(value, axis=-1, keepdims=True)
    spread = jnp.mean(centred * centred, axis=-1, keepdims=True)
    return centred * lax.rsqrt(spread + EPSILON) * gain + shift


def contract_rows(left, right):
    return lax.dot_general(
        left, right, (((0,), (0,)), ((), ())), preferred_element_type=jnp.float32
    )


def contract_cols(left, right):
    return lax.dot_general(
        left, right, (((1,), (1,)), ((), ())), preferred_element_type=jnp.float32
    )


def attend_forward(queries, keys_all, values):
    scale = float(queries.shape[-1]) ** (-0.5)
    scores = (
        jnp.einsum("qhd,khd->hqk", queries, keys_all, preferred_element_type=jnp.float32) * scale
    )
    peak_score = jnp.max(scores, axis=-1, keepdims=True)
    raised = jnp.exp(scores - peak_score)
    row_total = jnp.sum(raised, axis=-1, keepdims=True)
    weights_low = (raised / row_total).astype(jnp.bfloat16)
    output = jnp.einsum("hqk,khd->qhd", weights_low, values, preferred_element_type=jnp.float32)
    return (output.astype(jnp.bfloat16), peak_score + jnp.log(row_total))


def attend_backward(queries, keys_all, values, summary, upstream):
    scale = float(queries.shape[-1]) ** (-0.5)
    scores = (
        jnp.einsum("qhd,khd->hqk", queries, keys_all, preferred_element_type=jnp.float32) * scale
    )
    probs_full = jnp.exp(scores - summary)
    grad_probs = jnp.einsum("qhd,khd->hqk", upstream, values, preferred_element_type=jnp.float32)
    grad_values = jnp.einsum(
        "hqk,qhd->khd",
        probs_full.astype(jnp.bfloat16),
        upstream,
        preferred_element_type=jnp.float32,
    )
    centre = jnp.sum(probs_full * grad_probs, axis=-1, keepdims=True)
    grad_scores = (probs_full * (grad_probs - centre)).astype(jnp.bfloat16)
    grad_queries = (
        jnp.einsum("hqk,khd->qhd", grad_scores, keys_all, preferred_element_type=jnp.float32)
        * scale
    )
    grad_keys = (
        jnp.einsum("hqk,qhd->khd", grad_scores, queries, preferred_element_type=jnp.float32) * scale
    )
    return (
        grad_queries.astype(jnp.bfloat16),
        grad_keys.astype(jnp.bfloat16),
        grad_values.astype(jnp.bfloat16),
    )


def gelu_exact(value):
    return jax.nn.gelu(value, approximate=False)


def per_device_split(
    entering_states,
    bypass_states,
    mentor_states,
    occupancy_mask,
    bypass_merge_matrix,
    bypass_merge_offset,
    mixer_layernorm_scale,
    mixer_layernorm_offset,
    asking_map_matrix,
    lookup_map_matrix,
    content_map_matrix,
    mixer_result_matrix,
    mixer_result_offset,
    perceptron_layernorm_scale,
    perceptron_layernorm_offset,
    expand_layer_matrix,
    expand_layer_offset,
    contract_layer_matrix,
    contract_layer_offset,
):
    rows = entering_states.shape[0]
    width = D // HEADS
    position = lax.axis_index("tp")
    (
        merge_full,
        merge_add,
        gain_one,
        shift_one,
        output_add,
        gain_two,
        shift_two,
        hidden_add,
        down_add,
    ) = (
        lax.all_gather(bypass_merge_matrix, ("fsdp", "tp"), axis=0, tiled=True),
        lax.all_gather(bypass_merge_offset, ("fsdp", "tp"), axis=0, tiled=True),
        lax.all_gather(mixer_layernorm_scale, ("fsdp", "tp"), axis=0, tiled=True),
        lax.all_gather(mixer_layernorm_offset, ("fsdp", "tp"), axis=0, tiled=True),
        lax.all_gather(mixer_result_offset, ("fsdp", "tp"), axis=0, tiled=True),
        lax.all_gather(perceptron_layernorm_scale, ("fsdp", "tp"), axis=0, tiled=True),
        lax.all_gather(perceptron_layernorm_offset, ("fsdp", "tp"), axis=0, tiled=True),
        lax.all_gather(expand_layer_offset, ("fsdp", "tp"), axis=0, tiled=True),
        lax.all_gather(contract_layer_offset, ("fsdp", "tp"), axis=0, tiled=True),
    )
    query_full, key_full, value_full, output_full, hidden_full, down_full = (
        lax.all_gather(asking_map_matrix, "fsdp", axis=0, tiled=True),
        lax.all_gather(lookup_map_matrix, "fsdp", axis=0, tiled=True),
        lax.all_gather(content_map_matrix, "fsdp", axis=0, tiled=True),
        lax.all_gather(mixer_result_matrix, "fsdp", axis=1, tiled=True),
        lax.all_gather(expand_layer_matrix, "fsdp", axis=0, tiled=True),
        lax.all_gather(contract_layer_matrix, "fsdp", axis=1, tiled=True),
    )
    gain_one = gain_one.astype(jnp.float32)
    shift_one = shift_one.astype(jnp.float32)
    gain_two = gain_two.astype(jnp.float32)
    shift_two = shift_two.astype(jnp.float32)
    project = jnp.concatenate([query_full, key_full, value_full], axis=1)
    local_width = query_full.shape[1]
    local_heads = local_width // width
    local_hidden = hidden_full.shape[1]
    row_index = position * rows + jnp.arange(rows, dtype=jnp.int32)
    slot_of_row = row_index // SEQ_LEN
    series_place_total = occupancy_mask.shape[0]
    agreeing_lines = (
        slot_of_row[:, None] == jnp.arange(series_place_total, dtype=jnp.int32)[None, :]
    ).astype(jnp.float32)
    alive_tokens = jnp.sum(
        agreeing_lines * occupancy_mask.astype(jnp.float32)[None, :], axis=1, keepdims=True
    )
    joined = jnp.concatenate([entering_states, bypass_states], axis=1)
    merged = jnp.dot(joined, merge_full, preferred_element_type=jnp.float32) + merge_add.astype(
        jnp.float32
    )
    first = layer_norm(merged, gain_one, shift_one).astype(jnp.bfloat16)
    first_all = lax.all_gather(first, "tp", axis=0, tiled=True)
    group_rows = first_all.shape[0]
    slots = group_rows // SEQ_LEN
    projected = jnp.dot(first_all, project, preferred_element_type=jnp.float32).astype(jnp.bfloat16)
    shaped = projected.reshape(slots, SEQ_LEN, 3, local_heads, width)
    queries = shaped[:, :, 0]
    keys_all = shaped[:, :, 1]
    values = shaped[:, :, 2]
    attended, summary = lax.map(
        lambda item: attend_forward(item[0], item[1], item[2]), (queries, keys_all, values)
    )
    attended_flat = attended.reshape(group_rows, local_width)
    attention_term = jnp.dot(attended_flat, output_full, preferred_element_type=jnp.float32)
    after_attn = (
        merged
        + lax.psum_scatter(
            attention_term.astype(jnp.bfloat16), "tp", scatter_dimension=0, tiled=True
        ).astype(jnp.float32)
        + output_add.astype(jnp.float32)
    )
    second = layer_norm(after_attn, gain_two, shift_two).astype(jnp.bfloat16)
    second_all = lax.all_gather(second, "tp", axis=0, tiled=True)
    hidden_slice = lax.dynamic_slice_in_dim(
        hidden_add.astype(jnp.float32), position * local_hidden, local_hidden, 0
    )
    hidden = jnp.dot(second_all, hidden_full, preferred_element_type=jnp.float32) + hidden_slice
    active = gelu_exact(hidden).astype(jnp.bfloat16)
    feed_term = jnp.dot(active, down_full, preferred_element_type=jnp.float32)
    final = (
        after_attn
        + lax.psum_scatter(
            feed_term.astype(jnp.bfloat16), "tp", scatter_dimension=0, tiled=True
        ).astype(jnp.float32)
        + down_add.astype(jnp.float32)
    )
    missing = final - mentor_states.astype(jnp.float32)
    grad_final = alive_tokens * missing
    block_out = (final * alive_tokens).astype(jnp.bfloat16)
    energy, counted = lax.psum(
        (0.5 * jnp.sum(grad_final * missing), jnp.sum(alive_tokens)), ("fsdp", "tp")
    )
    loss_value = energy / (counted * D)
    grad_down_bias = jnp.sum(grad_final, axis=0)
    upstream = grad_final.astype(jnp.bfloat16)
    upstream_all = lax.all_gather(upstream, "tp", axis=0, tiled=True)
    grad_down = contract_rows(active, upstream_all)
    grad_active = contract_cols(upstream_all, down_full)
    gelu_value, gelu_pull = jax.vjp(gelu_exact, hidden)
    grad_hidden = gelu_pull(grad_active)[0].astype(jnp.bfloat16)
    grad_hidden_local = jnp.sum(grad_hidden.astype(jnp.float32), axis=0)
    grad_hidden_weight = contract_rows(second_all, grad_hidden)
    feed_back_term = contract_cols(grad_hidden, hidden_full)
    grad_second = lax.psum_scatter(
        feed_back_term.astype(jnp.bfloat16), "tp", scatter_dimension=0, tiled=True
    ).astype(jnp.float32)
    hidden_bias_term = lax.dynamic_update_slice_in_dim(
        jnp.zeros((hidden_add.shape[0],), jnp.float32),
        grad_hidden_local,
        position * local_hidden,
        0,
    )
    norm_value, second_pull = jax.vjp(layer_norm, after_attn, gain_two, shift_two)
    back_after, grad_gain_two, grad_shift_two = second_pull(grad_second)
    grad_after = grad_final + back_after
    grad_output_bias = jnp.sum(grad_after, axis=0)
    branch_all = lax.all_gather(grad_after.astype(jnp.bfloat16), "tp", axis=0, tiled=True)
    grad_output_weight = contract_rows(attended_flat, branch_all)
    grad_attended = contract_cols(branch_all, output_full).astype(jnp.bfloat16)
    upstream_heads = grad_attended.reshape(slots, SEQ_LEN, local_heads, width)
    grad_q_heads, grad_k_heads, grad_v_heads = lax.map(
        lambda item: attend_backward(item[0], item[1], item[2], item[3], item[4]),
        (queries, keys_all, values, summary, upstream_heads),
    )
    grad_projected = jnp.stack([grad_q_heads, grad_k_heads, grad_v_heads], axis=2).reshape(
        group_rows, 3 * local_width
    )
    grad_project = contract_rows(first_all, grad_projected)
    attention_back_term = contract_cols(grad_projected, project)
    grad_first = lax.psum_scatter(
        attention_back_term.astype(jnp.bfloat16), "tp", scatter_dimension=0, tiled=True
    ).astype(jnp.float32)
    first_value, first_pull = jax.vjp(layer_norm, merged, gain_one, shift_one)
    back_merged, grad_gain_one, grad_shift_one = first_pull(grad_first)
    grad_merged = grad_after + back_merged
    grad_merge_bias = jnp.sum(grad_merged, axis=0)
    merge_grad = grad_merged.astype(jnp.bfloat16)
    grad_merge_weight = contract_rows(joined, merge_grad)
    grad_joined = contract_cols(merge_grad, merge_full)
    model_width = entering_states.shape[1]
    grad_tokens = grad_joined[:, :model_width]
    grad_shortcut = grad_joined[:, model_width:]
    grad_query, grad_key, grad_value, grad_output, grad_hidden_full, grad_down_full = (
        lax.psum_scatter(
            grad_project[:, :local_width].astype(jnp.bfloat16),
            "fsdp",
            scatter_dimension=0,
            tiled=True,
        ).astype(jnp.float32),
        lax.psum_scatter(
            grad_project[:, local_width : 2 * local_width].astype(jnp.bfloat16),
            "fsdp",
            scatter_dimension=0,
            tiled=True,
        ).astype(jnp.float32),
        lax.psum_scatter(
            grad_project[:, 2 * local_width :].astype(jnp.bfloat16),
            "fsdp",
            scatter_dimension=0,
            tiled=True,
        ).astype(jnp.float32),
        lax.psum_scatter(
            grad_output_weight.astype(jnp.bfloat16), "fsdp", scatter_dimension=1, tiled=True
        ).astype(jnp.float32),
        lax.psum_scatter(
            grad_hidden_weight.astype(jnp.bfloat16), "fsdp", scatter_dimension=0, tiled=True
        ).astype(jnp.float32),
        lax.psum_scatter(
            grad_down.astype(jnp.bfloat16), "fsdp", scatter_dimension=1, tiled=True
        ).astype(jnp.float32),
    )
    (
        merge_weight_sum,
        merge_bias_sum,
        gain_one_sum,
        shift_one_sum,
        output_bias_sum,
        gain_two_sum,
        shift_two_sum,
        hidden_bias_sum,
        down_bias_sum,
    ) = (
        lax.psum_scatter(grad_merge_weight, ("fsdp", "tp"), scatter_dimension=0, tiled=True),
        lax.psum_scatter(grad_merge_bias, ("fsdp", "tp"), scatter_dimension=0, tiled=True),
        lax.psum_scatter(grad_gain_one, ("fsdp", "tp"), scatter_dimension=0, tiled=True),
        lax.psum_scatter(grad_shift_one, ("fsdp", "tp"), scatter_dimension=0, tiled=True),
        lax.psum_scatter(grad_output_bias, ("fsdp", "tp"), scatter_dimension=0, tiled=True),
        lax.psum_scatter(grad_gain_two, ("fsdp", "tp"), scatter_dimension=0, tiled=True),
        lax.psum_scatter(grad_shift_two, ("fsdp", "tp"), scatter_dimension=0, tiled=True),
        lax.psum_scatter(hidden_bias_term, ("fsdp", "tp"), scatter_dimension=0, tiled=True),
        lax.psum_scatter(grad_down_bias, ("fsdp", "tp"), scatter_dimension=0, tiled=True),
    )
    return (
        block_out,
        loss_value,
        grad_tokens,
        grad_shortcut,
        merge_weight_sum,
        merge_bias_sum,
        gain_one_sum,
        shift_one_sum,
        grad_query,
        grad_key,
        grad_value,
        grad_output,
        output_bias_sum,
        gain_two_sum,
        shift_two_sum,
        grad_hidden_full,
        hidden_bias_sum,
        grad_down_full,
        down_bias_sum,
    )


LOG2E = math.log2(math.e)
PAIR = 128
CHUNK = 368


def nn(a, b):
    return lax.dot_general(a, b, (((1,), (0,)), ((), ())), preferred_element_type=jnp.float32)


def nt(a, b):
    return lax.dot_general(a, b, (((1,), (1,)), ((), ())), preferred_element_type=jnp.float32)


def tn(a, b):
    return lax.dot_general(a, b, (((0,), (0,)), ((), ())), preferred_element_type=jnp.float32)


def vmem():
    return pltpu.CompilerParams(vmem_limit_bytes=60 * 2**20)


def cuts(count, size):
    edges = [i * size for i in range(count // size)] + [count]
    return [slice(a, b) for a, b in zip(edges, edges[1:])]


def attention_forward_kernel(q_ref, k_ref, v_ref, o_ref, l_ref):
    count = q_ref.shape[0]
    scale = (PAIR // 2) ** -0.5 * LOG2E
    low = lax.broadcasted_iota(jnp.int32, (1, PAIR), 1) < PAIR // 2
    keys, values = k_ref[...], v_ref[...]
    zero = jnp.zeros_like(keys)
    heads = (jnp.where(low, keys, zero), jnp.where(low, zero, keys))
    wide = jnp.concatenate([values, jnp.ones_like(values)], axis=1)
    for part in cuts(count, 512):
        queries = q_ref[part, :]
        outs, sums = [], []
        for scores in [nt(queries, head) for head in heads]:
            peak = jnp.max(scores, axis=1, keepdims=True) * scale
            raised = jnp.exp2(scores * scale - peak).astype(jnp.bfloat16)
            both = nn(raised, wide)
            total = both[:, PAIR:]
            outs.append(both[:, :PAIR] / total)
            sums.append(peak + jnp.log2(total))
        o_ref[part, :] = jnp.where(low, outs[0], outs[1]).astype(jnp.bfloat16)
        l_ref[part, :] = jnp.where(low, sums[0], sums[1])


def attention_backward_kernel(q_ref, k_ref, v_ref, o_ref, l_ref, u_ref, out_ref, total_ref):
    count = q_ref.shape[0]
    plain = (PAIR // 2) ** -0.5
    scale = plain * LOG2E
    low = lax.broadcasted_iota(jnp.int32, (1, PAIR), 1) < PAIR // 2
    queries, upstream = q_ref[...], u_ref[...]
    product = upstream.astype(jnp.float32) * o_ref[...].astype(jnp.float32)
    left = jnp.sum(jnp.where(low, product, 0.0), axis=1, keepdims=True)
    right = jnp.sum(jnp.where(low, 0.0, product), axis=1, keepdims=True)
    centres = jnp.transpose(jnp.where(low, left, right))
    logs = jnp.transpose(l_ref[...])
    for head in range(2):

        def own(value):
            zero = jnp.zeros_like(value)
            return jnp.where(low, value, zero) if head == 0 else jnp.where(low, zero, value)

        row = head * (PAIR // 2)
        own_queries, own_upstream = own(queries), own(upstream)
        log_row, centre = logs[row : row + 1, :], centres[row : row + 1, :]
        for part in cuts(count, 256):
            keys, values = k_ref[part, :], v_ref[part, :]
            probs = jnp.exp2(nt(keys, own_queries) * scale - log_row)
            slopes = (probs * (nt(values, own_upstream) - centre)).astype(jnp.bfloat16)
            grad_v = nn(probs.astype(jnp.bfloat16), own_upstream).astype(jnp.bfloat16)
            grad_k = (nn(slopes, own_queries) * plain).astype(jnp.bfloat16)
            grad_q = tn(slopes, own(keys))
            if head == 0:
                out_ref[1, part, :] = grad_k
                out_ref[2, part, :] = grad_v
            else:
                out_ref[1, part, :] = jnp.where(low, out_ref[1, part, :], grad_k)
                out_ref[2, part, :] = jnp.where(low, out_ref[2, part, :], grad_v)
            if head == 0 and part.start == 0:
                total_ref[...] = grad_q
            else:
                total_ref[...] += grad_q
    out_ref[0] = (total_ref[...] * plain).astype(jnp.bfloat16)


def gelu_both(value):
    t = 1.0 / (1.0 + 0.3275911 * math.sqrt(0.5) * jnp.abs(value))
    bell = jnp.exp2(value * value * (-0.5 * LOG2E))
    poly = 0.5 * 1.061405429 * t - 0.5 * 1.453152027
    poly = poly * t + 0.5 * 1.421413741
    poly = poly * t - 0.5 * 0.284496736
    poly = poly * t + 0.5 * 0.254829592
    rest = poly * t * bell
    below = jnp.where(value >= 0, 1.0 - rest, rest)
    return value * below, below + value * bell * (1.0 / math.sqrt(2.0 * math.pi))


def normalized(value):
    centred = value - jnp.mean(value, axis=-1, keepdims=True)
    spread = jnp.mean(centred * centred, axis=-1, keepdims=True)
    inverse = lax.rsqrt(spread + EPSILON)
    return centred * inverse, inverse


def place_at(where_ref, hi, lo, y_rel, c_rel, rows):
    y = jnp.bitwise_xor(where_ref[0], y_rel)
    c = jnp.bitwise_xor(where_ref[1], c_rel)
    return pl.multiple_of(((hi * 2 + lo) * 4 + y * 2 + c) * rows, rows)


BITS = (0, 1)


def once(block, index):
    return pl.BlockSpec(block, index, pipeline_mode=pl.Buffered(1))


def call(kernel, grid, where, ins, outs, scratch, name, after=(), aliases=(), flops=0):
    first, count = len(ins), len(after)

    def ordered_kernel(where_ref, *refs):
        kernel(where_ref, *refs[:first], *refs[first + count :])

    anywhere = pl.BlockSpec(memory_space=pl.ANY)
    return pl.pallas_call(
        ordered_kernel,
        grid_spec=pltpu.PrefetchScalarGridSpec(
            num_scalar_prefetch=1,
            grid=grid,
            in_specs=[spec for _, spec in ins] + [anywhere] * count,
            out_specs=[spec for _, _, spec in outs],
            scratch_shapes=scratch,
        ),
        out_shape=[jax.ShapeDtypeStruct(s, t) for s, t, _ in outs],
        input_output_aliases={1 + i: o for i, o in aliases},
        compiler_params=vmem(),
        cost_estimate=pl.CostEstimate(flops=flops, bytes_accessed=0, transcendentals=0),
        name=name,
    )(where, *(x for x, _ in ins), *after)


def resident(shape):
    return once(shape, lambda *_: (0,) * len(shape))


def attention_forward(where, projected):
    rows, columns = projected.shape
    pairs = columns // 3 // PAIR

    def block(offset):
        return pl.BlockSpec((rows, PAIR), lambda j, s: (0, offset + j))

    return call(
        lambda where_ref, *refs: attention_forward_kernel(*refs),
        (pairs,),
        where,
        [(projected, block(0)), (projected, block(pairs)), (projected, block(2 * pairs))],
        [
            ((rows, pairs * PAIR), jnp.bfloat16, block(0)),
            ((rows, pairs * PAIR), jnp.float32, block(0)),
        ],
        [],
        "attention_forward",
    )


def attention_backward(where, projected, attended, logs, upstream, index, of, grads):
    rows, columns = projected.shape
    pairs = columns // 3 // PAIR
    here = index * (pairs // of)

    def block(offset):
        return pl.BlockSpec((rows, PAIR), lambda j, s: (0, offset + here + j))

    ins = [
        (projected, block(0)),
        (projected, block(pairs)),
        (projected, block(2 * pairs)),
        (attended, block(0)),
        (logs, block(0)),
        (upstream, block(0)),
    ]
    aliases = ()
    if grads is not None:
        ins.append((grads, pl.BlockSpec(memory_space=pl.ANY)))
        aliases = ((6, 0),)

    def kernel(where_ref, *refs):
        attention_backward_kernel(*refs[:6], *refs[-2:])

    return call(
        kernel,
        (pairs // of,),
        where,
        ins,
        [((3, rows, pairs * PAIR), jnp.bfloat16, pl.BlockSpec((3, rows, PAIR), lambda j, s: (0, 0, here + j)))],
        [pltpu.VMEM((rows, PAIR), jnp.float32)],
        "attention_backward",
        (),
        aliases,
    )[0]


def gate(where, values, after):
    anywhere = pl.BlockSpec(memory_space=pl.ANY)
    return call(
        lambda *refs: None,
        (1,),
        where,
        [(v, anywhere) for v in values],
        [(v.shape, v.dtype, anywhere) for v in values],
        [],
        "gate",
        after,
        tuple((i, i) for i in range(len(values))),
    )


def fold_kernel(jobs, carried, waited, where, *refs):
    sources = iter(refs)
    total = sum(len(parts) for pieces, _ in jobs for parts in pieces)
    targets = iter(refs[total + carried + waited :])
    for pieces, results in jobs:
        held = [[next(sources) for _ in parts] for parts in pieces]
        for kind, select in results:
            out, begin = next(targets), 0
            at = tuple(slice(None) if t is None else jnp.bitwise_xor(where[t[0]], t[1]) for t in select)
            for parts in held:
                value = parts[0][at + (Ellipsis,)].astype(jnp.float32)
                for part in parts[1:]:
                    value = value + part[at + (Ellipsis,)].astype(jnp.float32)
                end = begin + value.shape[-1]
                out[..., begin:end] = value.astype(out.dtype)
                begin = end


def fold(where, jobs, carry=(), after=(), flops=0):
    ins, outs, plan = [], [], []
    for pieces, results in jobs:
        columns = 0
        for parts in pieces:
            for array, lead in parts:
                fixed = lead + (None, None)
                block = tuple(n if t is None else pl.squeezed for n, t in zip(array.shape, fixed))
                index = tuple(0 if t is None else t for t in fixed)
                ins.append((array, once(block, lambda i, s, index=index: index)))
            columns += array.shape[-1]
        shape = tuple(n for n, t in zip(array.shape, fixed) if t is None)[:-1] + (columns,)
        for kind, select in results:
            made = tuple(n for n, t in zip(shape, select) if t is None) + shape[len(select) :]
            outs.append((made, kind, resident(made)))
        plan.append((pieces, results))
    anywhere = pl.BlockSpec(memory_space=pl.ANY)
    count, made = len(ins), len(outs)
    ins += [(c, anywhere) for c in carry]
    outs += [(c.shape, c.dtype, anywhere) for c in carry]
    return call(
        functools.partial(fold_kernel, plan, len(carry), 0),
        (1,),
        where,
        ins,
        outs,
        [],
        "fold",
        after,
        tuple((count + i, made + i) for i in range(len(carry))),
        flops,
    )


def pile_kernel(slot, axis, where, mine, other, *outs):
    here = 0 if slot is None else where[slot]
    there = 1 - here
    lead = outs[0].shape[:axis]
    rows = outs[0].shape[-2]
    for number, out in enumerate(outs):
        part = slice(number * rows, (number + 1) * rows)
        for i in range(math.prod(lead)):
            at = ()
            for size in reversed(lead):
                at = (i % size,) + at
                i //= size
            out[at + (here,)] = mine[at + (Ellipsis, part, slice(None))]
            out[at + (there,)] = other[at + (Ellipsis, part, slice(None))]


def pile(where, slot, mine, other, axis, parts=1):
    shape = mine.shape[:axis] + (2,) + mine.shape[axis:-2] + (mine.shape[-2] // parts, mine.shape[-1])
    made = call(
        functools.partial(pile_kernel, slot, axis),
        (1,),
        where,
        [(mine, resident(mine.shape)), (other, resident(mine.shape))],
        [(shape, mine.dtype, resident(shape))] * parts,
        [],
        "pile",
    )
    return made if parts > 1 else made[0]


def merge_kernel(where, ent, byp, full, out):
    half = ent.shape[1]
    weight = full[...].reshape(2 * half, half)
    out[...] = nn(ent[...], weight[:half, :]) + nn(byp[...], weight[half:, :])


def merge_forward(where, ent, byp, gathered, r):
    rows, d = ent.shape
    part = pl.BlockSpec((CHUNK, d), lambda i, w: (i, 0))
    return call(
        merge_kernel,
        (rows // CHUNK,),
        where,
        [(ent, part), (byp, part), (gathered, resident((2, 2, 2, 2, 2, r, d)))],
        [((rows, d), jnp.float32, part)],
        [],
        "merge_forward",
    )[0]


def weight_block(r, col, number):
    def index(*args):
        which, x_rel = number(*args[:-1])
        return 0, 0, 0, 0, jnp.bitwise_xor(x_rel, args[-1][2]), 1 + which // 2, which % 2

    return pl.BlockSpec((2, 2, 2, 2, pl.squeezed, r, col), index)


def project_kernel(where, raw, vec, weight, merged, first, out):
    @pl.when((pl.program_id(0) == 0) & (pl.program_id(1) == 0))
    def _():
        for start in range(0, raw.shape[0], CHUNK):
            part = slice(start, start + CHUNK)
            total = raw[part, :] + vec[0:1, :]
            merged[part, :] = total
            norm, _ = normalized(total)
            first[part, :] = (norm * vec[1:2, :] + vec[2:3, :]).astype(jnp.bfloat16)

    out[...] = nn(first[...], weight[...].reshape(first.shape[1], -1)).astype(jnp.bfloat16)


def project_forward(where, raw, vec, gathered, r, col):
    rows, d = raw.shape
    f32, bf16 = jnp.float32, jnp.bfloat16
    return call(
        project_kernel,
        (3, 2),
        where,
        [
            (raw, resident((rows, d))),
            (vec, resident(vec.shape)),
            (gathered, weight_block(r, col, lambda w, x: (w, x))),
        ],
        [
            ((rows, d), f32, resident((rows, d))),
            ((rows, d), bf16, resident((rows, d))),
            ((rows, 6 * col), bf16, pl.BlockSpec((rows, col), lambda w, x, s: (0, w * 2 + x))),
        ],
        [],
        "project_forward",
    )


def result_kernel(where, attended, merged, vec, weight, after, second, total):
    step = pl.program_id(0)
    natural = weight[...].reshape(after.shape[1], -1)

    @pl.when(step == 0)
    def _():
        total[...] = nt(attended[...], natural)

    @pl.when(step == 1)
    def _():
        for start in range(0, after.shape[0], CHUNK):
            here = slice(start, start + CHUNK)
            part = nt(attended[here, :], natural)
            value = merged[here, :] + vec[3:4, :] + (total[here, :] + part)
            after[here, :] = value
            norm, _ = normalized(value)
            second[here, :] = (norm * vec[4:5, :] + vec[5:6, :]).astype(jnp.bfloat16)


def result_forward(where, attended, merged, vec, gathered, r, col):
    rows, d = merged.shape
    return call(
        result_kernel,
        (2,),
        where,
        [
            (attended, pl.BlockSpec((rows, col), lambda x, s: (0, x))),
            (merged, resident((rows, d))),
            (vec, resident(vec.shape)),
            (gathered, weight_block(r, col, lambda x: (3, x))),
        ],
        [
            ((rows, d), jnp.float32, resident((rows, d))),
            ((rows, d), jnp.bfloat16, resident((rows, d))),
        ],
        [pltpu.VMEM((rows, d), jnp.float32)],
        "result_forward",
    )


def fill_by_core(where, full, refs, rows):
    for c_rel, ref in enumerate(refs):
        for y_rel in BITS:
            for hi in BITS:
                for lo in BITS:
                    at = place_at(where, hi, lo, y_rel, c_rel, rows)
                    full[pl.ds(at, rows), :] = ref[y_rel, hi, lo]


def spill_by_core(where, full, refs, rows):
    for c_rel, ref in enumerate(refs):
        for y_rel in BITS:
            for hi in BITS:
                for lo in BITS:
                    at = place_at(where, hi, lo, y_rel, c_rel, rows)
                    ref[y_rel, hi, lo] = full[pl.ds(at, rows), :]


def expand_kernel(rows, where, second, bias, w0, w1, w2, w3, active, slope, full):
    @pl.when(pl.program_id(0) == 0)
    def _():
        fill_by_core(where, full, (w0, w1), rows)

    @pl.when(pl.program_id(0) == 1)
    def _():
        fill_by_core(where, full, (w2, w3), rows)

    for start in range(0, second.shape[0], CHUNK):
        part = slice(start, start + CHUNK)
        hidden = nn(second[part, :], full[...]) + bias[...]
        value, rate = gelu_both(hidden)
        active[part, :] = value.astype(jnp.bfloat16)
        slope[part, :] = rate.astype(jnp.bfloat16)


def expand_forward(where, second, bias, pieces, block=512):
    rows, d = second.shape
    *_, r, half = pieces[0][0].shape
    steps = half // block
    near = pl.BlockSpec((2, 2, 2, r, block), lambda x, j, s: (0, 0, 0, 0, jnp.where(x == 0, j, steps - 1)))
    far = pl.BlockSpec((2, 2, 2, r, block), lambda x, j, s: (0, 0, 0, 0, jnp.where(x == 0, 0, j)))
    out = pl.BlockSpec((pl.squeezed, rows, block), lambda x, j, s: (x, 0, j))
    return call(
        functools.partial(expand_kernel, r),
        (2, steps),
        where,
        [
            (second, resident((rows, d))),
            (bias, pl.BlockSpec((pl.squeezed, 1, block), lambda x, j, s: (jnp.bitwise_xor(x, s[2]), 0, j))),
        ]
        + [(p, near) for p in pieces[0]]
        + [(p, far) for p in pieces[1]],
        [((2, rows, half), jnp.bfloat16, out)] * 2,
        [pltpu.VMEM((d, block), jnp.bfloat16)],
        "expand_forward",
    )


def contract_kernel(steps, where, alive, active, after, mentor, vec, weight, out, upstream, sums, energy, total):
    step = pl.program_id(0)
    count, d = after.shape
    full = weight[...].reshape(d, -1)

    @pl.when(step == 0)
    def _():
        total[...] = nt(active[...], full)

    @pl.when((step > 0) & (step < 2 * steps - 1))
    def _():
        total[...] += nt(active[...], full)

    @pl.when(step == 2 * steps - 1)
    def _():
        live = alive[0]
        column, squares = 0.0, 0.0
        for start in range(0, count, CHUNK):
            part = slice(start, start + CHUNK)
            final = after[part, :] + (total[part, :] + nt(active[part, :], full)) + vec[6:7, :]
            missing = final - mentor[part, :].astype(jnp.float32)
            slope = live * missing
            out[part, :] = (live * final).astype(jnp.bfloat16)
            upstream[part, :] = slope.astype(jnp.bfloat16)
            column += jnp.sum(slope, axis=0, keepdims=True)
            squares += jnp.sum(slope * missing, axis=0, keepdims=True)
        sums[...] = jnp.broadcast_to(column, sums.shape)
        energy[...] = jnp.broadcast_to(0.5 * jnp.sum(squares, axis=1, keepdims=True), energy.shape)


def contract_forward(where, alive, active, after, mentor, vec, weights, block=1024):
    rows, d = after.shape
    *_, r, half = weights.shape
    steps = half // block
    weight = pl.BlockSpec(
        (2, 2, 2, 2, pl.squeezed, r, block),
        lambda j, s: (0, 0, 0, 0, jnp.bitwise_xor(j // steps, s[2]), 0, j % steps),
    )
    f32, bf16 = jnp.float32, jnp.bfloat16
    whole = resident((rows, d))
    return call(
        functools.partial(contract_kernel, steps),
        (2 * steps,),
        where,
        [
            (alive, pl.BlockSpec(memory_space=pltpu.SMEM)),
            (active, pl.BlockSpec((pl.squeezed, rows, block), lambda j, s: (j // steps, 0, j % steps))),
            (after, whole),
            (mentor, whole),
            (vec, resident(vec.shape)),
            (weights, weight),
        ],
        [
            ((rows, d), bf16, whole),
            ((rows, d), bf16, whole),
            ((8, d), f32, resident((8, d))),
            ((8, 128), f32, resident((8, 128))),
        ],
        [pltpu.VMEM((rows, d), f32)],
        "contract_forward",
    )


def feed_backward_kernel(rows, where, upstream, second, active, slope, weight, w0, w1,
                         grad_second, e0, e1, d0, d1, bias, up, result, total):
    step, last = pl.program_id(0), pl.num_programs(0) - 1
    fill_by_core(where, up, (w0, w1), rows)
    grad_active = nn(upstream[...], weight[...].reshape(up.shape))
    grad_hidden = grad_active * slope[...].astype(jnp.float32)
    bias[...] = jnp.broadcast_to(jnp.sum(grad_hidden, axis=0, keepdims=True), bias.shape)
    grad_hidden = grad_hidden.astype(jnp.bfloat16)
    result[...] = tn(upstream[...], active[...]).astype(jnp.bfloat16)
    spill_by_core(where, result, (d0, d1), rows)
    back = nt(grad_hidden, up[...])

    @pl.when(step == 0)
    def _():
        total[...] = back

    @pl.when((step > 0) & (step < last))
    def _():
        total[...] += back

    @pl.when(step == last)
    def _():
        grad_second[...] = (total[...] + back).astype(jnp.bfloat16)

    result[...] = tn(second[...], grad_hidden).astype(jnp.bfloat16)
    spill_by_core(where, result, (e0, e1), rows)


def feed_backward(where, upstream, second, active, slope, down, up, x_rel, block=512):
    rows, d = upstream.shape
    *_, r, half = up[0].shape
    f32, bf16 = jnp.float32, jnp.bfloat16
    whole = resident((rows, d))
    part = pl.BlockSpec((pl.squeezed, rows, block), lambda j, s: (x_rel, 0, j))
    piece = pl.BlockSpec((2, 2, 2, r, block), lambda j, s: (0, 0, 0, 0, j))
    weight = pl.BlockSpec(
        (2, 2, 2, 2, pl.squeezed, r, block),
        lambda j, s: (0, 0, 0, 0, jnp.bitwise_xor(x_rel, s[2]), 0, j),
    )
    return call(
        functools.partial(feed_backward_kernel, r),
        (half // block,),
        where,
        [(upstream, whole), (second, whole), (active, part), (slope, part), (down, weight)]
        + [(p, piece) for p in up],
        [((rows, d), bf16, whole)]
        + [((2, 2, 2, r, half), bf16, piece)] * 4
        + [((8, half), f32, pl.BlockSpec((8, block), lambda j, s: (0, j)))],
        [pltpu.VMEM((d, block), bf16)] * 2 + [pltpu.VMEM((rows, d), f32)],
        "feed_backward",
    )


def norm_backward_kernel(count, gain_row, last, where, value, base, vec, *refs):
    outs = 2 if last else 3
    grads, extra, (*total, low, sums) = refs[:count], refs[count:-outs], refs[-outs:]

    @pl.when(pl.program_id(0) == 0)
    def _():
        sums[...] = jnp.zeros_like(sums)
        if extra:
            column, energy, alive, own, other = extra
            d = sums.shape[1]
            sums[3:4, :] = column[0:1, :]
            sums[4:5, :] = jnp.broadcast_to(energy[0:1, 0:1], (1, d))
            sums[5:6, :] = jnp.full((1, d), alive[0] * (value.shape[0] * pl.num_programs(0)), jnp.float32)
            here = where[2] == 0
            for i in BITS:
                part = slice(i * d, (i + 1) * d)
                sums[8 + i : 9 + i, :] = jnp.where(here, own[0:1, part], other[0:1, part])
                sums[10 + i : 11 + i, :] = jnp.where(here, other[0:1, part], own[0:1, part])

    upstream = grads[0][...].astype(jnp.float32)
    for ref in grads[1:]:
        upstream = upstream + ref[...].astype(jnp.float32)
    norm, inverse = normalized(value[...])
    e = upstream * vec[gain_row : gain_row + 1, :]
    mean_e = jnp.mean(e, axis=-1, keepdims=True)
    mean_en = jnp.mean(e * norm, axis=-1, keepdims=True)
    result = base[...].astype(jnp.float32) + inverse * (e - mean_e - norm * mean_en)
    for ref in total:
        ref[...] = result
    low[...] = result.astype(jnp.bfloat16)
    for row, item in enumerate((upstream * norm, upstream, result)):
        sums[row : row + 1, :] += jnp.sum(item, axis=0, keepdims=True)


def norm_backward(where, value, base, vec, gain_row, grads, extra=(), last=False):
    rows, d = value.shape
    part = pl.BlockSpec((CHUNK, d), lambda i, s: (i, 0))
    height = 16 if extra else 8
    carried = [
        (x, pl.BlockSpec(memory_space=pltpu.SMEM) if x.ndim == 1 else resident(x.shape)) for x in extra
    ]
    return call(
        functools.partial(norm_backward_kernel, len(grads), gain_row, last),
        (rows // CHUNK,),
        where,
        [(value, part), (base, part), (vec, resident(vec.shape))] + [(g, part) for g in grads] + carried,
        [((rows, d), jnp.float32, part)] * (0 if last else 1)
        + [
            ((rows, d), jnp.bfloat16, part),
            ((height, d), jnp.float32, resident((height, d))),
        ],
        [],
        "norm_backward",
    )


def result_backward_kernel(rows, where, branch, attended, weight, grad, o0, o1, full):
    grad[...] = nn(branch[...], weight[...].reshape(branch.shape[1], -1)).astype(jnp.bfloat16)
    full[...] = tn(branch[...], attended[...]).astype(jnp.bfloat16)
    spill_by_core(where, full, (o0, o1), rows)


def result_backward(where, branch, attended, gathered, r, col):
    rows, d = branch.shape
    bf16 = jnp.bfloat16
    part = pl.BlockSpec((rows, col), lambda x, s: (0, x))
    piece = pl.BlockSpec((pl.squeezed, pl.squeezed, 2, 2, 2, r, col), lambda x, s: (1, x, 0, 0, 0, 0, 0))
    return call(
        functools.partial(result_backward_kernel, r),
        (2,),
        where,
        [
            (branch, resident((rows, d))),
            (attended, part),
            (gathered, weight_block(r, col, lambda x: (3, x))),
        ],
        [((rows, d), bf16, part)] + [((2, 2, 2, 2, 2, r, col), bf16, piece)] * 2,
        [pltpu.VMEM((d, col), bf16)],
        "result_backward",
    )


def project_weight_kernel(rows, where, first, grad, _, __, a0, a1, b0, b1, full):
    full[...] = tn(first[...], grad[...]).astype(jnp.bfloat16)

    @pl.when(pl.program_id(0) < 2)
    def _():
        spill_by_core(where, full, (a0, a1), rows)

    @pl.when(pl.program_id(0) == 2)
    def _():
        spill_by_core(where, full, (b0, b1), rows)


def project_weight(where, first, grads, with_result, r, col):
    rows, d = first.shape
    bf16 = jnp.bfloat16
    part = pl.BlockSpec((pl.squeezed, rows, col), lambda w, x, s: (w, 0, x))
    block = (pl.squeezed, pl.squeezed, 2, 2, 2, r, col)
    front = pl.BlockSpec(
        block, lambda w, x, s: (jnp.minimum(w, 1), jnp.where(w < 2, x, 1), 0, 0, 0, 0, 0)
    )
    back = pl.BlockSpec(block, lambda w, x, s: (0, jnp.where(w < 2, 0, x), 0, 0, 0, 0, 0))
    anywhere = pl.BlockSpec(memory_space=pl.ANY)
    return call(
        functools.partial(project_weight_kernel, r),
        (3, 2),
        where,
        [(first, resident((rows, d))), (grads, part)] + [(p, anywhere) for p in with_result],
        [((2, 2, 2, 2, 2, r, col), bf16, front)] * 2 + [((2, 2, 2, 2, 2, r, col), bf16, back)] * 2,
        [pltpu.VMEM((d, col), bf16)],
        "project_weight",
        (),
        ((2, 2), (3, 3)),
    )


def project_backward_kernel(where, grad, weight, out, total):
    part = nt(grad[...], weight[...].reshape(out.shape[1], -1))
    step = pl.program_id(0) * pl.num_programs(1) + pl.program_id(1)
    last = pl.num_programs(0) * pl.num_programs(1) - 1

    @pl.when(step == 0)
    def _():
        total[...] = part

    @pl.when((step > 0) & (step < last))
    def _():
        total[...] += part

    @pl.when(step == last)
    def _():
        out[...] = (total[...] + part).astype(jnp.bfloat16)


def project_backward(where, grads, gathered, r, col):
    _, rows, d = grads.shape
    return call(
        project_backward_kernel,
        (3, 2),
        where,
        [
            (grads, pl.BlockSpec((pl.squeezed, rows, col), lambda w, x, s: (w, 0, x))),
            (gathered, weight_block(r, col, lambda w, x: (w, x))),
        ],
        [((rows, d), jnp.bfloat16, resident((rows, d)))],
        [pltpu.VMEM((rows, d), jnp.float32)],
        "project_backward",
    )[0]


def merge_weight_kernel(where, ent, byp, grad, o0, o1, full):
    half = ent.shape[1]
    full[:half, :] = tn(ent[...], grad[...]).astype(jnp.bfloat16)
    full[half:, :] = tn(byp[...], grad[...]).astype(jnp.bfloat16)
    for c_rel, ref in enumerate((o0, o1)):
        for x_rel in BITS:
            x = jnp.bitwise_xor(where[2], x_rel)
            for y_rel in BITS:
                for hi in BITS:
                    for lo in BITS:
                        at = place_at(where, hi, lo, y_rel, c_rel, 128) + x * 64
                        ref[x_rel, y_rel, hi, lo] = full[pl.ds(pl.multiple_of(at, 64), 64), :]


def merge_weight(where, ent, byp, grad, r):
    rows, d = ent.shape
    half = d // 2
    bf16 = jnp.bfloat16
    whole = resident((rows, d))
    piece = pl.BlockSpec((pl.squeezed, 2, 2, 2, 2, r, half), lambda j, s: (j, 0, 0, 0, 0, 0, 0))
    return call(
        merge_weight_kernel,
        (2,),
        where,
        [(ent, whole), (byp, whole), (grad, pl.BlockSpec((rows, half), lambda j, s: (0, j)))],
        [((2, 2, 2, 2, 2, r, half), bf16, piece)] * 2,
        [pltpu.VMEM((2 * d, half), bf16)],
        "merge_weight",
    )


def merge_backward_kernel(where, grad, full, left, right):
    half = left.shape[1]
    weight = full[...].reshape(2 * half, half)
    left[...] = nt(grad[...], weight[:half, :])
    right[...] = nt(grad[...], weight[half:, :])


def merge_backward(where, grad, gathered, r, after):
    rows, d = grad.shape
    part = pl.BlockSpec((CHUNK, d), lambda i, w: (i, 0))
    return call(
        merge_backward_kernel,
        (rows // CHUNK,),
        where,
        [(grad, part), (gathered, resident((2, 2, 2, 2, 2, r, d)))],
        [((rows, d), jnp.float32, part)] * 2,
        [],
        "merge_backward",
        after,
    )


def swap(value, axis):
    return lax.ppermute(value, axis, [(0, 1), (1, 0)])


def swap_line(value, bit):
    return lax.ppermute(value, "z", [(i, i ^ bit) for i in range(4)])


def plus(*parts):
    total = parts[0].astype(jnp.float32)
    for part in parts[1:]:
        total = total + part.astype(jnp.float32)
    return total


def send(value, axis):
    return swap(value.astype(jnp.bfloat16), axis)


def line_parts(total, index, dim):
    mine = lax.dynamic_index_in_dim(total, index, dim, keepdims=False)
    other = lax.dynamic_index_in_dim(total, 1 - index, dim, keepdims=False)
    return mine, other.astype(jnp.bfloat16)


def one_sequence_plan(
    entering_states,
    bypass_states,
    mentor_states,
    occupancy_mask,
    bypass_merge_matrix,
    bypass_merge_offset,
    mixer_layernorm_scale,
    mixer_layernorm_offset,
    asking_map_matrix,
    lookup_map_matrix,
    content_map_matrix,
    mixer_result_matrix,
    mixer_result_offset,
    perceptron_layernorm_scale,
    perceptron_layernorm_offset,
    expand_layer_matrix,
    expand_layer_offset,
    contract_layer_matrix,
    contract_layer_offset,
):
    f32, bf16 = jnp.float32, jnp.bfloat16
    rows, d = entering_states.shape
    r, col = asking_map_matrix.shape
    half = expand_layer_matrix.shape[1]
    everyone = ("z", "y", "c", "x")
    z, y, c, x = (lax.axis_index(axis) for axis in everyone)
    hi, lo = z // 2, z % 2
    device = ((z * 2 + y) * 2 + c) * 2 + x
    where = jnp.stack([y, c, x, hi, lo]).astype(jnp.int32)
    small = (
        bypass_merge_offset,
        mixer_layernorm_scale,
        mixer_layernorm_offset,
        mixer_result_offset,
        perceptron_layernorm_scale,
        perceptron_layernorm_offset,
        contract_layer_offset,
        expand_layer_offset,
    )
    flat = jnp.concatenate(small)
    flat = jnp.pad(flat, (0, 8 * d - flat.shape[0])).reshape(8, d)
    pack = jnp.concatenate(
        [
            bypass_merge_matrix,
            jnp.concatenate([asking_map_matrix, lookup_map_matrix], axis=1),
            jnp.concatenate([content_map_matrix, mixer_result_matrix.T], axis=1),
            flat,
        ]
    )
    pack = lax.all_gather(pack, everyone, axis=0, tiled=False)
    gathered = pack.reshape((2,) * 5 + pack.shape[1:])

    down = lax.all_gather(contract_layer_matrix.T, everyone, axis=0, tiled=False)
    down = down.reshape((2,) * 5 + down.shape[1:])

    up = expand_layer_matrix
    up = pile(where, 3, up, swap_line(up, 2), 0)
    up = pile(where, 4, up, swap_line(up, 1), 1)
    up_block = pile(where, None, up, swap(up, "y"), 0)
    (gathered,) = gate(where, [gathered], (up_block,))
    raw = merge_forward(where, entering_states, bypass_states, gathered, r)

    rest = pack[:, 3 * r].astype(f32)
    count = pack.shape[0]
    vec = rest[:, : 7 * d // count].reshape(count, 7, d // count).transpose(1, 0, 2).reshape(7, d)
    vec = jnp.pad(vec, ((0, 1), (0, 0)))
    hidden_add = rest[:, 7 * d // count : 7 * d // count + 2 * half // count].reshape(2, 1, half)
    alive = lax.dynamic_index_in_dim(occupancy_mask, x, keepdims=True).astype(f32)

    merged, first, projected = project_forward(where, raw, vec, gathered, r, col)
    up_other, projected = gate(where, [swap(up_block, "x"), projected], ())
    up_away = [swap(up_block, "c"), swap(up_other, "c")]
    attended, logs = attention_forward(where, projected)
    *up_away, attended, logs = gate(where, up_away + [attended, logs], ())
    expand_pieces = ((up_block, up_away[0]), (up_other, up_away[1]))
    after_attn, second = result_forward(where, attended, merged, vec, gathered, r, col)
    active, slope = expand_forward(where, second, hidden_add, expand_pieces)
    block_out, upstream, down_bias, energy = contract_forward(
        where, alive, active, after_attn, mentor_states, vec, down
    )

    def feed(x_rel):
        return feed_backward(
            where, upstream, second, active, slope, down, expand_pieces[x_rel], x_rel
        )

    none2, none3 = (None,) * 2, (None,) * 3
    by_lo = [(f32, (None, (4, 0))), (bf16, (None, (4, 1)))]
    by_hi = [(f32, ((3, 0),)), (bf16, ((3, 1),))]

    gs1, e1, e1s, d1, d1s, hb1 = feed(1)
    e1c, d1c = swap(e1s, "c"), swap(d1s, "c")
    gs0, e0, e0s, d0, d0s, hb0 = feed(0)
    e1x, d1y, gs0, e0s, d0s = fold(
        where,
        [
            ([[(e1, none3), (e1c, none3)]], [(bf16, ())]),
            ([[(d1, (1,) + none2), (d1c, (1,) + none2)]], [(bf16, ())]),
        ],
        (gs0, e0s, d0s),
    )
    e1x, d1y, e0c, d0c = swap(e1x, "x"), swap(d1y, "y"), swap(e0s, "c"), swap(d0s, "c")
    grad_after, branch, sums_two = norm_backward(
        where, after_attn, upstream, vec, 4, [gs0, gs1], (down_bias, energy, alive, hb0, hb1)
    )
    parcel = lax.all_gather(sums_two, everyone, axis=0, tiled=False)
    d0y, branch = fold(
        where, [([[(d0, (1,) + none2), (d0c, (1,) + none2)]], [(bf16, ())])], (branch,), (e0c,)
    )
    d0y = swap(d0y, "y")
    grad_attended, o0, o1 = result_backward(where, branch, attended, gathered, r, col)

    def attend(part, grads):
        return attention_backward(where, projected, attended, logs, grad_attended, part, 2, grads)

    grads = attend(0, None)
    e_far, d_far, grads = fold(
        where,
        [
            ([[(a, (1,) + none2) for a in (e0, e0c, e1x)]], [(bf16, ())]),
            ([[(d1, (0,) + none2), (d1c, (0,) + none2), (d1y, none2)]], [(bf16, ())]),
        ],
        (grads,),
        (d0y,),
    )
    e_far, d_far = swap(e_far, "y"), swap(d_far, "x")
    grads = attend(1, grads)
    front = (0,) + none2
    ends, ends_z, grads = fold(
        where,
        [
            (
                [
                    [(e0, front), (e0c, front), (e1x, front), (e_far, none2)],
                    [(d0, front), (d0c, front), (d0y, none2), (d_far, none2)],
                ],
                by_lo,
            )
        ],
        (grads,),
        (parcel,),
    )
    ends_z = swap_line(ends_z, 1)
    p0, p1, vo0, vo1 = project_weight(where, first, grads, (o0, o1), r, col)
    qk_c, vo_c = swap(p1, "c"), swap(vo1, "c")
    grad_first = project_backward(where, grads, gathered, r, col)
    ends, ends_z, grad_first = fold(
        where, [([[(a, (None,)) for a in (ends, ends_z)]], by_hi)], (grad_first,), flops=4 * 10**10
    )
    qk_x, vo_y, grad_first = fold(
        where,
        [
            ([[(a, (None, 1) + none3) for a in (p0, qk_c)]], [(bf16, ())]),
            ([[(a, (None, None, 1) + none2) for a in (vo0, vo_c)]], [(bf16, ())]),
        ],
        (grad_first,),
    )
    qk_x, vo_y, ends_z = swap(qk_x, "x"), swap(vo_y, "y"), swap_line(ends_z, 2)
    merge_grad, three = norm_backward(where, merged, grad_after, vec, 1, [grad_first], last=True)
    m0, m1 = merge_weight(where, entering_states, bypass_states, merge_grad, r)
    three_c = swap(three, "c")
    ends, qk_y, vo_x, three, merge_grad, m1 = fold(
        where,
        [
            ([[(a, ()) for a in (ends, ends_z)]], [(f32, ())]),
            ([[(a, (None, 0, 1) + none2) for a in (p0, qk_c)] + [(qk_x, (None, 1) + none2)]], [(bf16, ())]),
            ([[(a, (None, 1, 0) + none2) for a in (vo0, vo_c)] + [(vo_y, (None, 1) + none2)]], [(bf16, ())]),
            ([[(three, ()), (three_c, ())]], [(f32, ())]),
        ],
        (merge_grad, m1),
    )
    qk_y, vo_x, m_c, three_x = swap(qk_y, "y"), swap(vo_x, "x"), swap(m1, "c"), swap_line(three, 1)
    grad_tokens, grad_shortcut = merge_backward(where, merge_grad, gathered, r, ())
    four_pieces = [
        [(a, (i, 0, 0) + none2) for a in (p0, qk_c)] + [(qk_x, (i, 0) + none2), (qk_y, (i,) + none2)]
        for i in BITS
    ] + [
        [(a, (i, 0, 0) + none2) for a in (vo0, vo_c)] + [(vo_y, (i, 0) + none2), (vo_x, (i,) + none2)]
        for i in BITS
    ]
    four, four_z, l_x, r_y, three, grad_tokens = fold(
        where,
        [
            (four_pieces, by_lo),
            ([[(a, (0, 1) + none3) for a in (m0, m_c)]], [(bf16, ())]),
            ([[(a, (1, None, 1) + none2) for a in (m0, m_c)]], [(bf16, ())]),
            ([[(three, ()), (three_x, ())]], [(f32, ())]),
        ],
        (grad_tokens,),
    )
    l_x, r_y, three_y, four_z = swap(l_x, "x"), swap(r_y, "y"), swap_line(three, 2), swap_line(four_z, 1)
    l_y, r_x, three, four, four_z = fold(
        where,
        [
            ([[(a, (0, 0, 1) + none2) for a in (m0, m_c)] + [(l_x, (1,) + none2)]], [(bf16, ())]),
            ([[(a, (1, 1, 0) + none2) for a in (m0, m_c)] + [(r_y, (1,) + none2)]], [(bf16, ())]),
            ([[(three, ()), (three_y, ())]], [(f32, ())]),
            ([[(a, (None,)) for a in (four, four_z)]], by_hi),
        ],
    )
    l_y, r_x, three_z, four_z = swap(l_y, "y"), swap(r_x, "x"), swap(three, "x"), swap_line(four_z, 2)
    grad_merge, merge_z, three = fold(
        where,
        [
            (
                [
                    [(a, (0, 0, 0) + none2) for a in (m0, m_c)] + [(l_x, (0,) + none2), (l_y, none2)],
                    [(a, (1, 0, 0) + none2) for a in (m0, m_c)] + [(r_y, (0,) + none2), (r_x, none2)],
                ],
                by_lo,
            ),
            ([[(a, ()) for a in (three, three_z)]], [(f32, ())]),
        ],
    )
    merge_z, three_z = swap_line(merge_z, 1), swap(three, "y")
    grad_merge, merge_z, four, three = fold(
        where,
        [
            ([[(a, (None,)) for a in (grad_merge, merge_z)]], by_hi),
            ([[(a, ()) for a in (four, four_z)]], [(f32, ())]),
            ([[(a, ()) for a in (three, three_z)]], [(f32, ())]),
        ],
    )
    grad_merge = plus(grad_merge, swap_line(merge_z, 2))
    own = jnp.sum(parcel, axis=0)
    grad_expand, grad_contract = ends[:, :half], ends[:, half:]
    grad_query, grad_key, grad_value, grad_result = (four[:, i * col : (i + 1) * col] for i in range(4))

    share = d // count
    three = lax.dynamic_slice_in_dim(three, device * share, share, 1)
    four_rows = lax.dynamic_slice_in_dim(own[:4], device * share, share, 1)
    loss_value = own[4, 0] / (own[5, 0] * d)
    share = 2 * half // count
    hidden_row = lax.dynamic_slice_in_dim(own[8:12].reshape(-1), device * share, share, 0)
    sums = (three[2], three[0], three[1], four_rows[2], four_rows[0], four_rows[1], four_rows[3], hidden_row)
    return (
        block_out,
        loss_value,
        grad_tokens,
        grad_shortcut,
        grad_merge,
        sums[0],
        sums[1],
        sums[2],
        grad_query,
        grad_key,
        grad_value,
        grad_result.T,
        sums[3],
        sums[4],
        sums[5],
        grad_expand,
        sums[7],
        grad_contract.T,
        sums[6],
    )


ARGUMENTS = (
    ("ft", None),
    ("ft", None),
    ("ft", None),
    ("f",),
    ("ft", None),
    ("ft",),
    ("ft",),
    ("ft",),
    ("f", "t"),
    ("f", "t"),
    ("f", "t"),
    ("t", "f"),
    ("ft",),
    ("ft",),
    ("ft",),
    ("f", "t"),
    ("ft",),
    ("t", "f"),
    ("ft",),
)
RESULTS = (
    ("ft", None),
    (),
    ("ft", None),
    ("ft", None),
    ("ft", None),
    ("ft",),
    ("ft",),
    ("ft",),
    ("f", "t"),
    ("f", "t"),
    ("f", "t"),
    ("t", "f"),
    ("ft",),
    ("ft",),
    ("ft",),
    ("f", "t"),
    ("ft",),
    ("t", "f"),
    ("ft",),
)


def solution(mesh):
    def whole(*args):
        rows = args[0].shape[0] // mesh.size
        if rows == SEQ_LEN and dict(mesh.shape) == {"fsdp": 16, "tp": 2}:
            plan = one_sequence_plan
            use = jax.sharding.Mesh(mesh.devices.reshape(4, 2, 2, 2), ("z", "y", "c", "x"))
            names = {"f": ("z", "y", "c"), "t": ("x",), "ft": ("z", "y", "c", "x")}
        else:
            plan = per_device_split
            use = mesh
            names = {"f": ("fsdp",), "t": ("tp",), "ft": ("fsdp", "tp")}

        def place(entry):
            return P(*(None if e is None else names[e] for e in entry))

        return jax.shard_map(
            plan,
            mesh=use,
            in_specs=tuple(place(e) for e in ARGUMENTS),
            out_specs=tuple(place(e) for e in RESULTS),
            check_vma=False,
        )(*args)

    return whole
```

```python
import functools
import math

import jax
import jax.numpy as jnp
from jax import lax
from jax.experimental import pallas as pl
from jax.experimental.pallas import tpu as pltpu
from jax.sharding import PartitionSpec as P

D = 1024
HEADS = 16
SEQ_LEN = 1104


EPSILON = 1e-05


def layer_norm(value, gain, shift):
    centred = value - jnp.mean(value, axis=-1, keepdims=True)
    spread = jnp.mean(centred * centred, axis=-1, keepdims=True)
    return centred * lax.rsqrt(spread + EPSILON) * gain + shift


def contract_rows(left, right):
    return lax.dot_general(
        left, right, (((0,), (0,)), ((), ())), preferred_element_type=jnp.float32
    )


def contract_cols(left, right):
    return lax.dot_general(
        left, right, (((1,), (1,)), ((), ())), preferred_element_type=jnp.float32
    )


def attend_forward(queries, keys_all, values):
    scale = float(queries.shape[-1]) ** (-0.5)
    scores = (
        jnp.einsum("qhd,khd->hqk", queries, keys_all, preferred_element_type=jnp.float32) * scale
    )
    peak_score = jnp.max(scores, axis=-1, keepdims=True)
    raised = jnp.exp(scores - peak_score)
    row_total = jnp.sum(raised, axis=-1, keepdims=True)
    weights_low = (raised / row_total).astype(jnp.bfloat16)
    output = jnp.einsum("hqk,khd->qhd", weights_low, values, preferred_element_type=jnp.float32)
    return (output.astype(jnp.bfloat16), peak_score + jnp.log(row_total))


def attend_backward(queries, keys_all, values, summary, upstream):
    scale = float(queries.shape[-1]) ** (-0.5)
    scores = (
        jnp.einsum("qhd,khd->hqk", queries, keys_all, preferred_element_type=jnp.float32) * scale
    )
    probs_full = jnp.exp(scores - summary)
    grad_probs = jnp.einsum("qhd,khd->hqk", upstream, values, preferred_element_type=jnp.float32)
    grad_values = jnp.einsum(
        "hqk,qhd->khd",
        probs_full.astype(jnp.bfloat16),
        upstream,
        preferred_element_type=jnp.float32,
    )
    centre = jnp.sum(probs_full * grad_probs, axis=-1, keepdims=True)
    grad_scores = (probs_full * (grad_probs - centre)).astype(jnp.bfloat16)
    grad_queries = (
        jnp.einsum("hqk,khd->qhd", grad_scores, keys_all, preferred_element_type=jnp.float32)
        * scale
    )
    grad_keys = (
        jnp.einsum("hqk,qhd->khd", grad_scores, queries, preferred_element_type=jnp.float32) * scale
    )
    return (
        grad_queries.astype(jnp.bfloat16),
        grad_keys.astype(jnp.bfloat16),
        grad_values.astype(jnp.bfloat16),
    )


def gelu_exact(value):
    return jax.nn.gelu(value, approximate=False)


def per_device_split(
    entering_states,
    bypass_states,
    mentor_states,
    occupancy_mask,
    bypass_merge_matrix,
    bypass_merge_offset,
    mixer_layernorm_scale,
    mixer_layernorm_offset,
    asking_map_matrix,
    lookup_map_matrix,
    content_map_matrix,
    mixer_result_matrix,
    mixer_result_offset,
    perceptron_layernorm_scale,
    perceptron_layernorm_offset,
    expand_layer_matrix,
    expand_layer_offset,
    contract_layer_matrix,
    contract_layer_offset,
):
    rows = entering_states.shape[0]
    width = D // HEADS
    position = lax.axis_index("tp")
    (
        merge_full,
        merge_add,
        gain_one,
        shift_one,
        output_add,
        gain_two,
        shift_two,
        hidden_add,
        down_add,
    ) = (
        lax.all_gather(bypass_merge_matrix, ("fsdp", "tp"), axis=0, tiled=True),
        lax.all_gather(bypass_merge_offset, ("fsdp", "tp"), axis=0, tiled=True),
        lax.all_gather(mixer_layernorm_scale, ("fsdp", "tp"), axis=0, tiled=True),
        lax.all_gather(mixer_layernorm_offset, ("fsdp", "tp"), axis=0, tiled=True),
        lax.all_gather(mixer_result_offset, ("fsdp", "tp"), axis=0, tiled=True),
        lax.all_gather(perceptron_layernorm_scale, ("fsdp", "tp"), axis=0, tiled=True),
        lax.all_gather(perceptron_layernorm_offset, ("fsdp", "tp"), axis=0, tiled=True),
        lax.all_gather(expand_layer_offset, ("fsdp", "tp"), axis=0, tiled=True),
        lax.all_gather(contract_layer_offset, ("fsdp", "tp"), axis=0, tiled=True),
    )
    query_full, key_full, value_full, output_full, hidden_full, down_full = (
        lax.all_gather(asking_map_matrix, "fsdp", axis=0, tiled=True),
        lax.all_gather(lookup_map_matrix, "fsdp", axis=0, tiled=True),
        lax.all_gather(content_map_matrix, "fsdp", axis=0, tiled=True),
        lax.all_gather(mixer_result_matrix, "fsdp", axis=1, tiled=True),
        lax.all_gather(expand_layer_matrix, "fsdp", axis=0, tiled=True),
        lax.all_gather(contract_layer_matrix, "fsdp", axis=1, tiled=True),
    )
    gain_one = gain_one.astype(jnp.float32)
    shift_one = shift_one.astype(jnp.float32)
    gain_two = gain_two.astype(jnp.float32)
    shift_two = shift_two.astype(jnp.float32)
    project = jnp.concatenate([query_full, key_full, value_full], axis=1)
    local_width = query_full.shape[1]
    local_heads = local_width // width
    local_hidden = hidden_full.shape[1]
    row_index = position * rows + jnp.arange(rows, dtype=jnp.int32)
    slot_of_row = row_index // SEQ_LEN
    series_place_total = occupancy_mask.shape[0]
    agreeing_lines = (
        slot_of_row[:, None] == jnp.arange(series_place_total, dtype=jnp.int32)[None, :]
    ).astype(jnp.float32)
    alive_tokens = jnp.sum(
        agreeing_lines * occupancy_mask.astype(jnp.float32)[None, :], axis=1, keepdims=True
    )
    joined = jnp.concatenate([entering_states, bypass_states], axis=1)
    merged = jnp.dot(joined, merge_full, preferred_element_type=jnp.float32) + merge_add.astype(
        jnp.float32
    )
    first = layer_norm(merged, gain_one, shift_one).astype(jnp.bfloat16)
    first_all = lax.all_gather(first, "tp", axis=0, tiled=True)
    group_rows = first_all.shape[0]
    slots = group_rows // SEQ_LEN
    projected = jnp.dot(first_all, project, preferred_element_type=jnp.float32).astype(jnp.bfloat16)
    shaped = projected.reshape(slots, SEQ_LEN, 3, local_heads, width)
    queries = shaped[:, :, 0]
    keys_all = shaped[:, :, 1]
    values = shaped[:, :, 2]
    attended, summary = lax.map(
        lambda item: attend_forward(item[0], item[1], item[2]), (queries, keys_all, values)
    )
    attended_flat = attended.reshape(group_rows, local_width)
    attention_term = jnp.dot(attended_flat, output_full, preferred_element_type=jnp.float32)
    after_attn = (
        merged
        + lax.psum_scatter(
            attention_term.astype(jnp.bfloat16), "tp", scatter_dimension=0, tiled=True
        ).astype(jnp.float32)
        + output_add.astype(jnp.float32)
    )
    second = layer_norm(after_attn, gain_two, shift_two).astype(jnp.bfloat16)
    second_all = lax.all_gather(second, "tp", axis=0, tiled=True)
    hidden_slice = lax.dynamic_slice_in_dim(
        hidden_add.astype(jnp.float32), position * local_hidden, local_hidden, 0
    )
    hidden = jnp.dot(second_all, hidden_full, preferred_element_type=jnp.float32) + hidden_slice
    active = gelu_exact(hidden).astype(jnp.bfloat16)
    feed_term = jnp.dot(active, down_full, preferred_element_type=jnp.float32)
    final = (
        after_attn
        + lax.psum_scatter(
            feed_term.astype(jnp.bfloat16), "tp", scatter_dimension=0, tiled=True
        ).astype(jnp.float32)
        + down_add.astype(jnp.float32)
    )
    missing = final - mentor_states.astype(jnp.float32)
    grad_final = alive_tokens * missing
    block_out = (final * alive_tokens).astype(jnp.bfloat16)
    energy, counted = lax.psum(
        (0.5 * jnp.sum(grad_final * missing), jnp.sum(alive_tokens)), ("fsdp", "tp")
    )
    loss_value = energy / (counted * D)
    grad_down_bias = jnp.sum(grad_final, axis=0)
    upstream = grad_final.astype(jnp.bfloat16)
    upstream_all = lax.all_gather(upstream, "tp", axis=0, tiled=True)
    grad_down = contract_rows(active, upstream_all)
    grad_active = contract_cols(upstream_all, down_full)
    gelu_value, gelu_pull = jax.vjp(gelu_exact, hidden)
    grad_hidden = gelu_pull(grad_active)[0].astype(jnp.bfloat16)
    grad_hidden_local = jnp.sum(grad_hidden.astype(jnp.float32), axis=0)
    grad_hidden_weight = contract_rows(second_all, grad_hidden)
    feed_back_term = contract_cols(grad_hidden, hidden_full)
    grad_second = lax.psum_scatter(
        feed_back_term.astype(jnp.bfloat16), "tp", scatter_dimension=0, tiled=True
    ).astype(jnp.float32)
    hidden_bias_term = lax.dynamic_update_slice_in_dim(
        jnp.zeros((hidden_add.shape[0],), jnp.float32),
        grad_hidden_local,
        position * local_hidden,
        0,
    )
    norm_value, second_pull = jax.vjp(layer_norm, after_attn, gain_two, shift_two)
    back_after, grad_gain_two, grad_shift_two = second_pull(grad_second)
    grad_after = grad_final + back_after
    grad_output_bias = jnp.sum(grad_after, axis=0)
    branch_all = lax.all_gather(grad_after.astype(jnp.bfloat16), "tp", axis=0, tiled=True)
    grad_output_weight = contract_rows(attended_flat, branch_all)
    grad_attended = contract_cols(branch_all, output_full).astype(jnp.bfloat16)
    upstream_heads = grad_attended.reshape(slots, SEQ_LEN, local_heads, width)
    grad_q_heads, grad_k_heads, grad_v_heads = lax.map(
        lambda item: attend_backward(item[0], item[1], item[2], item[3], item[4]),
        (queries, keys_all, values, summary, upstream_heads),
    )
    grad_projected = jnp.stack([grad_q_heads, grad_k_heads, grad_v_heads], axis=2).reshape(
        group_rows, 3 * local_width
    )
    grad_project = contract_rows(first_all, grad_projected)
    attention_back_term = contract_cols(grad_projected, project)
    grad_first = lax.psum_scatter(
        attention_back_term.astype(jnp.bfloat16), "tp", scatter_dimension=0, tiled=True
    ).astype(jnp.float32)
    first_value, first_pull = jax.vjp(layer_norm, merged, gain_one, shift_one)
    back_merged, grad_gain_one, grad_shift_one = first_pull(grad_first)
    grad_merged = grad_after + back_merged
    grad_merge_bias = jnp.sum(grad_merged, axis=0)
    merge_grad = grad_merged.astype(jnp.bfloat16)
    grad_merge_weight = contract_rows(joined, merge_grad)
    grad_joined = contract_cols(merge_grad, merge_full)
    model_width = entering_states.shape[1]
    grad_tokens = grad_joined[:, :model_width]
    grad_shortcut = grad_joined[:, model_width:]
    grad_query, grad_key, grad_value, grad_output, grad_hidden_full, grad_down_full = (
        lax.psum_scatter(
            grad_project[:, :local_width].astype(jnp.bfloat16),
            "fsdp",
            scatter_dimension=0,
            tiled=True,
        ).astype(jnp.float32),
        lax.psum_scatter(
            grad_project[:, local_width : 2 * local_width].astype(jnp.bfloat16),
            "fsdp",
            scatter_dimension=0,
            tiled=True,
        ).astype(jnp.float32),
        lax.psum_scatter(
            grad_project[:, 2 * local_width :].astype(jnp.bfloat16),
            "fsdp",
            scatter_dimension=0,
            tiled=True,
        ).astype(jnp.float32),
        lax.psum_scatter(
            grad_output_weight.astype(jnp.bfloat16), "fsdp", scatter_dimension=1, tiled=True
        ).astype(jnp.float32),
        lax.psum_scatter(
            grad_hidden_weight.astype(jnp.bfloat16), "fsdp", scatter_dimension=0, tiled=True
        ).astype(jnp.float32),
        lax.psum_scatter(
            grad_down.astype(jnp.bfloat16), "fsdp", scatter_dimension=1, tiled=True
        ).astype(jnp.float32),
    )
    (
        merge_weight_sum,
        merge_bias_sum,
        gain_one_sum,
        shift_one_sum,
        output_bias_sum,
        gain_two_sum,
        shift_two_sum,
        hidden_bias_sum,
        down_bias_sum,
    ) = (
        lax.psum_scatter(grad_merge_weight, ("fsdp", "tp"), scatter_dimension=0, tiled=True),
        lax.psum_scatter(grad_merge_bias, ("fsdp", "tp"), scatter_dimension=0, tiled=True),
        lax.psum_scatter(grad_gain_one, ("fsdp", "tp"), scatter_dimension=0, tiled=True),
        lax.psum_scatter(grad_shift_one, ("fsdp", "tp"), scatter_dimension=0, tiled=True),
        lax.psum_scatter(grad_output_bias, ("fsdp", "tp"), scatter_dimension=0, tiled=True),
        lax.psum_scatter(grad_gain_two, ("fsdp", "tp"), scatter_dimension=0, tiled=True),
        lax.psum_scatter(grad_shift_two, ("fsdp", "tp"), scatter_dimension=0, tiled=True),
        lax.psum_scatter(hidden_bias_term, ("fsdp", "tp"), scatter_dimension=0, tiled=True),
        lax.psum_scatter(grad_down_bias, ("fsdp", "tp"), scatter_dimension=0, tiled=True),
    )
    return (
        block_out,
        loss_value,
        grad_tokens,
        grad_shortcut,
        merge_weight_sum,
        merge_bias_sum,
        gain_one_sum,
        shift_one_sum,
        grad_query,
        grad_key,
        grad_value,
        grad_output,
        output_bias_sum,
        gain_two_sum,
        shift_two_sum,
        grad_hidden_full,
        hidden_bias_sum,
        grad_down_full,
        down_bias_sum,
    )


LOG2E = math.log2(math.e)
PAIR = 128
CHUNK = 368


def nn(a, b):
    return lax.dot_general(a, b, (((1,), (0,)), ((), ())), preferred_element_type=jnp.float32)


def nt(a, b):
    return lax.dot_general(a, b, (((1,), (1,)), ((), ())), preferred_element_type=jnp.float32)


def tn(a, b):
    return lax.dot_general(a, b, (((0,), (0,)), ((), ())), preferred_element_type=jnp.float32)


def vmem():
    return pltpu.CompilerParams(vmem_limit_bytes=60 * 2**20)


def cuts(count, size):
    edges = [i * size for i in range(count // size)] + [count]
    return [slice(a, b) for a, b in zip(edges, edges[1:])]


def attention_forward_kernel(q_ref, k_ref, v_ref, o_ref, l_ref):
    count = q_ref.shape[0]
    scale = (PAIR // 2) ** -0.5 * LOG2E
    low = lax.broadcasted_iota(jnp.int32, (1, PAIR), 1) < PAIR // 2
    keys, values = k_ref[...], v_ref[...]
    zero = jnp.zeros_like(keys)
    heads = (jnp.where(low, keys, zero), jnp.where(low, zero, keys))
    wide = jnp.concatenate([values, jnp.ones_like(values)], axis=1)
    for part in cuts(count, 512):
        queries = q_ref[part, :]
        outs, sums = [], []
        for scores in [nt(queries, head) for head in heads]:
            peak = jnp.max(scores, axis=1, keepdims=True) * scale
            raised = jnp.exp2(scores * scale - peak).astype(jnp.bfloat16)
            both = nn(raised, wide)
            total = both[:, PAIR:]
            outs.append(both[:, :PAIR] / total)
            sums.append(peak + jnp.log2(total))
        o_ref[part, :] = jnp.where(low, outs[0], outs[1]).astype(jnp.bfloat16)
        l_ref[part, :] = jnp.where(low, sums[0], sums[1])


def attention_backward_kernel(q_ref, k_ref, v_ref, o_ref, l_ref, u_ref, out_ref, total_ref):
    count = q_ref.shape[0]
    plain = (PAIR // 2) ** -0.5
    scale = plain * LOG2E
    low = lax.broadcasted_iota(jnp.int32, (1, PAIR), 1) < PAIR // 2
    queries, upstream = q_ref[...], u_ref[...]
    product = upstream.astype(jnp.float32) * o_ref[...].astype(jnp.float32)
    left = jnp.sum(jnp.where(low, product, 0.0), axis=1, keepdims=True)
    right = jnp.sum(jnp.where(low, 0.0, product), axis=1, keepdims=True)
    centres = jnp.transpose(jnp.where(low, left, right))
    logs = jnp.transpose(l_ref[...])
    for head in range(2):

        def own(value):
            zero = jnp.zeros_like(value)
            return jnp.where(low, value, zero) if head == 0 else jnp.where(low, zero, value)

        row = head * (PAIR // 2)
        own_queries, own_upstream = own(queries), own(upstream)
        log_row, centre = logs[row : row + 1, :], centres[row : row + 1, :]
        for part in cuts(count, 256):
            keys, values = k_ref[part, :], v_ref[part, :]
            probs = jnp.exp2(nt(keys, own_queries) * scale - log_row)
            slopes = (probs * (nt(values, own_upstream) - centre)).astype(jnp.bfloat16)
            grad_v = nn(probs.astype(jnp.bfloat16), own_upstream).astype(jnp.bfloat16)
            grad_k = (nn(slopes, own_queries) * plain).astype(jnp.bfloat16)
            grad_q = tn(slopes, own(keys))
            if head == 0:
                out_ref[1, part, :] = grad_k
                out_ref[2, part, :] = grad_v
            else:
                out_ref[1, part, :] = jnp.where(low, out_ref[1, part, :], grad_k)
                out_ref[2, part, :] = jnp.where(low, out_ref[2, part, :], grad_v)
            if head == 0 and part.start == 0:
                total_ref[...] = grad_q
            else:
                total_ref[...] += grad_q
    out_ref[0] = (total_ref[...] * plain).astype(jnp.bfloat16)


def gelu_both(value):
    t = 1.0 / (1.0 + 0.3275911 * math.sqrt(0.5) * jnp.abs(value))
    bell = jnp.exp2(value * value * (-0.5 * LOG2E))
    poly = 0.5 * 1.061405429 * t - 0.5 * 1.453152027
    poly = poly * t + 0.5 * 1.421413741
    poly = poly * t - 0.5 * 0.284496736
    poly = poly * t + 0.5 * 0.254829592
    rest = poly * t * bell
    below = jnp.where(value >= 0, 1.0 - rest, rest)
    return value * below, below + value * bell * (1.0 / math.sqrt(2.0 * math.pi))


def normalized(value):
    centred = value - jnp.mean(value, axis=-1, keepdims=True)
    spread = jnp.mean(centred * centred, axis=-1, keepdims=True)
    inverse = lax.rsqrt(spread + EPSILON)
    return centred * inverse, inverse


def place_at(where_ref, hi, lo, y_rel, c_rel, rows):
    y = jnp.bitwise_xor(where_ref[0], y_rel)
    c = jnp.bitwise_xor(where_ref[1], c_rel)
    return pl.multiple_of(((hi * 2 + lo) * 4 + y * 2 + c) * rows, rows)


BITS = (0, 1)


def once(block, index):
    return pl.BlockSpec(block, index, pipeline_mode=pl.Buffered(1))


def call(kernel, grid, where, ins, outs, scratch, name, after=(), aliases=(), flops=0):
    first, count = len(ins), len(after)

    def ordered_kernel(where_ref, *refs):
        kernel(where_ref, *refs[:first], *refs[first + count :])

    anywhere = pl.BlockSpec(memory_space=pl.ANY)
    return pl.pallas_call(
        ordered_kernel,
        grid_spec=pltpu.PrefetchScalarGridSpec(
            num_scalar_prefetch=1,
            grid=grid,
            in_specs=[spec for _, spec in ins] + [anywhere] * count,
            out_specs=[spec for _, _, spec in outs],
            scratch_shapes=scratch,
        ),
        out_shape=[jax.ShapeDtypeStruct(s, t) for s, t, _ in outs],
        input_output_aliases={1 + i: o for i, o in aliases},
        compiler_params=vmem(),
        cost_estimate=pl.CostEstimate(flops=flops, bytes_accessed=0, transcendentals=0),
        name=name,
    )(where, *(x for x, _ in ins), *after)


def resident(shape):
    return once(shape, lambda *_: (0,) * len(shape))


def attention_forward(where, projected):
    rows, columns = projected.shape
    pairs = columns // 3 // PAIR

    def block(offset):
        return pl.BlockSpec((rows, PAIR), lambda j, s: (0, offset + j))

    return call(
        lambda where_ref, *refs: attention_forward_kernel(*refs),
        (pairs,),
        where,
        [(projected, block(0)), (projected, block(pairs)), (projected, block(2 * pairs))],
        [
            ((rows, pairs * PAIR), jnp.bfloat16, block(0)),
            ((rows, pairs * PAIR), jnp.float32, block(0)),
        ],
        [],
        "attention_forward",
    )


def attention_backward(where, projected, attended, logs, upstream, index, of, grads):
    rows, columns = projected.shape
    pairs = columns // 3 // PAIR
    here = index * (pairs // of)

    def block(offset):
        return pl.BlockSpec((rows, PAIR), lambda j, s: (0, offset + here + j))

    ins = [
        (projected, block(0)),
        (projected, block(pairs)),
        (projected, block(2 * pairs)),
        (attended, block(0)),
        (logs, block(0)),
        (upstream, block(0)),
    ]
    aliases = ()
    if grads is not None:
        ins.append((grads, pl.BlockSpec(memory_space=pl.ANY)))
        aliases = ((6, 0),)

    def kernel(where_ref, *refs):
        attention_backward_kernel(*refs[:6], *refs[-2:])

    return call(
        kernel,
        (pairs // of,),
        where,
        ins,
        [((3, rows, pairs * PAIR), jnp.bfloat16, pl.BlockSpec((3, rows, PAIR), lambda j, s: (0, 0, here + j)))],
        [pltpu.VMEM((rows, PAIR), jnp.float32)],
        "attention_backward",
        (),
        aliases,
    )[0]


def gate(where, values, after):
    anywhere = pl.BlockSpec(memory_space=pl.ANY)
    return call(
        lambda *refs: None,
        (1,),
        where,
        [(v, anywhere) for v in values],
        [(v.shape, v.dtype, anywhere) for v in values],
        [],
        "gate",
        after,
        tuple((i, i) for i in range(len(values))),
    )


def fold_kernel(jobs, carried, waited, where, *refs):
    sources = iter(refs)
    total = sum(len(parts) for pieces, _ in jobs for parts in pieces)
    targets = iter(refs[total + carried + waited :])
    for pieces, results in jobs:
        held = [[next(sources) for _ in parts] for parts in pieces]
        for kind, select in results:
            out, begin = next(targets), 0
            at = tuple(slice(None) if t is None else jnp.bitwise_xor(where[t[0]], t[1]) for t in select)
            for parts in held:
                value = parts[0][at + (Ellipsis,)].astype(jnp.float32)
                for part in parts[1:]:
                    value = value + part[at + (Ellipsis,)].astype(jnp.float32)
                end = begin + value.shape[-1]
                out[..., begin:end] = value.astype(out.dtype)
                begin = end


def fold(where, jobs, carry=(), after=(), flops=0):
    ins, outs, plan = [], [], []
    for pieces, results in jobs:
        columns = 0
        for parts in pieces:
            for array, lead in parts:
                fixed = lead + (None, None)
                block = tuple(n if t is None else pl.squeezed for n, t in zip(array.shape, fixed))
                index = tuple(0 if t is None else t for t in fixed)
                ins.append((array, once(block, lambda i, s, index=index: index)))
            columns += array.shape[-1]
        shape = tuple(n for n, t in zip(array.shape, fixed) if t is None)[:-1] + (columns,)
        for kind, select in results:
            made = tuple(n for n, t in zip(shape, select) if t is None) + shape[len(select) :]
            outs.append((made, kind, resident(made)))
        plan.append((pieces, results))
    anywhere = pl.BlockSpec(memory_space=pl.ANY)
    count, made = len(ins), len(outs)
    ins += [(c, anywhere) for c in carry]
    outs += [(c.shape, c.dtype, anywhere) for c in carry]
    return call(
        functools.partial(fold_kernel, plan, len(carry), 0),
        (1,),
        where,
        ins,
        outs,
        [],
        "fold",
        after,
        tuple((count + i, made + i) for i in range(len(carry))),
        flops,
    )


def pile_kernel(slot, axis, where, mine, other, *outs):
    here = 0 if slot is None else where[slot]
    there = 1 - here
    lead = outs[0].shape[:axis]
    rows = outs[0].shape[-2]
    for number, out in enumerate(outs):
        part = slice(number * rows, (number + 1) * rows)
        for i in range(math.prod(lead)):
            at = ()
            for size in reversed(lead):
                at = (i % size,) + at
                i //= size
            out[at + (here,)] = mine[at + (Ellipsis, part, slice(None))]
            out[at + (there,)] = other[at + (Ellipsis, part, slice(None))]


def pile(where, slot, mine, other, axis, parts=1):
    shape = mine.shape[:axis] + (2,) + mine.shape[axis:-2] + (mine.shape[-2] // parts, mine.shape[-1])
    made = call(
        functools.partial(pile_kernel, slot, axis),
        (1,),
        where,
        [(mine, resident(mine.shape)), (other, resident(mine.shape))],
        [(shape, mine.dtype, resident(shape))] * parts,
        [],
        "pile",
    )
    return made if parts > 1 else made[0]


def weight_block(r, col, number):
    def index(*args):
        which, x_rel = number(*args[:-1])
        return 0, 0, 0, 0, jnp.bitwise_xor(x_rel, args[-1][2]), 1 + which // 2, which % 2

    return pl.BlockSpec((2, 2, 2, 2, pl.squeezed, r, col), index)


def project_kernel(where, ent, byp, full, vec, weight, merged, first, out):
    @pl.when((pl.program_id(0) == 0) & (pl.program_id(1) == 0))
    def _():
        d = ent.shape[1]
        merge = full[...].reshape(2 * d, d)
        for start in range(0, ent.shape[0], CHUNK):
            part = slice(start, start + CHUNK)
            total = nn(ent[part, :], merge[:d, :]) + nn(byp[part, :], merge[d:, :]) + vec[0:1, :]
            merged[part, :] = total
            norm, _ = normalized(total)
            first[part, :] = (norm * vec[1:2, :] + vec[2:3, :]).astype(jnp.bfloat16)

    out[...] = nn(first[...], weight[...].reshape(first.shape[1], -1)).astype(jnp.bfloat16)


def project_forward(where, ent, byp, vec, gathered, r, col):
    rows, d = ent.shape
    f32, bf16 = jnp.float32, jnp.bfloat16
    return call(
        project_kernel,
        (3, 2),
        where,
        [
            (ent, resident((rows, d))),
            (byp, resident((rows, d))),
            (gathered, resident((2, 2, 2, 2, 2, r, d))),
            (vec, resident(vec.shape)),
            (gathered, weight_block(r, col, lambda w, x: (w, x))),
        ],
        [
            ((rows, d), f32, resident((rows, d))),
            ((rows, d), bf16, resident((rows, d))),
            ((rows, 6 * col), bf16, pl.BlockSpec((rows, col), lambda w, x, s: (0, w * 2 + x))),
        ],
        [],
        "project_forward",
    )


def result_kernel(where, attended, merged, vec, weight, after, second):
    d, col = after.shape[1], weight.shape[-1]
    own = weight[:, :, :, :, where[2]].reshape(d, col)
    other = weight[:, :, :, :, 1 - where[2]].reshape(d, col)
    for start in range(0, after.shape[0], CHUNK):
        here = slice(start, start + CHUNK)
        part = nt(attended[here, :col], own) + nt(attended[here, col:], other)
        value = merged[here, :] + vec[3:4, :] + part
        after[here, :] = value
        norm, _ = normalized(value)
        second[here, :] = (norm * vec[4:5, :] + vec[5:6, :]).astype(jnp.bfloat16)


def result_forward(where, attended, merged, vec, gathered, r, col):
    rows, d = merged.shape
    return call(
        result_kernel,
        (1,),
        where,
        [
            (attended, resident((rows, d))),
            (merged, resident((rows, d))),
            (vec, resident(vec.shape)),
            (gathered, once((2, 2, 2, 2, 2, r, col), lambda i, s: (0, 0, 0, 0, 0, 2, 1))),
        ],
        [
            ((rows, d), jnp.float32, resident((rows, d))),
            ((rows, d), jnp.bfloat16, resident((rows, d))),
        ],
        [],
        "result_forward",
    )


def fill_by_core(where, full, refs, rows):
    for c_rel, ref in enumerate(refs):
        for y_rel in BITS:
            for hi in BITS:
                for lo in BITS:
                    at = place_at(where, hi, lo, y_rel, c_rel, rows)
                    full[pl.ds(at, rows), :] = ref[y_rel, hi, lo]


def spill_by_core(where, full, refs, rows):
    for c_rel, ref in enumerate(refs):
        for y_rel in BITS:
            for hi in BITS:
                for lo in BITS:
                    at = place_at(where, hi, lo, y_rel, c_rel, rows)
                    ref[y_rel, hi, lo] = full[pl.ds(at, rows), :]


def expand_kernel(rows, where, second, bias, w0, w1, w2, w3, active, slope, full):
    @pl.when(pl.program_id(0) == 0)
    def _():
        fill_by_core(where, full, (w0, w1), rows)

    @pl.when(pl.program_id(0) == 1)
    def _():
        fill_by_core(where, full, (w2, w3), rows)

    for start in range(0, second.shape[0], CHUNK):
        part = slice(start, start + CHUNK)
        hidden = nn(second[part, :], full[...]) + bias[...]
        value, rate = gelu_both(hidden)
        active[part, :] = value.astype(jnp.bfloat16)
        slope[part, :] = rate.astype(jnp.bfloat16)


def expand_forward(where, second, bias, pieces, block=512):
    rows, d = second.shape
    *_, r, half = pieces[0][0].shape
    steps = half // block
    near = pl.BlockSpec((2, 2, 2, r, block), lambda x, j, s: (0, 0, 0, 0, jnp.where(x == 0, j, steps - 1)))
    far = pl.BlockSpec((2, 2, 2, r, block), lambda x, j, s: (0, 0, 0, 0, jnp.where(x == 0, 0, j)))
    out = pl.BlockSpec((pl.squeezed, rows, block), lambda x, j, s: (x, 0, j))
    return call(
        functools.partial(expand_kernel, r),
        (2, steps),
        where,
        [
            (second, resident((rows, d))),
            (bias, pl.BlockSpec((pl.squeezed, 1, block), lambda x, j, s: (jnp.bitwise_xor(x, s[2]), 0, j))),
        ]
        + [(p, near) for p in pieces[0]]
        + [(p, far) for p in pieces[1]],
        [((2, rows, half), jnp.bfloat16, out)] * 2,
        [pltpu.VMEM((d, block), jnp.bfloat16)],
        "expand_forward",
    )


def contract_kernel(steps, where, alive, active, after, mentor, vec, weight, out, upstream, sums, energy, total):
    step = pl.program_id(0)
    count, d = after.shape
    full = weight[...].reshape(d, -1)

    @pl.when(step == 0)
    def _():
        total[...] = nt(active[...], full)

    @pl.when((step > 0) & (step < 2 * steps - 1))
    def _():
        total[...] += nt(active[...], full)

    @pl.when(step == 2 * steps - 1)
    def _():
        live = alive[0]
        column, squares = 0.0, 0.0
        for start in range(0, count, CHUNK):
            part = slice(start, start + CHUNK)
            final = after[part, :] + (total[part, :] + nt(active[part, :], full)) + vec[6:7, :]
            missing = final - mentor[part, :].astype(jnp.float32)
            slope = live * missing
            out[part, :] = (live * final).astype(jnp.bfloat16)
            upstream[part, :] = slope.astype(jnp.bfloat16)
            column += jnp.sum(slope, axis=0, keepdims=True)
            squares += jnp.sum(slope * missing, axis=0, keepdims=True)
        sums[...] = jnp.broadcast_to(column, sums.shape)
        energy[...] = jnp.broadcast_to(0.5 * jnp.sum(squares, axis=1, keepdims=True), energy.shape)


def contract_forward(where, alive, active, after, mentor, vec, weights, block=1024):
    rows, d = after.shape
    *_, r, half = weights.shape
    steps = half // block
    weight = pl.BlockSpec(
        (2, 2, 2, 2, pl.squeezed, r, block),
        lambda j, s: (0, 0, 0, 0, jnp.bitwise_xor(j // steps, s[2]), 0, j % steps),
    )
    f32, bf16 = jnp.float32, jnp.bfloat16
    whole = resident((rows, d))
    return call(
        functools.partial(contract_kernel, steps),
        (2 * steps,),
        where,
        [
            (alive, pl.BlockSpec(memory_space=pltpu.SMEM)),
            (active, pl.BlockSpec((pl.squeezed, rows, block), lambda j, s: (j // steps, 0, j % steps))),
            (after, whole),
            (mentor, whole),
            (vec, resident(vec.shape)),
            (weights, weight),
        ],
        [
            ((rows, d), bf16, whole),
            ((rows, d), bf16, whole),
            ((8, d), f32, resident((8, d))),
            ((8, 128), f32, resident((8, 128))),
        ],
        [pltpu.VMEM((rows, d), f32)],
        "contract_forward",
    )


def feed_backward_kernel(rows, where, upstream, second, active, slope, weight, w0, w1,
                         grad_second, e0, e1, d0, d1, bias, up, result, total):
    step, last = pl.program_id(0), pl.num_programs(0) - 1
    fill_by_core(where, up, (w0, w1), rows)
    grad_active = nn(upstream[...], weight[...].reshape(up.shape))
    grad_hidden = grad_active * slope[...].astype(jnp.float32)
    bias[...] = jnp.broadcast_to(jnp.sum(grad_hidden, axis=0, keepdims=True), bias.shape)
    grad_hidden = grad_hidden.astype(jnp.bfloat16)
    result[...] = tn(upstream[...], active[...]).astype(jnp.bfloat16)
    spill_by_core(where, result, (d0, d1), rows)
    back = nt(grad_hidden, up[...])

    @pl.when(step == 0)
    def _():
        total[...] = back

    @pl.when((step > 0) & (step < last))
    def _():
        total[...] += back

    @pl.when(step == last)
    def _():
        grad_second[...] = (total[...] + back).astype(jnp.bfloat16)

    result[...] = tn(second[...], grad_hidden).astype(jnp.bfloat16)
    spill_by_core(where, result, (e0, e1), rows)


def feed_backward(where, upstream, second, active, slope, down, up, x_rel, block=512):
    rows, d = upstream.shape
    *_, r, half = up[0].shape
    f32, bf16 = jnp.float32, jnp.bfloat16
    whole = resident((rows, d))
    part = pl.BlockSpec((pl.squeezed, rows, block), lambda j, s: (x_rel, 0, j))
    piece = pl.BlockSpec((2, 2, 2, r, block), lambda j, s: (0, 0, 0, 0, j))
    weight = pl.BlockSpec(
        (2, 2, 2, 2, pl.squeezed, r, block),
        lambda j, s: (0, 0, 0, 0, jnp.bitwise_xor(x_rel, s[2]), 0, j),
    )
    return call(
        functools.partial(feed_backward_kernel, r),
        (half // block,),
        where,
        [(upstream, whole), (second, whole), (active, part), (slope, part), (down, weight)]
        + [(p, piece) for p in up],
        [((rows, d), bf16, whole)]
        + [((2, 2, 2, r, half), bf16, piece)] * 4
        + [((8, half), f32, pl.BlockSpec((8, block), lambda j, s: (0, j)))],
        [pltpu.VMEM((d, block), bf16)] * 2 + [pltpu.VMEM((rows, d), f32)],
        "feed_backward",
    )


def norm_backward_kernel(count, gain_row, last, where, value, base, vec, *refs):
    outs = 2 if last else 3
    grads, extra, (*total, low, sums) = refs[:count], refs[count:-outs], refs[-outs:]

    @pl.when(pl.program_id(0) == 0)
    def _():
        sums[...] = jnp.zeros_like(sums)
        if extra:
            column, energy, alive, own, other = extra
            d = sums.shape[1]
            sums[3:4, :] = column[0:1, :]
            sums[4:5, :] = jnp.broadcast_to(energy[0:1, 0:1], (1, d))
            sums[5:6, :] = jnp.full((1, d), alive[0] * (value.shape[0] * pl.num_programs(0)), jnp.float32)
            here = where[2] == 0
            for i in BITS:
                part = slice(i * d, (i + 1) * d)
                sums[8 + i : 9 + i, :] = jnp.where(here, own[0:1, part], other[0:1, part])
                sums[10 + i : 11 + i, :] = jnp.where(here, other[0:1, part], own[0:1, part])

    upstream = grads[0][...].astype(jnp.float32)
    for ref in grads[1:]:
        upstream = upstream + ref[...].astype(jnp.float32)
    norm, inverse = normalized(value[...])
    e = upstream * vec[gain_row : gain_row + 1, :]
    mean_e = jnp.mean(e, axis=-1, keepdims=True)
    mean_en = jnp.mean(e * norm, axis=-1, keepdims=True)
    result = base[...].astype(jnp.float32) + inverse * (e - mean_e - norm * mean_en)
    for ref in total:
        ref[...] = result
    low[...] = result.astype(jnp.bfloat16)
    for row, item in enumerate((upstream * norm, upstream, result)):
        sums[row : row + 1, :] += jnp.sum(item, axis=0, keepdims=True)


def norm_backward(where, value, base, vec, gain_row, grads, extra=(), last=False):
    rows, d = value.shape
    part = pl.BlockSpec((CHUNK, d), lambda i, s: (i, 0))
    height = 16 if extra else 8
    carried = [
        (x, pl.BlockSpec(memory_space=pltpu.SMEM) if x.ndim == 1 else resident(x.shape)) for x in extra
    ]
    return call(
        functools.partial(norm_backward_kernel, len(grads), gain_row, last),
        (rows // CHUNK,),
        where,
        [(value, part), (base, part), (vec, resident(vec.shape))] + [(g, part) for g in grads] + carried,
        [((rows, d), jnp.float32, part)] * (0 if last else 1)
        + [
            ((rows, d), jnp.bfloat16, part),
            ((height, d), jnp.float32, resident((height, d))),
        ],
        [],
        "norm_backward",
    )


def result_backward_kernel(rows, where, branch, attended, weight, grad, o0, o1, full):
    grad[...] = nn(branch[...], weight[...].reshape(branch.shape[1], -1)).astype(jnp.bfloat16)
    full[...] = tn(branch[...], attended[...]).astype(jnp.bfloat16)
    spill_by_core(where, full, (o0, o1), rows)


def result_backward(where, branch, attended, gathered, r, col):
    rows, d = branch.shape
    bf16 = jnp.bfloat16
    part = pl.BlockSpec((rows, col), lambda x, s: (0, x))
    piece = pl.BlockSpec((pl.squeezed, pl.squeezed, 2, 2, 2, r, col), lambda x, s: (1, x, 0, 0, 0, 0, 0))
    return call(
        functools.partial(result_backward_kernel, r),
        (2,),
        where,
        [
            (branch, resident((rows, d))),
            (attended, part),
            (gathered, weight_block(r, col, lambda x: (3, x))),
        ],
        [((rows, d), bf16, part)] + [((2, 2, 2, 2, 2, r, col), bf16, piece)] * 2,
        [pltpu.VMEM((d, col), bf16)],
        "result_backward",
    )


def project_weight_kernel(rows, where, first, grad, _, __, a0, a1, b0, b1, full):
    full[...] = tn(first[...], grad[...]).astype(jnp.bfloat16)

    @pl.when(pl.program_id(0) < 2)
    def _():
        spill_by_core(where, full, (a0, a1), rows)

    @pl.when(pl.program_id(0) == 2)
    def _():
        spill_by_core(where, full, (b0, b1), rows)


def project_weight(where, first, grads, with_result, r, col):
    rows, d = first.shape
    bf16 = jnp.bfloat16
    part = pl.BlockSpec((pl.squeezed, rows, col), lambda w, x, s: (w, 0, x))
    block = (pl.squeezed, pl.squeezed, 2, 2, 2, r, col)
    front = pl.BlockSpec(
        block, lambda w, x, s: (jnp.minimum(w, 1), jnp.where(w < 2, x, 1), 0, 0, 0, 0, 0)
    )
    back = pl.BlockSpec(block, lambda w, x, s: (0, jnp.where(w < 2, 0, x), 0, 0, 0, 0, 0))
    anywhere = pl.BlockSpec(memory_space=pl.ANY)
    return call(
        functools.partial(project_weight_kernel, r),
        (3, 2),
        where,
        [(first, resident((rows, d))), (grads, part)] + [(p, anywhere) for p in with_result],
        [((2, 2, 2, 2, 2, r, col), bf16, front)] * 2 + [((2, 2, 2, 2, 2, r, col), bf16, back)] * 2,
        [pltpu.VMEM((d, col), bf16)],
        "project_weight",
        (),
        ((2, 2), (3, 3)),
    )


def project_backward_kernel(where, grad, weight, out, total):
    part = nt(grad[...], weight[...].reshape(out.shape[1], -1))
    step = pl.program_id(0) * pl.num_programs(1) + pl.program_id(1)
    last = pl.num_programs(0) * pl.num_programs(1) - 1

    @pl.when(step == 0)
    def _():
        total[...] = part

    @pl.when((step > 0) & (step < last))
    def _():
        total[...] += part

    @pl.when(step == last)
    def _():
        out[...] = (total[...] + part).astype(jnp.bfloat16)


def project_backward(where, grads, gathered, r, col):
    _, rows, d = grads.shape
    return call(
        project_backward_kernel,
        (3, 2),
        where,
        [
            (grads, pl.BlockSpec((pl.squeezed, rows, col), lambda w, x, s: (w, 0, x))),
            (gathered, weight_block(r, col, lambda w, x: (w, x))),
        ],
        [((rows, d), jnp.bfloat16, resident((rows, d)))],
        [pltpu.VMEM((rows, d), jnp.float32)],
        "project_backward",
    )[0]


def merge_weight_kernel(where, ent, byp, grad, o0, o1, full):
    half = ent.shape[1]
    full[:half, :] = tn(ent[...], grad[...]).astype(jnp.bfloat16)
    full[half:, :] = tn(byp[...], grad[...]).astype(jnp.bfloat16)
    for c_rel, ref in enumerate((o0, o1)):
        for x_rel in BITS:
            x = jnp.bitwise_xor(where[2], x_rel)
            for y_rel in BITS:
                for hi in BITS:
                    for lo in BITS:
                        at = place_at(where, hi, lo, y_rel, c_rel, 128) + x * 64
                        ref[x_rel, y_rel, hi, lo] = full[pl.ds(pl.multiple_of(at, 64), 64), :]


def merge_weight(where, ent, byp, grad, r):
    rows, d = ent.shape
    half = d // 2
    bf16 = jnp.bfloat16
    whole = resident((rows, d))
    piece = pl.BlockSpec((pl.squeezed, 2, 2, 2, 2, r, half), lambda j, s: (j, 0, 0, 0, 0, 0, 0))
    return call(
        merge_weight_kernel,
        (2,),
        where,
        [(ent, whole), (byp, whole), (grad, pl.BlockSpec((rows, half), lambda j, s: (0, j)))],
        [((2, 2, 2, 2, 2, r, half), bf16, piece)] * 2,
        [pltpu.VMEM((2 * d, half), bf16)],
        "merge_weight",
    )


def merge_backward_kernel(where, grad, full, left, right):
    half = left.shape[1]
    weight = full[...].reshape(2 * half, half)
    left[...] = nt(grad[...], weight[:half, :])
    right[...] = nt(grad[...], weight[half:, :])


def merge_backward(where, grad, gathered, r, after):
    rows, d = grad.shape
    part = pl.BlockSpec((CHUNK, d), lambda i, w: (i, 0))
    return call(
        merge_backward_kernel,
        (rows // CHUNK,),
        where,
        [(grad, part), (gathered, resident((2, 2, 2, 2, 2, r, d)))],
        [((rows, d), jnp.float32, part)] * 2,
        [],
        "merge_backward",
        after,
    )


def swap(value, axis):
    return lax.ppermute(value, axis, [(0, 1), (1, 0)])


def swap_line(value, bit):
    return lax.ppermute(value, "z", [(i, i ^ bit) for i in range(4)])


def plus(*parts):
    total = parts[0].astype(jnp.float32)
    for part in parts[1:]:
        total = total + part.astype(jnp.float32)
    return total


def send(value, axis):
    return swap(value.astype(jnp.bfloat16), axis)


def line_parts(total, index, dim):
    mine = lax.dynamic_index_in_dim(total, index, dim, keepdims=False)
    other = lax.dynamic_index_in_dim(total, 1 - index, dim, keepdims=False)
    return mine, other.astype(jnp.bfloat16)


def one_sequence_plan(
    entering_states,
    bypass_states,
    mentor_states,
    occupancy_mask,
    bypass_merge_matrix,
    bypass_merge_offset,
    mixer_layernorm_scale,
    mixer_layernorm_offset,
    asking_map_matrix,
    lookup_map_matrix,
    content_map_matrix,
    mixer_result_matrix,
    mixer_result_offset,
    perceptron_layernorm_scale,
    perceptron_layernorm_offset,
    expand_layer_matrix,
    expand_layer_offset,
    contract_layer_matrix,
    contract_layer_offset,
):
    f32, bf16 = jnp.float32, jnp.bfloat16
    rows, d = entering_states.shape
    r, col = asking_map_matrix.shape
    half = expand_layer_matrix.shape[1]
    everyone = ("z", "y", "c", "x")
    z, y, c, x = (lax.axis_index(axis) for axis in everyone)
    hi, lo = z // 2, z % 2
    device = ((z * 2 + y) * 2 + c) * 2 + x
    where = jnp.stack([y, c, x, hi, lo]).astype(jnp.int32)
    small = (
        bypass_merge_offset,
        mixer_layernorm_scale,
        mixer_layernorm_offset,
        mixer_result_offset,
        perceptron_layernorm_scale,
        perceptron_layernorm_offset,
        contract_layer_offset,
        expand_layer_offset,
    )
    share = d // (2**5)
    rows_of_vectors = jnp.concatenate([v.reshape(1, -1) for v in small[:7]], axis=0)
    flat = jnp.pad(rows_of_vectors, ((0, 1), (0, d - share)))
    flat = flat + jnp.pad(expand_layer_offset.reshape(1, -1), ((7, 0), (0, d - expand_layer_offset.shape[0])))
    pack = jnp.concatenate(
        [
            bypass_merge_matrix,
            jnp.concatenate([asking_map_matrix, lookup_map_matrix], axis=1),
            jnp.concatenate([content_map_matrix, mixer_result_matrix.T], axis=1),
            flat,
        ]
    )
    pack = lax.all_gather(pack, everyone, axis=0, tiled=False)
    gathered = pack.reshape((2,) * 5 + pack.shape[1:])

    down = lax.all_gather(contract_layer_matrix.T, everyone, axis=0, tiled=False)
    down = down.reshape((2,) * 5 + down.shape[1:])

    up = expand_layer_matrix
    up = pile(where, 3, up, swap_line(up, 2), 0)
    up = pile(where, 4, up, swap_line(up, 1), 1)
    up_block = pile(where, None, up, swap(up, "y"), 0)
    (gathered,) = gate(where, [gathered], (up_block,))

    rest = pack[:, 3 * r : 3 * r + 8].astype(f32)
    count = pack.shape[0]
    vec = rest[:, :7, : d // count].transpose(1, 0, 2).reshape(7, d)
    vec = jnp.pad(vec, ((0, 1), (0, 0)))
    hidden_add = rest[:, 7, : 2 * half // count].reshape(2, 1, half)
    alive = lax.dynamic_index_in_dim(occupancy_mask, x, keepdims=True).astype(f32)

    merged, first, projected = project_forward(
        where, entering_states, bypass_states, vec, gathered, r, col
    )
    up_other, projected = gate(where, [swap(up_block, "x"), projected], ())
    up_away = [swap(up_block, "c"), swap(up_other, "c")]
    attended, logs = attention_forward(where, projected)
    after_attn, second = result_forward(where, attended, merged, vec, gathered, r, col)
    *up_away, second = gate(where, up_away + [second], ())
    expand_pieces = ((up_block, up_away[0]), (up_other, up_away[1]))
    active, slope = expand_forward(where, second, hidden_add, expand_pieces)
    block_out, upstream, down_bias, energy = contract_forward(
        where, alive, active, after_attn, mentor_states, vec, down
    )

    def feed(x_rel):
        return feed_backward(
            where, upstream, second, active, slope, down, expand_pieces[x_rel], x_rel
        )

    none2, none3 = (None,) * 2, (None,) * 3
    by_lo = [(f32, (None, (4, 0))), (bf16, (None, (4, 1)))]
    by_hi = [(f32, ((3, 0),)), (bf16, ((3, 1),))]

    gs1, e1, e1s, d1, d1s, hb1 = feed(1)
    e1c, d1c = swap(e1s, "c"), swap(d1s, "c")
    gs0, e0, e0s, d0, d0s, hb0 = feed(0)
    e1x, d1y, gs0, e0s, d0s = fold(
        where,
        [
            ([[(e1, none3), (e1c, none3)]], [(bf16, ())]),
            ([[(d1, (1,) + none2), (d1c, (1,) + none2)]], [(bf16, ())]),
        ],
        (gs0, e0s, d0s),
    )
    e1x, d1y, e0c, d0c = swap(e1x, "x"), swap(d1y, "y"), swap(e0s, "c"), swap(d0s, "c")
    grad_after, branch, sums_two = norm_backward(
        where, after_attn, upstream, vec, 4, [gs0, gs1], (down_bias, energy, alive, hb0, hb1)
    )
    parcel = lax.all_gather(sums_two, everyone, axis=0, tiled=False)
    d0y, branch = fold(
        where, [([[(d0, (1,) + none2), (d0c, (1,) + none2)]], [(bf16, ())])], (branch,), (e0c,)
    )
    d0y = swap(d0y, "y")
    grad_attended, o0, o1 = result_backward(where, branch, attended, gathered, r, col)

    def attend(part, grads):
        return attention_backward(where, projected, attended, logs, grad_attended, part, 2, grads)

    grads = attend(0, None)
    e_far, d_far, grads = fold(
        where,
        [
            ([[(a, (1,) + none2) for a in (e0, e0c, e1x)]], [(bf16, ())]),
            ([[(d1, (0,) + none2), (d1c, (0,) + none2), (d1y, none2)]], [(bf16, ())]),
        ],
        (grads,),
        (d0y,),
    )
    e_far, d_far = swap(e_far, "y"), swap(d_far, "x")
    grads = attend(1, grads)
    front = (0,) + none2
    ends, ends_z, grads = fold(
        where,
        [
            (
                [
                    [(e0, front), (e0c, front), (e1x, front), (e_far, none2)],
                    [(d0, front), (d0c, front), (d0y, none2), (d_far, none2)],
                ],
                by_lo,
            )
        ],
        (grads,),
        (parcel,),
    )
    ends_z = swap_line(ends_z, 1)
    p0, p1, vo0, vo1 = project_weight(where, first, grads, (o0, o1), r, col)
    qk_c, vo_c = swap(p1, "c"), swap(vo1, "c")
    grad_first = project_backward(where, grads, gathered, r, col)
    ends, ends_z, grad_first = fold(
        where, [([[(a, (None,)) for a in (ends, ends_z)]], by_hi)], (grad_first,), flops=4 * 10**10
    )
    qk_x, vo_y, grad_first = fold(
        where,
        [
            ([[(a, (None, 1) + none3) for a in (p0, qk_c)]], [(bf16, ())]),
            ([[(a, (None, None, 1) + none2) for a in (vo0, vo_c)]], [(bf16, ())]),
        ],
        (grad_first,),
    )
    qk_x, vo_y, ends_z = swap(qk_x, "x"), swap(vo_y, "y"), swap_line(ends_z, 2)
    merge_grad, three = norm_backward(where, merged, grad_after, vec, 1, [grad_first], last=True)
    m0, m1 = merge_weight(where, entering_states, bypass_states, merge_grad, r)
    three_c = swap(three, "c")
    ends, qk_y, vo_x, three, merge_grad, m1 = fold(
        where,
        [
            ([[(a, ()) for a in (ends, ends_z)]], [(f32, ())]),
            ([[(a, (None, 0, 1) + none2) for a in (p0, qk_c)] + [(qk_x, (None, 1) + none2)]], [(bf16, ())]),
            ([[(a, (None, 1, 0) + none2) for a in (vo0, vo_c)] + [(vo_y, (None, 1) + none2)]], [(bf16, ())]),
            ([[(three, ()), (three_c, ())]], [(f32, ())]),
        ],
        (merge_grad, m1),
    )
    qk_y, vo_x, m_c, three_x = swap(qk_y, "y"), swap(vo_x, "x"), swap(m1, "c"), swap_line(three, 1)
    grad_tokens, grad_shortcut = merge_backward(where, merge_grad, gathered, r, ())
    four_pieces = [
        [(a, (i, 0, 0) + none2) for a in (p0, qk_c)] + [(qk_x, (i, 0) + none2), (qk_y, (i,) + none2)]
        for i in BITS
    ] + [
        [(a, (i, 0, 0) + none2) for a in (vo0, vo_c)] + [(vo_y, (i, 0) + none2), (vo_x, (i,) + none2)]
        for i in BITS
    ]
    four, four_z, l_x, r_y, three, grad_tokens = fold(
        where,
        [
            (four_pieces, by_lo),
            ([[(a, (0, 1) + none3) for a in (m0, m_c)]], [(bf16, ())]),
            ([[(a, (1, None, 1) + none2) for a in (m0, m_c)]], [(bf16, ())]),
            ([[(three, ()), (three_x, ())]], [(f32, ())]),
        ],
        (grad_tokens,),
    )
    l_x, r_y, three_y, four_z = swap(l_x, "x"), swap(r_y, "y"), swap_line(three, 2), swap_line(four_z, 1)
    l_y, r_x, three, four, four_z = fold(
        where,
        [
            ([[(a, (0, 0, 1) + none2) for a in (m0, m_c)] + [(l_x, (1,) + none2)]], [(bf16, ())]),
            ([[(a, (1, 1, 0) + none2) for a in (m0, m_c)] + [(r_y, (1,) + none2)]], [(bf16, ())]),
            ([[(three, ()), (three_y, ())]], [(f32, ())]),
            ([[(a, (None,)) for a in (four, four_z)]], by_hi),
        ],
    )
    l_y, r_x, three_z, four_z = swap(l_y, "y"), swap(r_x, "x"), swap(three, "x"), swap_line(four_z, 2)
    grad_merge, merge_z, three = fold(
        where,
        [
            (
                [
                    [(a, (0, 0, 0) + none2) for a in (m0, m_c)] + [(l_x, (0,) + none2), (l_y, none2)],
                    [(a, (1, 0, 0) + none2) for a in (m0, m_c)] + [(r_y, (0,) + none2), (r_x, none2)],
                ],
                by_lo,
            ),
            ([[(a, ()) for a in (three, three_z)]], [(f32, ())]),
        ],
    )
    merge_z, three_z = swap_line(merge_z, 1), swap(three, "y")
    grad_merge, merge_z, four, three = fold(
        where,
        [
            ([[(a, (None,)) for a in (grad_merge, merge_z)]], by_hi),
            ([[(a, ()) for a in (four, four_z)]], [(f32, ())]),
            ([[(a, ()) for a in (three, three_z)]], [(f32, ())]),
        ],
    )
    grad_merge = plus(grad_merge, swap_line(merge_z, 2))
    own = jnp.sum(parcel, axis=0)
    grad_expand, grad_contract = ends[:, :half], ends[:, half:]
    grad_query, grad_key, grad_value, grad_result = (four[:, i * col : (i + 1) * col] for i in range(4))

    share = d // count
    three = lax.dynamic_slice_in_dim(three, device * share, share, 1)
    four_rows = lax.dynamic_slice_in_dim(own[:4], device * share, share, 1)
    loss_value = own[4, 0] / (own[5, 0] * d)
    share = 2 * half // count
    hidden_row = lax.dynamic_slice_in_dim(own[8:12].reshape(-1), device * share, share, 0)
    sums = (three[2], three[0], three[1], four_rows[2], four_rows[0], four_rows[1], four_rows[3], hidden_row)
    return (
        block_out,
        loss_value,
        grad_tokens,
        grad_shortcut,
        grad_merge,
        sums[0],
        sums[1],
        sums[2],
        grad_query,
        grad_key,
        grad_value,
        grad_result.T,
        sums[3],
        sums[4],
        sums[5],
        grad_expand,
        sums[7],
        grad_contract.T,
        sums[6],
    )


ARGUMENTS = (
    ("ft", None),
    ("ft", None),
    ("ft", None),
    ("f",),
    ("ft", None),
    ("ft",),
    ("ft",),
    ("ft",),
    ("f", "t"),
    ("f", "t"),
    ("f", "t"),
    ("t", "f"),
    ("ft",),
    ("ft",),
    ("ft",),
    ("f", "t"),
    ("ft",),
    ("t", "f"),
    ("ft",),
)
RESULTS = (
    ("ft", None),
    (),
    ("ft", None),
    ("ft", None),
    ("ft", None),
    ("ft",),
    ("ft",),
    ("ft",),
    ("f", "t"),
    ("f", "t"),
    ("f", "t"),
    ("t", "f"),
    ("ft",),
    ("ft",),
    ("ft",),
    ("f", "t"),
    ("ft",),
    ("t", "f"),
    ("ft",),
)


def solution(mesh):
    def whole(*args):
        rows = args[0].shape[0] // mesh.size
        if rows == SEQ_LEN and dict(mesh.shape) == {"fsdp": 16, "tp": 2}:
            plan = one_sequence_plan
            use = jax.sharding.Mesh(mesh.devices.reshape(4, 2, 2, 2), ("z", "y", "c", "x"))
            names = {"f": ("z", "y", "c"), "t": ("x",), "ft": ("z", "y", "c", "x")}
        else:
            plan = per_device_split
            use = mesh
            names = {"f": ("fsdp",), "t": ("tp",), "ft": ("fsdp", "tp")}

        def place(entry):
            return P(*(None if e is None else names[e] for e in entry))

        return jax.shard_map(
            plan,
            mesh=use,
            in_specs=tuple(place(e) for e in ARGUMENTS),
            out_specs=tuple(place(e) for e in RESULTS),
            check_vma=False,
        )(*args)

    return whole
```

```python
import functools
import math

import jax
import jax.numpy as jnp
from jax import lax
from jax.experimental import pallas as pl
from jax.experimental.pallas import tpu as pltpu
from jax.sharding import PartitionSpec as P

D = 1024
HEADS = 16
SEQ_LEN = 1104


EPSILON = 1e-05


def layer_norm(value, gain, shift):
    centred = value - jnp.mean(value, axis=-1, keepdims=True)
    spread = jnp.mean(centred * centred, axis=-1, keepdims=True)
    return centred * lax.rsqrt(spread + EPSILON) * gain + shift


def contract_rows(left, right):
    return lax.dot_general(
        left, right, (((0,), (0,)), ((), ())), preferred_element_type=jnp.float32
    )


def contract_cols(left, right):
    return lax.dot_general(
        left, right, (((1,), (1,)), ((), ())), preferred_element_type=jnp.float32
    )


def attend_forward(queries, keys_all, values):
    scale = float(queries.shape[-1]) ** (-0.5)
    scores = (
        jnp.einsum("qhd,khd->hqk", queries, keys_all, preferred_element_type=jnp.float32) * scale
    )
    peak_score = jnp.max(scores, axis=-1, keepdims=True)
    raised = jnp.exp(scores - peak_score)
    row_total = jnp.sum(raised, axis=-1, keepdims=True)
    weights_low = (raised / row_total).astype(jnp.bfloat16)
    output = jnp.einsum("hqk,khd->qhd", weights_low, values, preferred_element_type=jnp.float32)
    return (output.astype(jnp.bfloat16), peak_score + jnp.log(row_total))


def attend_backward(queries, keys_all, values, summary, upstream):
    scale = float(queries.shape[-1]) ** (-0.5)
    scores = (
        jnp.einsum("qhd,khd->hqk", queries, keys_all, preferred_element_type=jnp.float32) * scale
    )
    probs_full = jnp.exp(scores - summary)
    grad_probs = jnp.einsum("qhd,khd->hqk", upstream, values, preferred_element_type=jnp.float32)
    grad_values = jnp.einsum(
        "hqk,qhd->khd",
        probs_full.astype(jnp.bfloat16),
        upstream,
        preferred_element_type=jnp.float32,
    )
    centre = jnp.sum(probs_full * grad_probs, axis=-1, keepdims=True)
    grad_scores = (probs_full * (grad_probs - centre)).astype(jnp.bfloat16)
    grad_queries = (
        jnp.einsum("hqk,khd->qhd", grad_scores, keys_all, preferred_element_type=jnp.float32)
        * scale
    )
    grad_keys = (
        jnp.einsum("hqk,qhd->khd", grad_scores, queries, preferred_element_type=jnp.float32) * scale
    )
    return (
        grad_queries.astype(jnp.bfloat16),
        grad_keys.astype(jnp.bfloat16),
        grad_values.astype(jnp.bfloat16),
    )


def gelu_exact(value):
    return jax.nn.gelu(value, approximate=False)


def per_device_split(
    entering_states,
    bypass_states,
    mentor_states,
    occupancy_mask,
    bypass_merge_matrix,
    bypass_merge_offset,
    mixer_layernorm_scale,
    mixer_layernorm_offset,
    asking_map_matrix,
    lookup_map_matrix,
    content_map_matrix,
    mixer_result_matrix,
    mixer_result_offset,
    perceptron_layernorm_scale,
    perceptron_layernorm_offset,
    expand_layer_matrix,
    expand_layer_offset,
    contract_layer_matrix,
    contract_layer_offset,
):
    rows = entering_states.shape[0]
    width = D // HEADS
    position = lax.axis_index("tp")
    (
        merge_full,
        merge_add,
        gain_one,
        shift_one,
        output_add,
        gain_two,
        shift_two,
        hidden_add,
        down_add,
    ) = (
        lax.all_gather(bypass_merge_matrix, ("fsdp", "tp"), axis=0, tiled=True),
        lax.all_gather(bypass_merge_offset, ("fsdp", "tp"), axis=0, tiled=True),
        lax.all_gather(mixer_layernorm_scale, ("fsdp", "tp"), axis=0, tiled=True),
        lax.all_gather(mixer_layernorm_offset, ("fsdp", "tp"), axis=0, tiled=True),
        lax.all_gather(mixer_result_offset, ("fsdp", "tp"), axis=0, tiled=True),
        lax.all_gather(perceptron_layernorm_scale, ("fsdp", "tp"), axis=0, tiled=True),
        lax.all_gather(perceptron_layernorm_offset, ("fsdp", "tp"), axis=0, tiled=True),
        lax.all_gather(expand_layer_offset, ("fsdp", "tp"), axis=0, tiled=True),
        lax.all_gather(contract_layer_offset, ("fsdp", "tp"), axis=0, tiled=True),
    )
    query_full, key_full, value_full, output_full, hidden_full, down_full = (
        lax.all_gather(asking_map_matrix, "fsdp", axis=0, tiled=True),
        lax.all_gather(lookup_map_matrix, "fsdp", axis=0, tiled=True),
        lax.all_gather(content_map_matrix, "fsdp", axis=0, tiled=True),
        lax.all_gather(mixer_result_matrix, "fsdp", axis=1, tiled=True),
        lax.all_gather(expand_layer_matrix, "fsdp", axis=0, tiled=True),
        lax.all_gather(contract_layer_matrix, "fsdp", axis=1, tiled=True),
    )
    gain_one = gain_one.astype(jnp.float32)
    shift_one = shift_one.astype(jnp.float32)
    gain_two = gain_two.astype(jnp.float32)
    shift_two = shift_two.astype(jnp.float32)
    project = jnp.concatenate([query_full, key_full, value_full], axis=1)
    local_width = query_full.shape[1]
    local_heads = local_width // width
    local_hidden = hidden_full.shape[1]
    row_index = position * rows + jnp.arange(rows, dtype=jnp.int32)
    slot_of_row = row_index // SEQ_LEN
    series_place_total = occupancy_mask.shape[0]
    agreeing_lines = (
        slot_of_row[:, None] == jnp.arange(series_place_total, dtype=jnp.int32)[None, :]
    ).astype(jnp.float32)
    alive_tokens = jnp.sum(
        agreeing_lines * occupancy_mask.astype(jnp.float32)[None, :], axis=1, keepdims=True
    )
    joined = jnp.concatenate([entering_states, bypass_states], axis=1)
    merged = jnp.dot(joined, merge_full, preferred_element_type=jnp.float32) + merge_add.astype(
        jnp.float32
    )
    first = layer_norm(merged, gain_one, shift_one).astype(jnp.bfloat16)
    first_all = lax.all_gather(first, "tp", axis=0, tiled=True)
    group_rows = first_all.shape[0]
    slots = group_rows // SEQ_LEN
    projected = jnp.dot(first_all, project, preferred_element_type=jnp.float32).astype(jnp.bfloat16)
    shaped = projected.reshape(slots, SEQ_LEN, 3, local_heads, width)
    queries = shaped[:, :, 0]
    keys_all = shaped[:, :, 1]
    values = shaped[:, :, 2]
    attended, summary = lax.map(
        lambda item: attend_forward(item[0], item[1], item[2]), (queries, keys_all, values)
    )
    attended_flat = attended.reshape(group_rows, local_width)
    attention_term = jnp.dot(attended_flat, output_full, preferred_element_type=jnp.float32)
    after_attn = (
        merged
        + lax.psum_scatter(
            attention_term.astype(jnp.bfloat16), "tp", scatter_dimension=0, tiled=True
        ).astype(jnp.float32)
        + output_add.astype(jnp.float32)
    )
    second = layer_norm(after_attn, gain_two, shift_two).astype(jnp.bfloat16)
    second_all = lax.all_gather(second, "tp", axis=0, tiled=True)
    hidden_slice = lax.dynamic_slice_in_dim(
        hidden_add.astype(jnp.float32), position * local_hidden, local_hidden, 0
    )
    hidden = jnp.dot(second_all, hidden_full, preferred_element_type=jnp.float32) + hidden_slice
    active = gelu_exact(hidden).astype(jnp.bfloat16)
    feed_term = jnp.dot(active, down_full, preferred_element_type=jnp.float32)
    final = (
        after_attn
        + lax.psum_scatter(
            feed_term.astype(jnp.bfloat16), "tp", scatter_dimension=0, tiled=True
        ).astype(jnp.float32)
        + down_add.astype(jnp.float32)
    )
    missing = final - mentor_states.astype(jnp.float32)
    grad_final = alive_tokens * missing
    block_out = (final * alive_tokens).astype(jnp.bfloat16)
    energy, counted = lax.psum(
        (0.5 * jnp.sum(grad_final * missing), jnp.sum(alive_tokens)), ("fsdp", "tp")
    )
    loss_value = energy / (counted * D)
    grad_down_bias = jnp.sum(grad_final, axis=0)
    upstream = grad_final.astype(jnp.bfloat16)
    upstream_all = lax.all_gather(upstream, "tp", axis=0, tiled=True)
    grad_down = contract_rows(active, upstream_all)
    grad_active = contract_cols(upstream_all, down_full)
    gelu_value, gelu_pull = jax.vjp(gelu_exact, hidden)
    grad_hidden = gelu_pull(grad_active)[0].astype(jnp.bfloat16)
    grad_hidden_local = jnp.sum(grad_hidden.astype(jnp.float32), axis=0)
    grad_hidden_weight = contract_rows(second_all, grad_hidden)
    feed_back_term = contract_cols(grad_hidden, hidden_full)
    grad_second = lax.psum_scatter(
        feed_back_term.astype(jnp.bfloat16), "tp", scatter_dimension=0, tiled=True
    ).astype(jnp.float32)
    hidden_bias_term = lax.dynamic_update_slice_in_dim(
        jnp.zeros((hidden_add.shape[0],), jnp.float32),
        grad_hidden_local,
        position * local_hidden,
        0,
    )
    norm_value, second_pull = jax.vjp(layer_norm, after_attn, gain_two, shift_two)
    back_after, grad_gain_two, grad_shift_two = second_pull(grad_second)
    grad_after = grad_final + back_after
    grad_output_bias = jnp.sum(grad_after, axis=0)
    branch_all = lax.all_gather(grad_after.astype(jnp.bfloat16), "tp", axis=0, tiled=True)
    grad_output_weight = contract_rows(attended_flat, branch_all)
    grad_attended = contract_cols(branch_all, output_full).astype(jnp.bfloat16)
    upstream_heads = grad_attended.reshape(slots, SEQ_LEN, local_heads, width)
    grad_q_heads, grad_k_heads, grad_v_heads = lax.map(
        lambda item: attend_backward(item[0], item[1], item[2], item[3], item[4]),
        (queries, keys_all, values, summary, upstream_heads),
    )
    grad_projected = jnp.stack([grad_q_heads, grad_k_heads, grad_v_heads], axis=2).reshape(
        group_rows, 3 * local_width
    )
    grad_project = contract_rows(first_all, grad_projected)
    attention_back_term = contract_cols(grad_projected, project)
    grad_first = lax.psum_scatter(
        attention_back_term.astype(jnp.bfloat16), "tp", scatter_dimension=0, tiled=True
    ).astype(jnp.float32)
    first_value, first_pull = jax.vjp(layer_norm, merged, gain_one, shift_one)
    back_merged, grad_gain_one, grad_shift_one = first_pull(grad_first)
    grad_merged = grad_after + back_merged
    grad_merge_bias = jnp.sum(grad_merged, axis=0)
    merge_grad = grad_merged.astype(jnp.bfloat16)
    grad_merge_weight = contract_rows(joined, merge_grad)
    grad_joined = contract_cols(merge_grad, merge_full)
    model_width = entering_states.shape[1]
    grad_tokens = grad_joined[:, :model_width]
    grad_shortcut = grad_joined[:, model_width:]
    grad_query, grad_key, grad_value, grad_output, grad_hidden_full, grad_down_full = (
        lax.psum_scatter(
            grad_project[:, :local_width].astype(jnp.bfloat16),
            "fsdp",
            scatter_dimension=0,
            tiled=True,
        ).astype(jnp.float32),
        lax.psum_scatter(
            grad_project[:, local_width : 2 * local_width].astype(jnp.bfloat16),
            "fsdp",
            scatter_dimension=0,
            tiled=True,
        ).astype(jnp.float32),
        lax.psum_scatter(
            grad_project[:, 2 * local_width :].astype(jnp.bfloat16),
            "fsdp",
            scatter_dimension=0,
            tiled=True,
        ).astype(jnp.float32),
        lax.psum_scatter(
            grad_output_weight.astype(jnp.bfloat16), "fsdp", scatter_dimension=1, tiled=True
        ).astype(jnp.float32),
        lax.psum_scatter(
            grad_hidden_weight.astype(jnp.bfloat16), "fsdp", scatter_dimension=0, tiled=True
        ).astype(jnp.float32),
        lax.psum_scatter(
            grad_down.astype(jnp.bfloat16), "fsdp", scatter_dimension=1, tiled=True
        ).astype(jnp.float32),
    )
    (
        merge_weight_sum,
        merge_bias_sum,
        gain_one_sum,
        shift_one_sum,
        output_bias_sum,
        gain_two_sum,
        shift_two_sum,
        hidden_bias_sum,
        down_bias_sum,
    ) = (
        lax.psum_scatter(grad_merge_weight, ("fsdp", "tp"), scatter_dimension=0, tiled=True),
        lax.psum_scatter(grad_merge_bias, ("fsdp", "tp"), scatter_dimension=0, tiled=True),
        lax.psum_scatter(grad_gain_one, ("fsdp", "tp"), scatter_dimension=0, tiled=True),
        lax.psum_scatter(grad_shift_one, ("fsdp", "tp"), scatter_dimension=0, tiled=True),
        lax.psum_scatter(grad_output_bias, ("fsdp", "tp"), scatter_dimension=0, tiled=True),
        lax.psum_scatter(grad_gain_two, ("fsdp", "tp"), scatter_dimension=0, tiled=True),
        lax.psum_scatter(grad_shift_two, ("fsdp", "tp"), scatter_dimension=0, tiled=True),
        lax.psum_scatter(hidden_bias_term, ("fsdp", "tp"), scatter_dimension=0, tiled=True),
        lax.psum_scatter(grad_down_bias, ("fsdp", "tp"), scatter_dimension=0, tiled=True),
    )
    return (
        block_out,
        loss_value,
        grad_tokens,
        grad_shortcut,
        merge_weight_sum,
        merge_bias_sum,
        gain_one_sum,
        shift_one_sum,
        grad_query,
        grad_key,
        grad_value,
        grad_output,
        output_bias_sum,
        gain_two_sum,
        shift_two_sum,
        grad_hidden_full,
        hidden_bias_sum,
        grad_down_full,
        down_bias_sum,
    )


LOG2E = math.log2(math.e)
PAIR = 128
CHUNK = 368


def nn(a, b):
    return lax.dot_general(a, b, (((1,), (0,)), ((), ())), preferred_element_type=jnp.float32)


def nt(a, b):
    return lax.dot_general(a, b, (((1,), (1,)), ((), ())), preferred_element_type=jnp.float32)


def tn(a, b):
    return lax.dot_general(a, b, (((0,), (0,)), ((), ())), preferred_element_type=jnp.float32)


def vmem():
    return pltpu.CompilerParams(vmem_limit_bytes=60 * 2**20)


def cuts(count, size):
    edges = [i * size for i in range(count // size)] + [count]
    return [slice(a, b) for a, b in zip(edges, edges[1:])]


def attention_forward_kernel(q_ref, k_ref, v_ref, o_ref, l_ref):
    count = q_ref.shape[0]
    scale = (PAIR // 2) ** -0.5 * LOG2E
    low = lax.broadcasted_iota(jnp.int32, (1, PAIR), 1) < PAIR // 2
    keys, values = k_ref[...], v_ref[...]
    zero = jnp.zeros_like(keys)
    heads = (jnp.where(low, keys, zero), jnp.where(low, zero, keys))
    wide = jnp.concatenate([values, jnp.ones_like(values)], axis=1)
    for part in cuts(count, 512):
        queries = q_ref[part, :]
        outs, sums = [], []
        for scores in [nt(queries, head) for head in heads]:
            peak = jnp.max(scores, axis=1, keepdims=True) * scale
            raised = jnp.exp2(scores * scale - peak).astype(jnp.bfloat16)
            both = nn(raised, wide)
            total = both[:, PAIR:]
            outs.append(both[:, :PAIR] / total)
            sums.append(peak + jnp.log2(total))
        o_ref[part, :] = jnp.where(low, outs[0], outs[1]).astype(jnp.bfloat16)
        l_ref[part, :] = jnp.where(low, sums[0], sums[1])


def attention_backward_kernel(q_ref, k_ref, v_ref, o_ref, l_ref, u_ref, out_ref, total_ref):
    count = q_ref.shape[0]
    plain = (PAIR // 2) ** -0.5
    scale = plain * LOG2E
    low = lax.broadcasted_iota(jnp.int32, (1, PAIR), 1) < PAIR // 2
    queries, upstream = q_ref[...], u_ref[...]
    product = upstream.astype(jnp.float32) * o_ref[...].astype(jnp.float32)
    left = jnp.sum(jnp.where(low, product, 0.0), axis=1, keepdims=True)
    right = jnp.sum(jnp.where(low, 0.0, product), axis=1, keepdims=True)
    centres = jnp.transpose(jnp.where(low, left, right))
    logs = jnp.transpose(l_ref[...])
    for head in range(2):

        def own(value):
            zero = jnp.zeros_like(value)
            return jnp.where(low, value, zero) if head == 0 else jnp.where(low, zero, value)

        row = head * (PAIR // 2)
        own_queries, own_upstream = own(queries), own(upstream)
        log_row, centre = logs[row : row + 1, :], centres[row : row + 1, :]
        for part in cuts(count, 256):
            keys, values = k_ref[part, :], v_ref[part, :]
            probs = jnp.exp2(nt(keys, own_queries) * scale - log_row)
            slopes = (probs * (nt(values, own_upstream) - centre)).astype(jnp.bfloat16)
            grad_v = nn(probs.astype(jnp.bfloat16), own_upstream).astype(jnp.bfloat16)
            grad_k = (nn(slopes, own_queries) * plain).astype(jnp.bfloat16)
            grad_q = tn(slopes, own(keys))
            if head == 0:
                out_ref[1, part, :] = grad_k
                out_ref[2, part, :] = grad_v
            else:
                out_ref[1, part, :] = jnp.where(low, out_ref[1, part, :], grad_k)
                out_ref[2, part, :] = jnp.where(low, out_ref[2, part, :], grad_v)
            if head == 0 and part.start == 0:
                total_ref[...] = grad_q
            else:
                total_ref[...] += grad_q
    out_ref[0] = (total_ref[...] * plain).astype(jnp.bfloat16)


def gelu_both(value):
    t = 1.0 / (1.0 + 0.3275911 * math.sqrt(0.5) * jnp.abs(value))
    bell = jnp.exp2(value * value * (-0.5 * LOG2E))
    poly = 0.5 * 1.061405429 * t - 0.5 * 1.453152027
    poly = poly * t + 0.5 * 1.421413741
    poly = poly * t - 0.5 * 0.284496736
    poly = poly * t + 0.5 * 0.254829592
    rest = poly * t * bell
    below = jnp.where(value >= 0, 1.0 - rest, rest)
    return value * below, below + value * bell * (1.0 / math.sqrt(2.0 * math.pi))


def normalized(value):
    centred = value - jnp.mean(value, axis=-1, keepdims=True)
    spread = jnp.mean(centred * centred, axis=-1, keepdims=True)
    inverse = lax.rsqrt(spread + EPSILON)
    return centred * inverse, inverse


def place_at(where_ref, hi, lo, y_rel, c_rel, rows):
    y = jnp.bitwise_xor(where_ref[0], y_rel)
    c = jnp.bitwise_xor(where_ref[1], c_rel)
    return pl.multiple_of(((hi * 2 + lo) * 4 + y * 2 + c) * rows, rows)


BITS = (0, 1)


def once(block, index):
    return pl.BlockSpec(block, index, pipeline_mode=pl.Buffered(1))


def call(kernel, grid, where, ins, outs, scratch, name, after=(), aliases=(), flops=0):
    first, count = len(ins), len(after)

    def ordered_kernel(where_ref, *refs):
        kernel(where_ref, *refs[:first], *refs[first + count :])

    anywhere = pl.BlockSpec(memory_space=pl.ANY)
    return pl.pallas_call(
        ordered_kernel,
        grid_spec=pltpu.PrefetchScalarGridSpec(
            num_scalar_prefetch=1,
            grid=grid,
            in_specs=[spec for _, spec in ins] + [anywhere] * count,
            out_specs=[spec for _, _, spec in outs],
            scratch_shapes=scratch,
        ),
        out_shape=[jax.ShapeDtypeStruct(s, t) for s, t, _ in outs],
        input_output_aliases={1 + i: o for i, o in aliases},
        compiler_params=vmem(),
        cost_estimate=pl.CostEstimate(flops=flops, bytes_accessed=0, transcendentals=0),
        name=name,
    )(where, *(x for x, _ in ins), *after)


def resident(shape):
    return once(shape, lambda *_: (0,) * len(shape))


def attention_forward(where, projected):
    rows, columns = projected.shape
    pairs = columns // 3 // PAIR

    def block(offset):
        return pl.BlockSpec((rows, PAIR), lambda j, s: (0, offset + j))

    return call(
        lambda where_ref, *refs: attention_forward_kernel(*refs),
        (pairs,),
        where,
        [(projected, block(0)), (projected, block(pairs)), (projected, block(2 * pairs))],
        [
            ((rows, pairs * PAIR), jnp.bfloat16, block(0)),
            ((rows, pairs * PAIR), jnp.float32, block(0)),
        ],
        [],
        "attention_forward",
    )


def attention_backward(where, projected, attended, logs, upstream, index, of, grads):
    rows, columns = projected.shape
    pairs = columns // 3 // PAIR
    here = index * (pairs // of)

    def block(offset):
        return pl.BlockSpec((rows, PAIR), lambda j, s: (0, offset + here + j))

    ins = [
        (projected, block(0)),
        (projected, block(pairs)),
        (projected, block(2 * pairs)),
        (attended, block(0)),
        (logs, block(0)),
        (upstream, block(0)),
    ]
    aliases = ()
    if grads is not None:
        ins.append((grads, pl.BlockSpec(memory_space=pl.ANY)))
        aliases = ((6, 0),)

    def kernel(where_ref, *refs):
        attention_backward_kernel(*refs[:6], *refs[-2:])

    return call(
        kernel,
        (pairs // of,),
        where,
        ins,
        [((3, rows, pairs * PAIR), jnp.bfloat16, pl.BlockSpec((3, rows, PAIR), lambda j, s: (0, 0, here + j)))],
        [pltpu.VMEM((rows, PAIR), jnp.float32)],
        "attention_backward",
        (),
        aliases,
    )[0]


def gate(where, values, after):
    anywhere = pl.BlockSpec(memory_space=pl.ANY)
    return call(
        lambda *refs: None,
        (1,),
        where,
        [(v, anywhere) for v in values],
        [(v.shape, v.dtype, anywhere) for v in values],
        [],
        "gate",
        after,
        tuple((i, i) for i in range(len(values))),
    )


def fold_kernel(jobs, carried, waited, where, *refs):
    sources = iter(refs)
    total = sum(len(parts) for pieces, _ in jobs for parts in pieces)
    targets = iter(refs[total + carried + waited :])
    for pieces, results in jobs:
        held = [[next(sources) for _ in parts] for parts in pieces]
        for kind, select in results:
            out, begin = next(targets), 0
            at = tuple(slice(None) if t is None else jnp.bitwise_xor(where[t[0]], t[1]) for t in select)
            for parts in held:
                value = parts[0][at + (Ellipsis,)].astype(jnp.float32)
                for part in parts[1:]:
                    value = value + part[at + (Ellipsis,)].astype(jnp.float32)
                end = begin + value.shape[-1]
                out[..., begin:end] = value.astype(out.dtype)
                begin = end


def fold(where, jobs, carry=(), after=(), flops=0):
    ins, outs, plan = [], [], []
    for pieces, results in jobs:
        columns = 0
        for parts in pieces:
            for array, lead in parts:
                fixed = lead + (None, None)
                block = tuple(n if t is None else pl.squeezed for n, t in zip(array.shape, fixed))
                index = tuple(0 if t is None else t for t in fixed)
                ins.append((array, once(block, lambda i, s, index=index: index)))
            columns += array.shape[-1]
        shape = tuple(n for n, t in zip(array.shape, fixed) if t is None)[:-1] + (columns,)
        for kind, select in results:
            made = tuple(n for n, t in zip(shape, select) if t is None) + shape[len(select) :]
            outs.append((made, kind, resident(made)))
        plan.append((pieces, results))
    anywhere = pl.BlockSpec(memory_space=pl.ANY)
    count, made = len(ins), len(outs)
    ins += [(c, anywhere) for c in carry]
    outs += [(c.shape, c.dtype, anywhere) for c in carry]
    return call(
        functools.partial(fold_kernel, plan, len(carry), 0),
        (1,),
        where,
        ins,
        outs,
        [],
        "fold",
        after,
        tuple((count + i, made + i) for i in range(len(carry))),
        flops,
    )


def pile_kernel(slot, axis, where, mine, other, *outs):
    here = 0 if slot is None else where[slot]
    there = 1 - here
    lead = outs[0].shape[:axis]
    rows = outs[0].shape[-2]
    for number, out in enumerate(outs):
        part = slice(number * rows, (number + 1) * rows)
        for i in range(math.prod(lead)):
            at = ()
            for size in reversed(lead):
                at = (i % size,) + at
                i //= size
            out[at + (here,)] = mine[at + (Ellipsis, part, slice(None))]
            out[at + (there,)] = other[at + (Ellipsis, part, slice(None))]


def pile(where, slot, mine, other, axis, parts=1):
    shape = mine.shape[:axis] + (2,) + mine.shape[axis:-2] + (mine.shape[-2] // parts, mine.shape[-1])
    made = call(
        functools.partial(pile_kernel, slot, axis),
        (1,),
        where,
        [(mine, resident(mine.shape)), (other, resident(mine.shape))],
        [(shape, mine.dtype, resident(shape))] * parts,
        [],
        "pile",
    )
    return made if parts > 1 else made[0]


def weight_block(r, col, number):
    def index(*args):
        which, x_rel = number(*args[:-1])
        return 0, 0, 0, 0, jnp.bitwise_xor(x_rel, args[-1][2]), 1 + which // 2, which % 2

    return pl.BlockSpec((2, 2, 2, 2, pl.squeezed, r, col), index)


def project_kernel(where, ent, byp, full, vec, weight, merged, first, out):
    @pl.when((pl.program_id(0) == 0) & (pl.program_id(1) == 0))
    def _():
        d = ent.shape[1]
        merge = full[...].reshape(2 * d, d)
        for start in range(0, ent.shape[0], CHUNK):
            part = slice(start, start + CHUNK)
            total = nn(ent[part, :], merge[:d, :]) + nn(byp[part, :], merge[d:, :]) + vec[0:1, :]
            merged[part, :] = total
            norm, _ = normalized(total)
            first[part, :] = (norm * vec[1:2, :] + vec[2:3, :]).astype(jnp.bfloat16)

    out[...] = nn(first[...], weight[...].reshape(first.shape[1], -1)).astype(jnp.bfloat16)


def project_forward(where, ent, byp, vec, gathered, r, col):
    rows, d = ent.shape
    f32, bf16 = jnp.float32, jnp.bfloat16
    return call(
        project_kernel,
        (3, 2),
        where,
        [
            (ent, resident((rows, d))),
            (byp, resident((rows, d))),
            (gathered, resident((2, 2, 2, 2, 2, r, d))),
            (vec, resident(vec.shape)),
            (gathered, weight_block(r, col, lambda w, x: (w, x))),
        ],
        [
            ((rows, d), f32, resident((rows, d))),
            ((rows, d), bf16, resident((rows, d))),
            ((rows, 6 * col), bf16, pl.BlockSpec((rows, col), lambda w, x, s: (0, w * 2 + x))),
        ],
        [],
        "project_forward",
    )


def result_kernel(where, attended, merged, vec, weight, after, second):
    d, col = after.shape[1], weight.shape[-1]
    own = weight[:, :, :, :, where[2]].reshape(d, col)
    other = weight[:, :, :, :, 1 - where[2]].reshape(d, col)
    for start in range(0, after.shape[0], CHUNK):
        here = slice(start, start + CHUNK)
        part = nt(attended[here, :col], own) + nt(attended[here, col:], other)
        value = merged[here, :] + vec[3:4, :] + part
        after[here, :] = value
        norm, _ = normalized(value)
        second[here, :] = (norm * vec[4:5, :] + vec[5:6, :]).astype(jnp.bfloat16)


def result_forward(where, attended, merged, vec, gathered, r, col):
    rows, d = merged.shape
    return call(
        result_kernel,
        (1,),
        where,
        [
            (attended, resident((rows, d))),
            (merged, resident((rows, d))),
            (vec, resident(vec.shape)),
            (gathered, once((2, 2, 2, 2, 2, r, col), lambda i, s: (0, 0, 0, 0, 0, 2, 1))),
        ],
        [
            ((rows, d), jnp.float32, resident((rows, d))),
            ((rows, d), jnp.bfloat16, resident((rows, d))),
        ],
        [],
        "result_forward",
    )


def fill_by_core(where, full, refs, rows):
    for c_rel, ref in enumerate(refs):
        for y_rel in BITS:
            for hi in BITS:
                for lo in BITS:
                    at = place_at(where, hi, lo, y_rel, c_rel, rows)
                    full[pl.ds(at, rows), :] = ref[y_rel, hi, lo]


def spill_by_core(where, full, refs, rows):
    for c_rel, ref in enumerate(refs):
        for y_rel in BITS:
            for hi in BITS:
                for lo in BITS:
                    at = place_at(where, hi, lo, y_rel, c_rel, rows)
                    ref[y_rel, hi, lo] = full[pl.ds(at, rows), :]


def expand_kernel(rows, where, second, bias, w0, w1, w2, w3, active, slope, full):
    @pl.when(pl.program_id(0) == 0)
    def _():
        fill_by_core(where, full, (w0, w1), rows)

    @pl.when(pl.program_id(0) == 1)
    def _():
        fill_by_core(where, full, (w2, w3), rows)

    for start in range(0, second.shape[0], CHUNK):
        part = slice(start, start + CHUNK)
        hidden = nn(second[part, :], full[...]) + bias[...]
        value, rate = gelu_both(hidden)
        active[part, :] = value.astype(jnp.bfloat16)
        slope[part, :] = rate.astype(jnp.bfloat16)


def expand_forward(where, second, bias, pieces, block=512):
    rows, d = second.shape
    *_, r, half = pieces[0][0].shape
    steps = half // block
    near = pl.BlockSpec((2, 2, 2, r, block), lambda x, j, s: (0, 0, 0, 0, jnp.where(x == 0, j, steps - 1)))
    far = pl.BlockSpec((2, 2, 2, r, block), lambda x, j, s: (0, 0, 0, 0, jnp.where(x == 0, 0, j)))
    out = pl.BlockSpec((pl.squeezed, rows, block), lambda x, j, s: (x, 0, j))
    return call(
        functools.partial(expand_kernel, r),
        (2, steps),
        where,
        [
            (second, resident((rows, d))),
            (bias, pl.BlockSpec((pl.squeezed, 1, block), lambda x, j, s: (jnp.bitwise_xor(x, s[2]), 0, j))),
        ]
        + [(p, near) for p in pieces[0]]
        + [(p, far) for p in pieces[1]],
        [((2, rows, half), jnp.bfloat16, out)] * 2,
        [pltpu.VMEM((d, block), jnp.bfloat16)],
        "expand_forward",
    )


def contract_kernel(steps, where, alive, active, after, mentor, vec, weight, out, upstream, sums, energy, total):
    step = pl.program_id(0)
    count, d = after.shape
    full = weight[...].reshape(d, -1)

    @pl.when(step == 0)
    def _():
        total[...] = nt(active[...], full)

    @pl.when((step > 0) & (step < 2 * steps - 1))
    def _():
        total[...] += nt(active[...], full)

    @pl.when(step == 2 * steps - 1)
    def _():
        live = alive[0]
        column, squares = 0.0, 0.0
        for start in range(0, count, CHUNK):
            part = slice(start, start + CHUNK)
            final = after[part, :] + (total[part, :] + nt(active[part, :], full)) + vec[6:7, :]
            missing = final - mentor[part, :].astype(jnp.float32)
            slope = live * missing
            out[part, :] = (live * final).astype(jnp.bfloat16)
            upstream[part, :] = slope.astype(jnp.bfloat16)
            column += jnp.sum(slope, axis=0, keepdims=True)
            squares += jnp.sum(slope * missing, axis=0, keepdims=True)
        sums[...] = jnp.broadcast_to(column, sums.shape)
        energy[...] = jnp.broadcast_to(0.5 * jnp.sum(squares, axis=1, keepdims=True), energy.shape)


def contract_forward(where, alive, active, after, mentor, vec, weights, block=1024):
    rows, d = after.shape
    *_, r, half = weights.shape
    steps = half // block
    weight = pl.BlockSpec(
        (2, 2, 2, 2, pl.squeezed, r, block),
        lambda j, s: (0, 0, 0, 0, jnp.bitwise_xor(j // steps, s[2]), 0, j % steps),
    )
    f32, bf16 = jnp.float32, jnp.bfloat16
    whole = resident((rows, d))
    return call(
        functools.partial(contract_kernel, steps),
        (2 * steps,),
        where,
        [
            (alive, pl.BlockSpec(memory_space=pltpu.SMEM)),
            (active, pl.BlockSpec((pl.squeezed, rows, block), lambda j, s: (j // steps, 0, j % steps))),
            (after, whole),
            (mentor, whole),
            (vec, resident(vec.shape)),
            (weights, weight),
        ],
        [
            ((rows, d), bf16, whole),
            ((rows, d), bf16, whole),
            ((8, d), f32, resident((8, d))),
            ((8, 128), f32, resident((8, 128))),
        ],
        [pltpu.VMEM((rows, d), f32)],
        "contract_forward",
    )


def feed_backward_kernel(rows, where, upstream, second, active, slope, weight, w0, w1,
                         grad_second, e0, e1, d0, d1, bias, up, result, total):
    step, last = pl.program_id(0), pl.num_programs(0) - 1
    fill_by_core(where, up, (w0, w1), rows)
    grad_active = nn(upstream[...], weight[...].reshape(up.shape))
    grad_hidden = grad_active * slope[...].astype(jnp.float32)
    bias[...] = jnp.broadcast_to(jnp.sum(grad_hidden, axis=0, keepdims=True), bias.shape)
    grad_hidden = grad_hidden.astype(jnp.bfloat16)
    result[...] = tn(upstream[...], active[...]).astype(jnp.bfloat16)
    spill_by_core(where, result, (d0, d1), rows)
    back = nt(grad_hidden, up[...])

    @pl.when(step == 0)
    def _():
        total[...] = back

    @pl.when((step > 0) & (step < last))
    def _():
        total[...] += back

    @pl.when(step == last)
    def _():
        grad_second[...] = (total[...] + back).astype(jnp.bfloat16)

    result[...] = tn(second[...], grad_hidden).astype(jnp.bfloat16)
    spill_by_core(where, result, (e0, e1), rows)


def feed_backward(where, upstream, second, active, slope, down, up, x_rel, block=512):
    rows, d = upstream.shape
    *_, r, half = up[0].shape
    f32, bf16 = jnp.float32, jnp.bfloat16
    whole = resident((rows, d))
    part = pl.BlockSpec((pl.squeezed, rows, block), lambda j, s: (x_rel, 0, j))
    piece = pl.BlockSpec((2, 2, 2, r, block), lambda j, s: (0, 0, 0, 0, j))
    weight = pl.BlockSpec(
        (2, 2, 2, 2, pl.squeezed, r, block),
        lambda j, s: (0, 0, 0, 0, jnp.bitwise_xor(x_rel, s[2]), 0, j),
    )
    return call(
        functools.partial(feed_backward_kernel, r),
        (half // block,),
        where,
        [(upstream, whole), (second, whole), (active, part), (slope, part), (down, weight)]
        + [(p, piece) for p in up],
        [((rows, d), bf16, whole)]
        + [((2, 2, 2, r, half), bf16, piece)] * 4
        + [((8, half), f32, pl.BlockSpec((8, block), lambda j, s: (0, j)))],
        [pltpu.VMEM((d, block), bf16)] * 2 + [pltpu.VMEM((rows, d), f32)],
        "feed_backward",
    )


def norm_backward_kernel(count, gain_row, last, where, value, base, vec, *refs):
    outs = 2 if last else 3
    grads, extra, (*total, low, sums) = refs[:count], refs[count:-outs], refs[-outs:]

    @pl.when(pl.program_id(0) == 0)
    def _():
        sums[...] = jnp.zeros_like(sums)
        if extra:
            column, energy, alive, own, other = extra
            d = sums.shape[1]
            sums[3:4, :] = column[0:1, :]
            sums[4:5, :] = jnp.broadcast_to(energy[0:1, 0:1], (1, d))
            sums[5:6, :] = jnp.full((1, d), alive[0] * (value.shape[0] * pl.num_programs(0)), jnp.float32)
            here = where[2] == 0
            for i in BITS:
                part = slice(i * d, (i + 1) * d)
                sums[8 + i : 9 + i, :] = jnp.where(here, own[0:1, part], other[0:1, part])
                sums[10 + i : 11 + i, :] = jnp.where(here, other[0:1, part], own[0:1, part])

    upstream = grads[0][...].astype(jnp.float32)
    for ref in grads[1:]:
        upstream = upstream + ref[...].astype(jnp.float32)
    norm, inverse = normalized(value[...])
    e = upstream * vec[gain_row : gain_row + 1, :]
    mean_e = jnp.mean(e, axis=-1, keepdims=True)
    mean_en = jnp.mean(e * norm, axis=-1, keepdims=True)
    result = base[...].astype(jnp.float32) + inverse * (e - mean_e - norm * mean_en)
    for ref in total:
        ref[...] = result
    low[...] = result.astype(jnp.bfloat16)
    for row, item in enumerate((upstream * norm, upstream, result)):
        sums[row : row + 1, :] += jnp.sum(item, axis=0, keepdims=True)


def norm_backward(where, value, base, vec, gain_row, grads, extra=(), last=False):
    rows, d = value.shape
    part = pl.BlockSpec((CHUNK, d), lambda i, s: (i, 0))
    height = 16 if extra else 8
    carried = [
        (x, pl.BlockSpec(memory_space=pltpu.SMEM) if x.ndim == 1 else resident(x.shape)) for x in extra
    ]
    return call(
        functools.partial(norm_backward_kernel, len(grads), gain_row, last),
        (rows // CHUNK,),
        where,
        [(value, part), (base, part), (vec, resident(vec.shape))] + [(g, part) for g in grads] + carried,
        [((rows, d), jnp.float32, part)] * (0 if last else 1)
        + [
            ((rows, d), jnp.bfloat16, part),
            ((height, d), jnp.float32, resident((height, d))),
        ],
        [],
        "norm_backward",
    )


def result_backward_kernel(rows, where, branch, attended, weight, grad, o0, o1, full):
    grad[...] = nn(branch[...], weight[...].reshape(branch.shape[1], -1)).astype(jnp.bfloat16)
    full[...] = tn(branch[...], attended[...]).astype(jnp.bfloat16)
    spill_by_core(where, full, (o0, o1), rows)


def result_backward(where, branch, attended, gathered, r, col):
    rows, d = branch.shape
    bf16 = jnp.bfloat16
    part = pl.BlockSpec((rows, col), lambda x, s: (0, x))
    piece = pl.BlockSpec((pl.squeezed, pl.squeezed, 2, 2, 2, r, col), lambda x, s: (1, x, 0, 0, 0, 0, 0))
    return call(
        functools.partial(result_backward_kernel, r),
        (2,),
        where,
        [
            (branch, resident((rows, d))),
            (attended, part),
            (gathered, weight_block(r, col, lambda x: (3, x))),
        ],
        [((rows, d), bf16, part)] + [((2, 2, 2, 2, 2, r, col), bf16, piece)] * 2,
        [pltpu.VMEM((d, col), bf16)],
        "result_backward",
    )


def project_weight_kernel(rows, where, first, grad, _, __, a0, a1, b0, b1, full):
    full[...] = tn(first[...], grad[...]).astype(jnp.bfloat16)

    @pl.when(pl.program_id(0) < 2)
    def _():
        spill_by_core(where, full, (a0, a1), rows)

    @pl.when(pl.program_id(0) == 2)
    def _():
        spill_by_core(where, full, (b0, b1), rows)


def project_weight(where, first, grads, with_result, r, col):
    rows, d = first.shape
    bf16 = jnp.bfloat16
    part = pl.BlockSpec((pl.squeezed, rows, col), lambda w, x, s: (w, 0, x))
    block = (pl.squeezed, pl.squeezed, 2, 2, 2, r, col)
    front = pl.BlockSpec(
        block, lambda w, x, s: (jnp.minimum(w, 1), jnp.where(w < 2, x, 1), 0, 0, 0, 0, 0)
    )
    back = pl.BlockSpec(block, lambda w, x, s: (0, jnp.where(w < 2, 0, x), 0, 0, 0, 0, 0))
    anywhere = pl.BlockSpec(memory_space=pl.ANY)
    return call(
        functools.partial(project_weight_kernel, r),
        (3, 2),
        where,
        [(first, resident((rows, d))), (grads, part)] + [(p, anywhere) for p in with_result],
        [((2, 2, 2, 2, 2, r, col), bf16, front)] * 2 + [((2, 2, 2, 2, 2, r, col), bf16, back)] * 2,
        [pltpu.VMEM((d, col), bf16)],
        "project_weight",
        (),
        ((2, 2), (3, 3)),
    )


def project_backward_kernel(where, grad, weight, out, total):
    part = nt(grad[...], weight[...].reshape(out.shape[1], -1))
    step = pl.program_id(0) * pl.num_programs(1) + pl.program_id(1)
    last = pl.num_programs(0) * pl.num_programs(1) - 1

    @pl.when(step == 0)
    def _():
        total[...] = part

    @pl.when((step > 0) & (step < last))
    def _():
        total[...] += part

    @pl.when(step == last)
    def _():
        out[...] = (total[...] + part).astype(jnp.bfloat16)


def project_backward(where, grads, gathered, r, col):
    _, rows, d = grads.shape
    return call(
        project_backward_kernel,
        (3, 2),
        where,
        [
            (grads, pl.BlockSpec((pl.squeezed, rows, col), lambda w, x, s: (w, 0, x))),
            (gathered, weight_block(r, col, lambda w, x: (w, x))),
        ],
        [((rows, d), jnp.bfloat16, resident((rows, d)))],
        [pltpu.VMEM((rows, d), jnp.float32)],
        "project_backward",
    )[0]


def merge_weight_kernel(where, ent, byp, grad, o0, o1, full):
    half = ent.shape[1]
    full[:half, :] = tn(ent[...], grad[...]).astype(jnp.bfloat16)
    full[half:, :] = tn(byp[...], grad[...]).astype(jnp.bfloat16)
    for c_rel, ref in enumerate((o0, o1)):
        for x_rel in BITS:
            x = jnp.bitwise_xor(where[2], x_rel)
            for y_rel in BITS:
                for hi in BITS:
                    for lo in BITS:
                        at = place_at(where, hi, lo, y_rel, c_rel, 128) + x * 64
                        ref[x_rel, y_rel, hi, lo] = full[pl.ds(pl.multiple_of(at, 64), 64), :]


def merge_weight(where, ent, byp, grad, r):
    rows, d = ent.shape
    half = d // 2
    bf16 = jnp.bfloat16
    whole = resident((rows, d))
    piece = pl.BlockSpec((pl.squeezed, 2, 2, 2, 2, r, half), lambda j, s: (j, 0, 0, 0, 0, 0, 0))
    return call(
        merge_weight_kernel,
        (2,),
        where,
        [(ent, whole), (byp, whole), (grad, pl.BlockSpec((rows, half), lambda j, s: (0, j)))],
        [((2, 2, 2, 2, 2, r, half), bf16, piece)] * 2,
        [pltpu.VMEM((2 * d, half), bf16)],
        "merge_weight",
    )


def merge_backward_kernel(where, grad, full, left, right):
    half = left.shape[1]
    weight = full[...].reshape(2 * half, half)
    left[...] = nt(grad[...], weight[:half, :])
    right[...] = nt(grad[...], weight[half:, :])


def merge_backward(where, grad, gathered, r, after):
    rows, d = grad.shape
    part = pl.BlockSpec((CHUNK, d), lambda i, w: (i, 0))
    return call(
        merge_backward_kernel,
        (rows // CHUNK,),
        where,
        [(grad, part), (gathered, resident((2, 2, 2, 2, 2, r, d)))],
        [((rows, d), jnp.float32, part)] * 2,
        [],
        "merge_backward",
        after,
    )


def swap(value, axis):
    return lax.ppermute(value, axis, [(0, 1), (1, 0)])


def swap_line(value, bit):
    return lax.ppermute(value, "z", [(i, i ^ bit) for i in range(4)])


def plus(*parts):
    total = parts[0].astype(jnp.float32)
    for part in parts[1:]:
        total = total + part.astype(jnp.float32)
    return total


def send(value, axis):
    return swap(value.astype(jnp.bfloat16), axis)


def line_parts(total, index, dim):
    mine = lax.dynamic_index_in_dim(total, index, dim, keepdims=False)
    other = lax.dynamic_index_in_dim(total, 1 - index, dim, keepdims=False)
    return mine, other.astype(jnp.bfloat16)


def one_sequence_plan(
    entering_states,
    bypass_states,
    mentor_states,
    occupancy_mask,
    bypass_merge_matrix,
    bypass_merge_offset,
    mixer_layernorm_scale,
    mixer_layernorm_offset,
    asking_map_matrix,
    lookup_map_matrix,
    content_map_matrix,
    mixer_result_matrix,
    mixer_result_offset,
    perceptron_layernorm_scale,
    perceptron_layernorm_offset,
    expand_layer_matrix,
    expand_layer_offset,
    contract_layer_matrix,
    contract_layer_offset,
):
    f32, bf16 = jnp.float32, jnp.bfloat16
    rows, d = entering_states.shape
    r, col = asking_map_matrix.shape
    half = expand_layer_matrix.shape[1]
    everyone = ("z", "y", "c", "x")
    z, y, c, x = (lax.axis_index(axis) for axis in everyone)
    hi, lo = z // 2, z % 2
    device = ((z * 2 + y) * 2 + c) * 2 + x
    where = jnp.stack([y, c, x, hi, lo]).astype(jnp.int32)
    small = (
        bypass_merge_offset,
        mixer_layernorm_scale,
        mixer_layernorm_offset,
        mixer_result_offset,
        perceptron_layernorm_scale,
        perceptron_layernorm_offset,
        contract_layer_offset,
        expand_layer_offset,
    )
    share = d // (2**5)
    rows_of_vectors = jnp.concatenate([v.reshape(1, -1) for v in small[:7]], axis=0)
    flat = jnp.pad(rows_of_vectors, ((0, 1), (0, d - share)))
    flat = flat + jnp.pad(expand_layer_offset.reshape(1, -1), ((7, 0), (0, d - expand_layer_offset.shape[0])))
    pack = jnp.concatenate(
        [
            bypass_merge_matrix,
            jnp.concatenate([asking_map_matrix, lookup_map_matrix], axis=1),
            jnp.concatenate([content_map_matrix, mixer_result_matrix.T], axis=1),
            flat,
        ]
    )
    pack = lax.all_gather(pack, everyone, axis=0, tiled=False)
    gathered = pack.reshape((2,) * 5 + pack.shape[1:])

    down = lax.all_gather(contract_layer_matrix.T, everyone, axis=0, tiled=False)
    down = down.reshape((2,) * 5 + down.shape[1:])

    up = expand_layer_matrix
    up = pile(where, 3, up, swap_line(up, 2), 0)
    up = pile(where, 4, up, swap_line(up, 1), 1)
    up_block = pile(where, None, up, swap(up, "y"), 0)
    (gathered,) = gate(where, [gathered], (up_block,))

    rest = pack[:, 3 * r : 3 * r + 8].astype(f32)
    count = pack.shape[0]
    vec = rest[:, :7, : d // count].transpose(1, 0, 2).reshape(7, d)
    vec = jnp.pad(vec, ((0, 1), (0, 0)))
    hidden_add = rest[:, 7, : 2 * half // count].reshape(2, 1, half)
    alive = lax.dynamic_index_in_dim(occupancy_mask, x, keepdims=True).astype(f32)

    merged, first, projected = project_forward(
        where, entering_states, bypass_states, vec, gathered, r, col
    )
    up_other, projected = gate(where, [swap(up_block, "x"), projected], ())
    up_away = [swap(up_block, "c"), swap(up_other, "c")]
    attended, logs = attention_forward(where, projected)
    after_attn, second = result_forward(where, attended, merged, vec, gathered, r, col)
    *up_away, second = gate(where, up_away + [second], ())
    expand_pieces = ((up_block, up_away[0]), (up_other, up_away[1]))
    active, slope = expand_forward(where, second, hidden_add, expand_pieces)
    block_out, upstream, down_bias, energy = contract_forward(
        where, alive, active, after_attn, mentor_states, vec, down
    )

    def feed(x_rel):
        return feed_backward(
            where, upstream, second, active, slope, down, expand_pieces[x_rel], x_rel
        )

    none2, none3 = (None,) * 2, (None,) * 3
    by_lo = [(f32, (None, (4, 0))), (bf16, (None, (4, 1)))]
    by_hi = [(f32, ((3, 0),)), (bf16, ((3, 1),))]

    gs1, e1, e1s, d1, d1s, hb1 = feed(1)
    e1c, d1c = swap(e1s, "c"), swap(d1s, "c")
    gs0, e0, e0s, d0, d0s, hb0 = feed(0)
    e1x, d1y, gs0, e0s, d0s = fold(
        where,
        [
            ([[(e1, none3), (e1c, none3)]], [(bf16, ())]),
            ([[(d1, (1,) + none2), (d1c, (1,) + none2)]], [(bf16, ())]),
        ],
        (gs0, e0s, d0s),
    )
    e1x, d1y, e0c, d0c = swap(e1x, "x"), swap(d1y, "y"), swap(e0s, "c"), swap(d0s, "c")
    branch, sums_two = norm_backward(
        where, after_attn, upstream, vec, 4, [gs0, gs1], (down_bias, energy, alive, hb0, hb1), True
    )
    parcel = lax.all_gather(sums_two, everyone, axis=0, tiled=False)
    d0y, branch = fold(
        where, [([[(d0, (1,) + none2), (d0c, (1,) + none2)]], [(bf16, ())])], (branch,), (e0c,)
    )
    d0y = swap(d0y, "y")
    grad_attended, o0, o1 = result_backward(where, branch, attended, gathered, r, col)

    def attend(part, grads):
        return attention_backward(where, projected, attended, logs, grad_attended, part, 2, grads)

    grads = attend(0, None)
    e_far, d_far, grads = fold(
        where,
        [
            ([[(a, (1,) + none2) for a in (e0, e0c, e1x)]], [(bf16, ())]),
            ([[(d1, (0,) + none2), (d1c, (0,) + none2), (d1y, none2)]], [(bf16, ())]),
        ],
        (grads,),
        (d0y,),
    )
    e_far, d_far = swap(e_far, "y"), swap(d_far, "x")
    grads = attend(1, grads)
    front = (0,) + none2
    ends, ends_z, grads = fold(
        where,
        [
            (
                [
                    [(e0, front), (e0c, front), (e1x, front), (e_far, none2)],
                    [(d0, front), (d0c, front), (d0y, none2), (d_far, none2)],
                ],
                by_lo,
            )
        ],
        (grads,),
        (parcel,),
    )
    ends_z = swap_line(ends_z, 1)
    p0, p1, vo0, vo1 = project_weight(where, first, grads, (o0, o1), r, col)
    qk_c, vo_c = swap(p1, "c"), swap(vo1, "c")
    grad_first = project_backward(where, grads, gathered, r, col)
    ends, ends_z, grad_first = fold(
        where, [([[(a, (None,)) for a in (ends, ends_z)]], by_hi)], (grad_first,), flops=4 * 10**10
    )
    qk_x, vo_y, grad_first = fold(
        where,
        [
            ([[(a, (None, 1) + none3) for a in (p0, qk_c)]], [(bf16, ())]),
            ([[(a, (None, None, 1) + none2) for a in (vo0, vo_c)]], [(bf16, ())]),
        ],
        (grad_first,),
    )
    qk_x, vo_y, ends_z = swap(qk_x, "x"), swap(vo_y, "y"), swap_line(ends_z, 2)
    merge_grad, three = norm_backward(where, merged, branch, vec, 1, [grad_first], last=True)
    m0, m1 = merge_weight(where, entering_states, bypass_states, merge_grad, r)
    three_c = swap(three, "c")
    ends, qk_y, vo_x, three, merge_grad, m1 = fold(
        where,
        [
            ([[(a, ()) for a in (ends, ends_z)]], [(f32, ())]),
            ([[(a, (None, 0, 1) + none2) for a in (p0, qk_c)] + [(qk_x, (None, 1) + none2)]], [(bf16, ())]),
            ([[(a, (None, 1, 0) + none2) for a in (vo0, vo_c)] + [(vo_y, (None, 1) + none2)]], [(bf16, ())]),
            ([[(three, ()), (three_c, ())]], [(f32, ())]),
        ],
        (merge_grad, m1),
    )
    qk_y, vo_x, m_c, three_x = swap(qk_y, "y"), swap(vo_x, "x"), swap(m1, "c"), swap_line(three, 1)
    grad_tokens, grad_shortcut = merge_backward(where, merge_grad, gathered, r, ())
    four_pieces = [
        [(a, (i, 0, 0) + none2) for a in (p0, qk_c)] + [(qk_x, (i, 0) + none2), (qk_y, (i,) + none2)]
        for i in BITS
    ] + [
        [(a, (i, 0, 0) + none2) for a in (vo0, vo_c)] + [(vo_y, (i, 0) + none2), (vo_x, (i,) + none2)]
        for i in BITS
    ]
    four, four_z, l_x, r_y, three, grad_tokens = fold(
        where,
        [
            (four_pieces, by_lo),
            ([[(a, (0, 1) + none3) for a in (m0, m_c)]], [(bf16, ())]),
            ([[(a, (1, None, 1) + none2) for a in (m0, m_c)]], [(bf16, ())]),
            ([[(three, ()), (three_x, ())]], [(f32, ())]),
        ],
        (grad_tokens,),
    )
    l_x, r_y, three_y, four_z = swap(l_x, "x"), swap(r_y, "y"), swap_line(three, 2), swap_line(four_z, 1)
    l_y, r_x, three, four, four_z = fold(
        where,
        [
            ([[(a, (0, 0, 1) + none2) for a in (m0, m_c)] + [(l_x, (1,) + none2)]], [(bf16, ())]),
            ([[(a, (1, 1, 0) + none2) for a in (m0, m_c)] + [(r_y, (1,) + none2)]], [(bf16, ())]),
            ([[(three, ()), (three_y, ())]], [(f32, ())]),
            ([[(a, (None,)) for a in (four, four_z)]], by_hi),
        ],
    )
    l_y, r_x, three_z, four_z = swap(l_y, "y"), swap(r_x, "x"), swap(three, "x"), swap_line(four_z, 2)
    grad_merge, merge_z, three = fold(
        where,
        [
            (
                [
                    [(a, (0, 0, 0) + none2) for a in (m0, m_c)] + [(l_x, (0,) + none2), (l_y, none2)],
                    [(a, (1, 0, 0) + none2) for a in (m0, m_c)] + [(r_y, (0,) + none2), (r_x, none2)],
                ],
                by_lo,
            ),
            ([[(a, ()) for a in (three, three_z)]], [(f32, ())]),
        ],
    )
    merge_z, three_z = swap_line(merge_z, 1), swap(three, "y")
    grad_merge, merge_z, four, three = fold(
        where,
        [
            ([[(a, (None,)) for a in (grad_merge, merge_z)]], by_hi),
            ([[(a, ()) for a in (four, four_z)]], [(f32, ())]),
            ([[(a, ()) for a in (three, three_z)]], [(f32, ())]),
        ],
    )
    grad_merge = plus(grad_merge, swap_line(merge_z, 2))
    own = jnp.sum(parcel, axis=0)
    grad_expand, grad_contract = ends[:, :half], ends[:, half:]
    grad_query, grad_key, grad_value, grad_result = (four[:, i * col : (i + 1) * col] for i in range(4))

    share = d // count
    three = lax.dynamic_slice_in_dim(three, device * share, share, 1)
    four_rows = lax.dynamic_slice_in_dim(own[:4], device * share, share, 1)
    loss_value = own[4, 0] / (own[5, 0] * d)
    share = 2 * half // count
    hidden_row = lax.dynamic_slice_in_dim(own[8:12].reshape(-1), device * share, share, 0)
    sums = (three[2], three[0], three[1], four_rows[2], four_rows[0], four_rows[1], four_rows[3], hidden_row)
    return (
        block_out,
        loss_value,
        grad_tokens,
        grad_shortcut,
        grad_merge,
        sums[0],
        sums[1],
        sums[2],
        grad_query,
        grad_key,
        grad_value,
        grad_result.T,
        sums[3],
        sums[4],
        sums[5],
        grad_expand,
        sums[7],
        grad_contract.T,
        sums[6],
    )


ARGUMENTS = (
    ("ft", None),
    ("ft", None),
    ("ft", None),
    ("f",),
    ("ft", None),
    ("ft",),
    ("ft",),
    ("ft",),
    ("f", "t"),
    ("f", "t"),
    ("f", "t"),
    ("t", "f"),
    ("ft",),
    ("ft",),
    ("ft",),
    ("f", "t"),
    ("ft",),
    ("t", "f"),
    ("ft",),
)
RESULTS = (
    ("ft", None),
    (),
    ("ft", None),
    ("ft", None),
    ("ft", None),
    ("ft",),
    ("ft",),
    ("ft",),
    ("f", "t"),
    ("f", "t"),
    ("f", "t"),
    ("t", "f"),
    ("ft",),
    ("ft",),
    ("ft",),
    ("f", "t"),
    ("ft",),
    ("t", "f"),
    ("ft",),
)


def solution(mesh):
    def whole(*args):
        rows = args[0].shape[0] // mesh.size
        if rows == SEQ_LEN and dict(mesh.shape) == {"fsdp": 16, "tp": 2}:
            plan = one_sequence_plan
            use = jax.sharding.Mesh(mesh.devices.reshape(4, 2, 2, 2), ("z", "y", "c", "x"))
            names = {"f": ("z", "y", "c"), "t": ("x",), "ft": ("z", "y", "c", "x")}
        else:
            plan = per_device_split
            use = mesh
            names = {"f": ("fsdp",), "t": ("tp",), "ft": ("fsdp", "tp")}

        def place(entry):
            return P(*(None if e is None else names[e] for e in entry))

        return jax.shard_map(
            plan,
            mesh=use,
            in_specs=tuple(place(e) for e in ARGUMENTS),
            out_specs=tuple(place(e) for e in RESULTS),
            check_vma=False,
        )(*args)

    return whole
```
